256 devices in a mesh: tm: 8 (over z_hi, core), space: 32 (over y, x, z_lo).
Axes of the slice: x: 4, y: 4, z: 8 (z_hi: 4, z_lo: 2; z = z_hi * 2 + z_lo), core: 2. Of those that a mesh axis runs over, the one named last changes fastest.
Arguments:
- pressure: float32 [8, 2, 8, 512, 2048], P('tm', None, None, 'space'), may hold values from -6 to 6
- mobility: float32 [8, 2, 8, 512, 2048], P('tm', None, None, 'space'), may hold values from 0.05 to 1
- capacity: float32 [8, 2, 8, 512, 2048], P('tm', None, None, 'space'), may hold values from 0.5 to 2
- misfit_weight: float32 [8, 8, 512, 2048], P('tm', None, 'space'), may hold values from 0.2 to 1
- log_permeability: float32 [512, 2048], P('space'), may hold values from -3 to 3
- direction: float32 [512, 2048], P('space'), may hold values from -9 to 9
Outputs:
- hessian_product: float32 [512, 2048], P('space')
- curvature: float32 [], replicated
The draws below stay inside these ranges and needn't reach their ends.
All inputs are finite; a program needn't handle non-finite values.
Results may differ from the reference program's by a relative error of at most 0.00002.
Values sent between devices are 32-bit elements; how exact they have to be, the bound alone decides.
A program may use at most 64 MiB of HBM per device.

```python
import jax
import jax.numpy as jnp
from jax import lax

NY = 2048
LAYERS = 8
STEPS = 2
WINDOWS = 8
NX = 512


def draw_direction(key, part):
    key = jax.random.fold_in(key, 7)
    ramp = 1.0 + 2.0 * jnp.arange(NX, dtype=jnp.float32) / (NX - 1)
    base = jnp.clip(jax.random.normal(key, (NX, NY), jnp.float32), -3.0, 3.0)
    factor = ramp
    return (base * factor[:, None]).astype(jnp.float32)


def steps_of(key, dims, pieces, smallest, largest):
    loudness, own = 1.0, jax.random.fold_in(key, 6)
    for position, shards_of in pieces:
        steps = jnp.exp(jax.random.uniform(jax.random.fold_in(own, position), (shards_of,), jnp.float32, smallest / len(pieces), largest / len(pieces)))
        loudness = loudness * jnp.repeat(steps, dims[position] // shards_of).reshape([-1 if axis == position else 1 for axis in range(len(dims))])
    return loudness


def gaussian(key, shape, spread, reach, split=(), kind=jnp.bfloat16):
    drawn = spread * jax.random.normal(key, shape, jnp.float32)
    if split:
        drawn = drawn * steps_of(key, shape, split, -0.22, 0.18)
    return jnp.clip(drawn, -reach, reach).astype(kind)


def setup_inputs(seed: int = 0) -> dict:
    key_of = jax.random.split(jax.random.key(seed), 7)
    pressure = gaussian(key_of[0], (WINDOWS, STEPS, LAYERS, NX, NY), 1.0, 6.0, ((0, 8), (3, 32)), jnp.float32)
    mobility = jnp.clip(0.05 + 0.95 * jax.random.uniform(key_of[1], (WINDOWS, STEPS, LAYERS, NX, NY), jnp.float32) ** steps_of(key_of[1], (WINDOWS, STEPS, LAYERS, NX, NY), ((0, 8), (3, 32)), -0.2, 0.2), 0.05, 1.0)
    capacity = jnp.clip(0.5 + 1.5 * jax.random.uniform(key_of[2], (WINDOWS, STEPS, LAYERS, NX, NY), jnp.float32) ** steps_of(key_of[2], (WINDOWS, STEPS, LAYERS, NX, NY), ((0, 8), (3, 32)), -0.2, 0.2), 0.5, 2.0)
    misfit_weight = jnp.clip(0.2 + 0.8 * jax.random.uniform(key_of[3], (WINDOWS, LAYERS, NX, NY), jnp.float32) ** steps_of(key_of[3], (WINDOWS, LAYERS, NX, NY), ((0, 8), (2, 32)), -0.2, 0.2), 0.2, 1.0)
    log_permeability = gaussian(key_of[4], (NX, NY), 0.5, 3.0, ((0, 32),), jnp.float32)
    direction = draw_direction(jax.random.fold_in(key_of[6], 71), 0)
    return {"pressure": pressure, "mobility": mobility, "capacity": capacity, "misfit_weight": misfit_weight, "log_permeability": log_permeability, "direction": direction}


def window_total(items, scaled):
    pressure_w, mobility_w, capacity_w, weight_w = items
    face_x = 0.5 * (mobility_w[..., 1:, :] + mobility_w[..., :-1, :]) * (pressure_w[..., 1:, :] - pressure_w[..., :-1, :])
    face_y = 0.5 * (mobility_w[..., 1:] + mobility_w[..., :-1]) * (pressure_w[..., 1:] - pressure_w[..., :-1])
    flux_x = 0.5 * (scaled[1:, :] + scaled[:-1, :]) * face_x
    flux_y = 0.5 * (scaled[:, 1:] + scaled[:, :-1]) * face_y
    padded_x = jnp.pad(flux_x, ((0, 0), (0, 0), (1, 1), (0, 0)))
    padded_y = jnp.pad(flux_y, ((0, 0), (0, 0), (0, 0), (1, 1)))
    change = padded_x[..., 1:, :] - padded_x[..., :-1, :] + padded_y[..., 1:] - padded_y[..., :-1]
    tangent = change / capacity_w
    adjoint = weight_w[None] * tangent / capacity_w
    term_x = face_x * (adjoint[..., :-1, :] - adjoint[..., 1:, :])
    term_y = face_y * (adjoint[..., :-1] - adjoint[..., 1:])
    padded_tx = jnp.pad(term_x, ((0, 0), (0, 0), (1, 1), (0, 0)))
    padded_ty = jnp.pad(term_y, ((0, 0), (0, 0), (0, 0), (1, 1)))
    total = padded_tx[..., 1:, :] + padded_tx[..., :-1, :] + padded_ty[..., 1:] + padded_ty[..., :-1]
    return jnp.sum(total, axis=(0, 1))


def reference(pressure, mobility, capacity, misfit_weight, log_permeability, direction):
    conduct = jnp.exp(log_permeability)
    scaled = conduct * direction
    sums = lax.map(lambda items: window_total(items, scaled), (pressure, mobility, capacity, misfit_weight))
    hessian_product = 0.5 * conduct * jnp.sum(sums, axis=0) / (LAYERS * STEPS * WINDOWS)
    curvature = jnp.sum(direction * hessian_product) / (NX * NY)
    return hessian_product, curvature
```

```python
import functools

import jax
import jax.numpy as jnp
from jax import lax
from jax.experimental import pallas as pl
from jax.experimental.pallas import tpu as pltpu
from jax.sharding import PartitionSpec as P

LANES = 128
SUBLANES = 8
CHIPS_X = 4
CORES = 2
Z_LO = 2
MESH = pl.DeviceIdType.MESH
F32 = jnp.float32


def kernel(
    dims,
    p_hbm,
    m_hbm,
    c_hbm,
    w_hbm,
    lp_hbm,
    d_hbm,
    out,
    cur,
    pv,
    mv,
    cv,
    wv,
    lpv,
    dv,
    pm,
    fx,
    adj,
    txa,
    tyc,
    sbx,
    sby,
    sce,
    rce,
    gsend,
    grecv,
    tot,
    rec,
    part,
    rsb,
    agb,
    sx,
    sz,
    sy,
    local_sem,
    send_sem,
    recv_sem,
):
    tms, spaces, steps, layers, rows, width = dims
    tiles = width // LANES
    zhs = tms // CORES
    ys = spaces // (CHIPS_X * Z_LO)
    zs = zhs * Z_LO
    quarter = tiles // zhs
    last = rows

    tm = lax.axis_index("tm")
    sp = lax.axis_index("space")
    zh, core = tm // CORES, tm % CORES
    zl = sp % Z_LO
    x = (sp // Z_LO) % CHIPS_X
    y = sp // (Z_LO * CHIPS_X)
    z = zh * Z_LO + zl
    left = (sp + spaces - 1) % spaces
    right = (sp + 1) % spaces
    other = (tm + 1) - 2 * core

    per = layers * rows

    def tile_loads(src, dst, first, count, sem):
        def one(j, carry):
            pltpu.make_async_copy(
                src.at[pl.ds(first, count), pl.ds(pl.multiple_of(j * LANES, LANES), LANES)],
                dst.at[j],
                sem,
            ).start()
            return carry

        lax.fori_loop(0, tiles, one, 0)

    def await_tiles(dst, sem):
        pltpu.make_async_copy(dst, dst, sem).wait()

    for s in range(steps):
        tile_loads(p_hbm, pv.at[s], s * per, per, local_sem.at[s])
        tile_loads(m_hbm, mv.at[s], s * per, per, local_sem.at[steps + s])
    load_lp = pltpu.make_async_copy(lp_hbm, lpv, local_sem.at[2 * steps])
    load_d = pltpu.make_async_copy(d_hbm, dv, local_sem.at[2 * steps + 1])
    load_lp.start()
    load_d.start()

    x_group = CORES * CHIPS_X
    my_x = core * CHIPS_X + x

    def x_peer(k):
        index = (my_x + k) % x_group
        return (zh * CORES + index // CHIPS_X, sp + (index % CHIPS_X - x) * Z_LO)

    def z_peer(k):
        to = (z + k) % zs
        return ((to // Z_LO) * CORES + core, sp - zl + to % Z_LO)

    def y_peer(k):
        to = (y + k) % ys
        return (tm, sp + (to - y) * CHIPS_X * Z_LO)

    def tm_peer(k, c):
        return (((zh + k) % zhs) * CORES + (core + c) % CORES, sp)

    greet = [(zh * CORES + c, side) for side in (left, right) for c in range(CORES)]
    greet += [tm_peer(k, c) for k in range(zhs) for c in range(CORES) if (k, c) != (0, 0)]
    greet += [z_peer(k) for k in range(1, zs)]
    greet += [x_peer(k) for k in range(1, x_group)]
    greet += [y_peer(k) for k in range(1, ys)]
    barrier = pltpu.get_barrier_semaphore()
    for peer in greet:
        pl.semaphore_signal(barrier, inc=1, device_id=peer, device_id_type=MESH)

    tile_loads(c_hbm, cv, 0, steps * per, local_sem.at[2 * steps + 2])
    tile_loads(w_hbm, wv, 0, per, local_sem.at[2 * steps + 3])

    sem_count = [0]
    started = []

    def send(src, dst, device, send_index, recv_index):
        copy = pltpu.make_async_remote_copy(
            src_ref=src,
            dst_ref=dst,
            send_sem=send_sem.at[send_index],
            recv_sem=recv_sem.at[recv_index],
            device_id=device,
            device_id_type=MESH,
        )
        copy.start()
        started.append(copy)

    def arrived(dst, recv_index):
        pltpu.make_async_copy(dst, dst, recv_sem.at[recv_index]).wait()

    def take(n):
        first = sem_count[0]
        sem_count[0] += n
        return first

    def transposed(ref, base, i):
        return [ref[j, pl.ds(base + i, layers, stride=rows), :] for j in range(tiles)]

    def spread(s, i):
        for which, ref in enumerate((pv, mv)):
            for j, tile in enumerate(transposed(ref.at[s], 0, i)):
                pm[i + 1, s, which, :, j * LANES : (j + 1) * LANES] = tile

    halo = take(2 * steps)
    for s in range(steps):
        await_tiles(pv.at[s], local_sem.at[s])
        await_tiles(mv.at[s], local_sem.at[steps + s])
        spread(s, 0)
        spread(s, rows - 1)
        if s == 0:
            pl.semaphore_wait(barrier, len(greet))
        send(pm.at[1, s], pm.at[last + 1, s], (tm, left), halo + 2 * s, halo + 2 * s)
        send(pm.at[last, s], pm.at[0, s], (tm, right), halo + 2 * s + 1, halo + 2 * s + 1)

    load_lp.wait()
    load_d.wait()
    scaled = jnp.exp(lpv[...]) * dv[...]
    sce[0] = scaled[0:1, :]
    sce[1] = scaled[rows - 1 : rows, :]
    edge = take(2)
    send(sce.at[0], rce.at[1], (tm, left), edge, edge)
    send(sce.at[1], rce.at[0], (tm, right), edge + 1, edge + 1)

    wide = (layers, width)
    for i in range(rows):
        row = scaled[i : i + 1, :]
        if i + 1 < rows:
            sbx[i + 1] = jnp.broadcast_to(0.25 * (row + scaled[i + 1 : i + 2, :]), wide)
        sby[i] = jnp.broadcast_to(0.25 * (row + pltpu.roll(row, width - 1, 1)), wide)

    def spread_inner(i, carry):
        for s in range(steps):
            spread(s, i)
        return carry

    lax.fori_loop(1, rows - 1, spread_inner, 0)

    lane = lax.broadcasted_iota(jnp.int32, (layers, LANES), 1)
    not_last = lane < LANES - 1
    not_first = lane > 0

    def cut(j):
        return slice(j * LANES, (j + 1) * LANES)

    def face_x(f, carry):
        for s in range(steps):
            for j in range(tiles):
                c = cut(j)
                fx[f, s, :, c] = (pm[f, s, 1, :, c] + pm[f + 1, s, 1, :, c]) * (
                    pm[f + 1, s, 0, :, c] - pm[f, s, 0, :, c]
                )
        return carry

    def cell_row(r, curvature):
        i = r - 1

        def one_step(s):
            held = {}

            def once(name, j, make):
                if (name, j) not in held:
                    held[name, j] = make()
                return held[name, j]

            def pressure(j):
                return once("p", j, lambda: pm[r, s, 0, :, cut(j)])

            def mobility(j):
                return once("m", j, lambda: pm[r, s, 1, :, cut(j)])

            def back(name, get, j):
                return once("b" + name, j, lambda: pltpu.roll(get(j), LANES - 1, 1))

            def ahead(name, get, j):
                after = back(name, get, j + 1) if j + 1 < tiles else get(j)
                return jnp.where(not_last, back(name, get, j), after)

            def before(name, get, j):
                here = once("f" + name, j, lambda: pltpu.roll(get(j), 1, 1))
                if j == 0:
                    return jnp.where(not_first, here, 0.0)
                return jnp.where(not_first, here, held["f" + name, j - 1])

            def face_y(j):
                return once(
                    "fy",
                    j,
                    lambda: (mobility(j) + ahead("m", mobility, j))
                    * (ahead("p", pressure, j) - pressure(j)),
                )

            def flux_y(j):
                return once("gy", j, lambda: face_y(j) * sby[i, :, cut(j)])

            def change(j):
                c = cut(j)
                return once(
                    "ch",
                    j,
                    lambda: fx[r, s, :, c] * sbx[r, :, c]
                    - fx[r - 1, s, :, c] * sbx[r - 1, :, c]
                    + (flux_y(j) - before("gy", flux_y, j)),
                )

            def adjoint(j):
                def make():
                    cap = cv[j, pl.ds(s * per + i, layers, stride=rows), :]
                    weight = wv[j, pl.ds(i, layers, stride=rows), :]
                    value = weight * change(j) / (cap * cap)
                    adj[r, s, :, cut(j)] = value
                    return value

                return once("a", j, make)

            def term_y(j):
                return once(
                    "ty", j, lambda: face_y(j) * (adjoint(j) - ahead("a", adjoint, j))
                )

            return change, adjoint, lambda j: term_y(j) + before("ty", term_y, j)

        parts = [one_step(s) for s in range(steps)]
        for j in range(tiles):
            total = None
            for change, adjoint, both in parts:
                value = both(j)
                total = value if total is None else total + value
                curvature = curvature + adjoint(j) * change(j)
            tyc[i, :, cut(j)] = total
        return curvature

    def face_terms(f, low=True, high=True):
        for j in range(tiles):
            c = cut(j)
            total = None
            for s in range(steps):
                if low and high:
                    difference = adj[f, s, :, c] - adj[f + 1, s, :, c]
                elif low:
                    difference = adj[f, s, :, c]
                else:
                    difference = -adj[f + 1, s, :, c]
                value = fx[f, s, :, c] * difference
                total = value if total is None else total + value
            txa[f, :, c] = total

    def total_row(i):
        for j in range(tiles):
            c = cut(j)
            value = txa[i, :, c] + txa[i + 1, :, c] + tyc[i, :, c]
            tot[j, pl.ds(i, 1), :] = jnp.sum(value, axis=0, keepdims=True)

    lax.fori_loop(1, rows, face_x, 0)
    await_tiles(cv, local_sem.at[2 * steps + 2])
    await_tiles(wv, local_sem.at[2 * steps + 3])
    curvature = lax.fori_loop(2, rows, cell_row, jnp.zeros((layers, LANES), F32))

    def inner_faces(f, carry):
        face_terms(f)
        return carry

    lax.fori_loop(2, rows - 1, inner_faces, 0)

    def inner_rows(i, carry):
        total_row(i)
        return carry

    lax.fori_loop(2, rows - 2, inner_rows, 0)

    arrived(rce.at[0], edge + 1)
    arrived(rce.at[1], edge)
    sbx[0] = jnp.broadcast_to(0.25 * (rce[0] + scaled[0:1, :]), wide)
    sbx[last] = jnp.broadcast_to(0.25 * (rce[1] + scaled[rows - 1 : rows, :]), wide)
    for s in range(steps):
        arrived(pm.at[last + 1, s], halo + 2 * s)
        arrived(pm.at[0, s], halo + 2 * s + 1)

    @pl.when(sp == 0)
    def _():
        pm[0] = pm[1]

    @pl.when(sp == spaces - 1)
    def _():
        pm[last + 1] = pm[last]

    lax.fori_loop(0, 2, lambda k, carry: face_x(k * last, carry), 0)
    curvature = lax.fori_loop(0, 2, lambda k, carry: cell_row(1 + k * (rows - 1), carry), curvature)
    face_terms(0, low=False)
    face_terms(last, high=False)
    face_terms(1)
    face_terms(rows - 1)
    for j in range(tiles):
        gsend[0, :, cut(j)] = jnp.sum(txa[0, :, cut(j)], axis=0, keepdims=True)
        gsend[1, :, cut(j)] = jnp.sum(txa[last, :, cut(j)], axis=0, keepdims=True)
    for i in (0, 1, rows - 2, rows - 1):
        total_row(i)

    half = rows // CORES
    pair = take(1)
    ghost = take(2)
    ghost_in = take(2)
    send(
        tot.at[:, pl.ds(pl.multiple_of((1 - core) * half, half), half), :],
        rec,
        (other, sp),
        pair,
        pair,
    )
    send(gsend.at[0], grecv.at[core], (zh * CORES + 1, left), ghost, ghost_in + core)
    send(gsend.at[1], grecv.at[core], (zh * CORES, right), ghost + 1, ghost_in + core)

    sx[my_x] = jnp.sum(curvature, axis=0, keepdims=True)
    over_x = take(x_group)
    for k in range(1, x_group):
        send(sx.at[my_x], sx.at[my_x], x_peer(k), over_x + k, over_x + k)

    arrived(grecv.at[0], ghost_in)
    arrived(grecv.at[1], ghost_in + 1)
    sub = lax.broadcasted_iota(jnp.int32, (half, LANES), 0)
    here = sub == core * (half - 1)
    for j in range(tiles):
        c = cut(j)
        mine = tot[j, pl.ds(pl.multiple_of(core * half, half), half), :]
        part[j] = mine + jnp.where(here, grecv[0, :, c] + grecv[1, :, c], 0.0)
    arrived(rec, pair)
    part[...] = part[...] + rec[...]

    scatter = take(zhs)

    def columns(q):
        return pl.ds(q * quarter, quarter)

    for k in range(1, zhs):
        to = (zh + k) % zhs
        send(part.at[columns(to)], rsb.at[k], tm_peer(k, 0), scatter + k, scatter + k)

    for k in range(1, x_group):
        arrived(sx.at[(my_x + x_group - k) % x_group], over_x + k)
    sz[z] = jnp.sum(sx[...], axis=0)
    over_z = take(zs)
    for k in range(1, zs):
        send(sz.at[z], sz.at[z], z_peer(k), over_z + k, over_z + k)

    reduced = part[columns(zh)]
    for k in range(1, zhs):
        arrived(rsb.at[k], scatter + k)
        reduced = reduced + rsb[k]
    agb[core, zh] = reduced
    gather = take(tms)
    for k in range(zhs):
        for c in range(CORES):
            if (k, c) != (0, 0):
                index = gather + k * CORES + c
                send(agb.at[core, zh], agb.at[core, zh], tm_peer(k, c), index, index)

    for k in range(1, zs):
        arrived(sz.at[(z + zs - k) % zs], over_z + k)
    sy[y] = jnp.sum(sz[...], axis=0)
    over_y = take(ys)
    for k in range(1, ys):
        send(sy.at[y], sy.at[y], y_peer(k), over_y + k, over_y + k)

    for k in range(zhs):
        for c in range(CORES):
            if (k, c) != (0, 0):
                source = agb.at[(core + c) % CORES, (zh + zhs - k) % zhs]
                arrived(source, gather + k * CORES + c)
    for c in range(CORES):
        for q in range(zhs):
            for j in range(quarter):
                out[c * half : (c + 1) * half, cut(q * quarter + j)] = agb[c, q, j]

    for k in range(1, ys):
        arrived(sy.at[(y + ys - k) % ys], over_y + k)
    whole = jnp.sum(sy[...], axis=0)
    scale = 1.0 / (layers * steps * tms * rows * spaces * width)
    cur[...] = jnp.broadcast_to(jnp.sum(whole, axis=1, keepdims=True) * scale, cur.shape)

    for copy in started:
        copy.wait_send()


def shards(tms, spaces, pressure, mobility, capacity, misfit_weight, log_permeability, direction):
    _, steps, layers, rows, width = pressure.shape
    dims = (tms, spaces, steps, layers, rows, width)
    tiles = width // LANES
    zhs = tms // CORES
    ys = spaces // (CHIPS_X * Z_LO)
    zs = zhs * Z_LO
    x_group = CORES * CHIPS_X
    per = layers * rows
    half = rows // CORES
    copies = 2 * steps + 2 + 1 + 4 + x_group + zhs + zs + tms + ys
    vmem = pltpu.VMEM
    total, curvature = pl.pallas_call(
        functools.partial(kernel, dims),
        out_shape=(
            jax.ShapeDtypeStruct((rows, width), F32),
            jax.ShapeDtypeStruct((1, LANES), F32),
        ),
        in_specs=[pl.BlockSpec(memory_space=pl.ANY)] * 6,
        out_specs=(
            pl.BlockSpec(memory_space=pltpu.VMEM),
            pl.BlockSpec(memory_space=pltpu.VMEM),
        ),
        scratch_shapes=[
            vmem((steps, tiles, per, LANES), F32),
            vmem((steps, tiles, per, LANES), F32),
            vmem((tiles, steps * per, LANES), F32),
            vmem((tiles, per, LANES), F32),
            vmem((rows, width), F32),
            vmem((rows, width), F32),
            vmem((rows + 2, steps, 2, layers, width), F32),
            vmem((rows + 1, steps, layers, width), F32),
            vmem((rows + 2, steps, layers, width), F32),
            vmem((rows + 1, layers, width), F32),
            vmem((rows, layers, width), F32),
            vmem((rows + 1, layers, width), F32),
            vmem((rows, layers, width), F32),
            vmem((2, 1, width), F32),
            vmem((2, 1, width), F32),
            vmem((2, 1, width), F32),
            vmem((2, 1, width), F32),
            vmem((tiles, rows, LANES), F32),
            vmem((tiles, half, LANES), F32),
            vmem((tiles, half, LANES), F32),
            vmem((zhs, tiles // zhs, half, LANES), F32),
            vmem((CORES, zhs, tiles // zhs, half, LANES), F32),
            vmem((x_group, 1, LANES), F32),
            vmem((zs, 1, LANES), F32),
            vmem((ys, 1, LANES), F32),
            pltpu.SemaphoreType.DMA((2 * steps + 4,)),
            pltpu.SemaphoreType.DMA((copies,)),
            pltpu.SemaphoreType.DMA((copies,)),
        ],
        compiler_params=pltpu.CompilerParams(
            collective_id=0, has_side_effects=True, vmem_limit_bytes=56 << 20
        ),
        cost_estimate=pl.CostEstimate(
            flops=50 * steps * per * width,
            bytes_accessed=4 * (7 * steps * per * width // 2),
            transcendentals=rows * width,
        ),
    )(
        pressure.reshape(steps * per, width),
        mobility.reshape(steps * per, width),
        capacity.reshape(steps * per, width),
        misfit_weight.reshape(per, width),
        log_permeability,
        direction,
    )
    factor = 0.25 / (layers * steps * tms)
    return jnp.exp(log_permeability) * total * factor, curvature[0, 0]


def solution(mesh):
    placed = (
        P("tm", None, None, "space", None),
        P("tm", None, None, "space", None),
        P("tm", None, None, "space", None),
        P("tm", None, "space", None),
        P("space", None),
        P("space", None),
    )
    return jax.shard_map(
        functools.partial(shards, mesh.shape["tm"], mesh.shape["space"]),
        mesh=mesh,
        in_specs=placed,
        out_specs=(P("space", None), P()),
        check_vma=False,
    )
```

```python
import functools

import jax
import jax.numpy as jnp
from jax import lax
from jax.experimental import pallas as pl
from jax.experimental.pallas import tpu as pltpu
from jax.sharding import PartitionSpec as P

LANES = 128
SUBLANES = 8
CHIPS_X = 4
CORES = 2
Z_LO = 2
MESH = pl.DeviceIdType.MESH
F32 = jnp.float32


def kernel(
    dims,
    p_hbm,
    m_hbm,
    c_hbm,
    w_hbm,
    lp_hbm,
    d_hbm,
    out,
    cur,
    pv,
    mv,
    cv,
    wv,
    lpv,
    dv,
    pm,
    fx,
    adj,
    txa,
    tyc,
    sbx,
    sby,
    sce,
    rce,
    inner,
    inner_in,
    inner_sum,
    rsb,
    agb,
    edges,
    edges_in,
    edge_z,
    ghost_z,
    final,
    sz,
    sxy,
    local_sem,
    send_sem,
    recv_sem,
):
    tms, spaces, steps, layers, rows, width = dims
    tiles = width // LANES
    zhs = tms // CORES
    ys = spaces // (CHIPS_X * Z_LO)
    zs = zhs * Z_LO
    last = rows
    row_tiles = tiles // SUBLANES
    row_blocks = rows // SUBLANES
    layer_rows = row_blocks * tiles * SUBLANES
    state_rows = layers * layer_rows

    tm = lax.axis_index("tm")
    sp = lax.axis_index("space")
    zh, core = tm // CORES, tm % CORES
    zl = sp % Z_LO
    x = (sp // Z_LO) % CHIPS_X
    y = sp // (Z_LO * CHIPS_X)
    z = zh * Z_LO + zl
    left = (sp + spaces - 1) % spaces
    right = (sp + 1) % spaces
    other = (tm + 1) - 2 * core

    loads = {}

    def load(name, src, dst, index):
        loads[name] = pltpu.make_async_copy(src, dst, local_sem.at[index])
        loads[name].start()

    for s in range(steps):
        part = pl.ds(s * state_rows, state_rows)
        load(("p", s), p_hbm.at[part, :], pv.at[part, :], 2 * s)
        load(("m", s), m_hbm.at[part, :], mv.at[part, :], 2 * s + 1)
    load("lp", lp_hbm, lpv, 2 * steps)
    load("d", d_hbm, dv, 2 * steps + 1)

    line = zs * CORES
    my_line = z * CORES + core
    plane = ys * CHIPS_X
    my_plane = y * CHIPS_X + x

    def line_peer(k):
        index = (my_line + k) % line
        to = index // CORES
        return ((to // Z_LO) * CORES + index % CORES, sp - zl + to % Z_LO)

    def plane_peer(k):
        return (tm, ((my_plane + k) % plane) * Z_LO + zl)

    def z_peer(k):
        return (((zh + k) % zhs) * CORES + core, sp)

    greet = [(t, side) for side in (left, right) for t in range(tms)]
    greet += [((tm + k) % tms, sp) for k in range(1, tms)]
    greet += [plane_peer(k) for k in range(1, plane)]
    barrier = pltpu.get_barrier_semaphore()
    for peer in greet:
        pl.semaphore_signal(barrier, inc=1, device_id=peer, device_id_type=MESH)

    sem_count = [0]
    started = []

    def send(src, dst, device, send_index, recv_index):
        copy = pltpu.make_async_remote_copy(
            src_ref=src,
            dst_ref=dst,
            send_sem=send_sem.at[send_index],
            recv_sem=recv_sem.at[recv_index],
            device_id=device,
            device_id_type=MESH,
        )
        copy.start()
        started.append(copy)

    def arrived(dst, recv_index):
        pltpu.make_async_copy(dst, dst, recv_sem.at[recv_index]).wait()

    def take(n):
        first = sem_count[0]
        sem_count[0] += n
        return first

    def layers_of(ref, s, i, j):
        first = (
            s * state_rows + (i // SUBLANES) * (tiles * SUBLANES) + j * SUBLANES + i % SUBLANES
        )
        return ref[pl.ds(first, layers, stride=layer_rows), :]

    def cut(j):
        return slice(j * LANES, (j + 1) * LANES)

    def spread(s, i):
        for which, ref in enumerate((pv, mv)):
            for j in range(tiles):
                pm[i + 1, s, which, :, cut(j)] = layers_of(ref, s, i, j)

    halo = take(2 * steps)
    for s in range(steps):
        loads["p", s].wait()
        loads["m", s].wait()
        spread(s, 0)
        spread(s, rows - 1)
        if s == 0:
            pl.semaphore_wait(barrier, len(greet))
        send(pm.at[1, s], pm.at[last + 1, s], (tm, left), halo + 2 * s, halo + 2 * s)
        send(pm.at[last, s], pm.at[0, s], (tm, right), halo + 2 * s + 1, halo + 2 * s + 1)
    load("c", c_hbm, cv, 2 * steps + 2)
    load("w", w_hbm, wv, 2 * steps + 3)

    loads["lp"].wait()
    loads["d"].wait()
    scaled = jnp.exp(lpv[...]) * dv[...]
    sce[0] = scaled[0:1, :]
    sce[1] = scaled[rows - 1 : rows, :]
    edge = take(2)
    send(sce.at[0], rce.at[1], (tm, left), edge, edge)
    send(sce.at[1], rce.at[0], (tm, right), edge + 1, edge + 1)

    wide = (layers, width)
    for i in range(rows):
        row = scaled[i : i + 1, :]
        if i + 1 < rows:
            sbx[i + 1] = jnp.broadcast_to(0.25 * (row + scaled[i + 1 : i + 2, :]), wide)
        sby[i] = jnp.broadcast_to(0.25 * (row + pltpu.roll(row, width - 1, 1)), wide)

    def spread_inner(i, carry):
        for s in range(steps):
            spread(s, i)
        return carry

    lax.fori_loop(1, rows - 1, spread_inner, 0)

    lane = lax.broadcasted_iota(jnp.int32, (layers, LANES), 1)
    not_last = lane < LANES - 1
    not_first = lane > 0

    def face_x(f, carry):
        for s in range(steps):
            for j in range(tiles):
                c = cut(j)
                fx[f, s, :, c] = (pm[f, s, 1, :, c] + pm[f + 1, s, 1, :, c]) * (
                    pm[f + 1, s, 0, :, c] - pm[f, s, 0, :, c]
                )
        return carry

    def cell_row(r, curvature):
        i = r - 1

        def one_step(s):
            held = {}

            def once(name, j, make):
                if (name, j) not in held:
                    held[name, j] = make()
                return held[name, j]

            def pressure(j):
                return once("p", j, lambda: pm[r, s, 0, :, cut(j)])

            def mobility(j):
                return once("m", j, lambda: pm[r, s, 1, :, cut(j)])

            def back(name, get, j):
                return once("b" + name, j, lambda: pltpu.roll(get(j), LANES - 1, 1))

            def ahead(name, get, j):
                after = back(name, get, j + 1) if j + 1 < tiles else get(j)
                return jnp.where(not_last, back(name, get, j), after)

            def before(name, get, j):
                here = once("f" + name, j, lambda: pltpu.roll(get(j), 1, 1))
                if j == 0:
                    return jnp.where(not_first, here, 0.0)
                return jnp.where(not_first, here, held["f" + name, j - 1])

            def face_y(j):
                return once(
                    "fy",
                    j,
                    lambda: (mobility(j) + ahead("m", mobility, j))
                    * (ahead("p", pressure, j) - pressure(j)),
                )

            def flux_y(j):
                return once("gy", j, lambda: face_y(j) * sby[i, :, cut(j)])

            def change(j):
                c = cut(j)
                return once(
                    "ch",
                    j,
                    lambda: fx[r, s, :, c] * sbx[r, :, c]
                    - fx[r - 1, s, :, c] * sbx[r - 1, :, c]
                    + (flux_y(j) - before("gy", flux_y, j)),
                )

            def adjoint(j):
                def make():
                    cap = layers_of(cv, s, i, j)
                    weight = layers_of(wv, 0, i, j)
                    square = cap * cap
                    inverse = pl.reciprocal(square, approx=True)
                    inverse = inverse * (2.0 - square * inverse)
                    value = weight * change(j) * inverse
                    adj[r, s, :, cut(j)] = value
                    return value

                return once("a", j, make)

            def term_y(j):
                return once(
                    "ty", j, lambda: face_y(j) * (adjoint(j) - ahead("a", adjoint, j))
                )

            return change, adjoint, lambda j: term_y(j) + before("ty", term_y, j)

        parts = [one_step(s) for s in range(steps)]
        for j in range(tiles):
            total = None
            for change, adjoint, both in parts:
                value = both(j)
                total = value if total is None else total + value
                curvature = curvature + adjoint(j) * change(j)
            tyc[i, :, cut(j)] = total
        return curvature

    def face_terms(f, low=True, high=True):
        for j in range(tiles):
            c = cut(j)
            total = None
            for s in range(steps):
                if low and high:
                    difference = adj[f, s, :, c] - adj[f + 1, s, :, c]
                elif low:
                    difference = adj[f, s, :, c]
                else:
                    difference = -adj[f + 1, s, :, c]
                value = fx[f, s, :, c] * difference
                total = value if total is None else total + value
            txa[f, :, c] = total

    def pack(dst, first, j, value):
        tile = first + j // SUBLANES
        low = j % SUBLANES
        dst[tile, low : low + 1, :] = jnp.sum(value, axis=0, keepdims=True)

    def pack_total(dst, first, i):
        for j in range(tiles):
            c = cut(j)
            pack(dst, first, j, txa[i, :, c] + txa[i + 1, :, c] + tyc[i, :, c])

    lax.fori_loop(1, rows, face_x, 0)
    loads["c"].wait()
    loads["w"].wait()
    curvature = lax.fori_loop(2, rows, cell_row, jnp.zeros((layers, LANES), F32))

    def inner_faces(f, carry):
        face_terms(f)
        return carry

    lax.fori_loop(2, rows - 1, inner_faces, 0)

    def inner_rows(i, carry):
        pack_total(inner, (i - 2) * row_tiles, i)
        return carry

    lax.fori_loop(2, rows - 2, inner_rows, 0)

    half_tiles = (rows // CORES - 2) * row_tiles
    chunk = half_tiles // zhs
    inner_pair = take(1)
    send(
        inner.at[pl.ds((1 - core) * half_tiles, half_tiles)],
        inner_in,
        (other, sp),
        inner_pair,
        inner_pair,
    )
    arrived(inner_in, inner_pair)
    inner_sum[...] = inner[pl.ds(core * half_tiles, half_tiles)] + inner_in[...]
    scatter = take(zhs)
    for k in range(1, zhs):
        to = (zh + k) % zhs
        send(
            inner_sum.at[pl.ds(to * chunk, chunk)],
            rsb.at[k],
            z_peer(k),
            scatter + k,
            scatter + k,
        )

    arrived(rce.at[0], edge + 1)
    arrived(rce.at[1], edge)
    sbx[0] = jnp.broadcast_to(0.25 * (rce[0] + scaled[0:1, :]), wide)
    sbx[last] = jnp.broadcast_to(0.25 * (rce[1] + scaled[rows - 1 : rows, :]), wide)
    for s in range(steps):
        arrived(pm.at[last + 1, s], halo + 2 * s)
        arrived(pm.at[0, s], halo + 2 * s + 1)

    @pl.when(sp == 0)
    def _():
        pm[0] = pm[1]

    @pl.when(sp == spaces - 1)
    def _():
        pm[last + 1] = pm[last]

    lax.fori_loop(0, 2, lambda k, carry: face_x(k * last, carry), 0)
    curvature = lax.fori_loop(0, 2, lambda k, carry: cell_row(1 + k * (rows - 1), carry), curvature)

    sz[my_line] = jnp.sum(curvature, axis=0, keepdims=True)
    over_line = take(line)
    for k in range(1, line):
        send(sz.at[my_line], sz.at[my_line], line_peer(k), over_line + k, over_line + k)

    face_terms(0, low=False)
    face_terms(last, high=False)
    face_terms(1)
    face_terms(rows - 1)
    for c, (edge_row, inner_row, face) in enumerate(((0, 1, 0), (rows - 1, rows - 2, last))):
        pack_total(edges.at[c], 0, edge_row)
        pack_total(edges.at[c], row_tiles, inner_row)
        for j in range(tiles):
            pack(edges.at[c], 2 * row_tiles, j, txa[face, :, cut(j)])
    edge_pair = take(1)
    send(edges.at[1 - core], edges_in, (other, sp), edge_pair, edge_pair)

    reduced = inner_sum[pl.ds(zh * chunk, chunk)]
    for k in range(1, zhs):
        arrived(rsb.at[k], scatter + k)
        reduced = reduced + rsb[k]
    agb[core, pl.ds(zh * chunk, chunk)] = reduced
    mine = agb.at[core, pl.ds(zh * chunk, chunk)]
    gather = take(zhs)
    forward = take(zhs)
    for k in range(1, zhs):
        send(mine, mine, z_peer(k), gather + k, gather + k)
    send(mine, mine, (other, sp), forward, forward)

    two = 2 * row_tiles
    arrived(edges_in, edge_pair)
    summed = edges[core] + edges_in[...]
    edge_z[zh] = summed
    over_z = take(zhs)
    ghost = take(zhs)
    for k in range(1, zhs):
        send(
            edge_z.at[zh, pl.ds(0, two)],
            edge_z.at[zh, pl.ds(0, two)],
            z_peer(k),
            over_z + k,
            over_z + k,
        )
    side = left + core * (right - left)
    for k in range(zhs):
        send(
            edge_z.at[zh, pl.ds(two, row_tiles)],
            ghost_z.at[zh],
            (((zh + k) % zhs) * CORES + 1 - core, side),
            ghost + k,
            ghost + k,
        )

    for k in range(1, line):
        arrived(sz.at[(my_line + line - k) % line], over_line + k)
    sxy[my_plane] = jnp.sum(sz[...], axis=0)
    over_plane = take(plane)
    for k in range(1, plane):
        send(sxy.at[my_plane], sxy.at[my_plane], plane_peer(k), over_plane + k, over_plane + k)

    def unpack(src, first, i):
        for j in range(tiles):
            low = j % SUBLANES
            out[i : i + 1, cut(j)] = src[first + j // SUBLANES, low : low + 1, :]

    for k in range(1, zhs):
        whose = agb.at[core, pl.ds(((zh + zhs - k) % zhs) * chunk, chunk)]
        arrived(whose, gather + k)
        send(whose, whose, (other, sp), forward + k, forward + k)

    for k in range(1, zhs):
        arrived(edge_z.at[(zh + zhs - k) % zhs, pl.ds(0, two)], over_z + k)
    for k in range(zhs):
        arrived(ghost_z.at[(zh + zhs - k) % zhs], ghost + k)
    total = edge_z[0, 0:two]
    beyond = ghost_z[0]
    for k in range(1, zhs):
        total = total + edge_z[k, 0:two]
        beyond = beyond + ghost_z[k]
    final[core, pl.ds(0, row_tiles)] = total[:row_tiles] + beyond
    final[core, pl.ds(row_tiles, row_tiles)] = total[row_tiles:]
    final_pair = take(1)
    send(final.at[core], final.at[core], (other, sp), final_pair, final_pair)

    for k in range(zhs):
        whose = agb.at[1 - core, pl.ds(((zh + zhs - k) % zhs) * chunk, chunk)]
        arrived(whose, forward + k)
    for i in range(2, rows - 2):
        first = (i - 2) * row_tiles
        unpack(agb.at[first // half_tiles], first % half_tiles, i)
    arrived(final.at[1 - core], final_pair)
    for c, (edge_row, inner_row) in enumerate(((0, 1), (rows - 1, rows - 2))):
        unpack(final.at[c], 0, edge_row)
        unpack(final.at[c], row_tiles, inner_row)

    for k in range(1, plane):
        arrived(sxy.at[(my_plane + plane - k) % plane], over_plane + k)
    whole = jnp.sum(sxy[...], axis=0)
    scale = 1.0 / (layers * steps * tms * rows * spaces * width)
    cur[...] = jnp.broadcast_to(jnp.sum(whole, axis=1, keepdims=True) * scale, cur.shape)

    for copy in started:
        copy.wait_send()


def shards(tms, spaces, pressure, mobility, capacity, misfit_weight, log_permeability, direction):
    _, steps, layers, rows, width = pressure.shape
    dims = (tms, spaces, steps, layers, rows, width)
    tiles = width // LANES
    zhs = tms // CORES
    ys = spaces // (CHIPS_X * Z_LO)
    line = zhs * Z_LO * CORES
    plane = ys * CHIPS_X
    flat = layers * rows * tiles
    row_tiles = tiles // SUBLANES
    half_tiles = (rows // CORES - 2) * row_tiles
    chunk = half_tiles // zhs
    copies = 2 * steps + 2 + 3 + 5 * zhs + line + plane
    vmem = pltpu.VMEM

    def in_tiles(array):
        count = array.size // (SUBLANES * width)
        cut = array.reshape(count, SUBLANES, tiles, LANES).transpose(0, 2, 1, 3)
        return cut.reshape(count * tiles * SUBLANES, LANES)

    def block(*shape):
        return vmem((*shape, SUBLANES, LANES), F32)

    total, curvature = pl.pallas_call(
        functools.partial(kernel, dims),
        out_shape=(
            jax.ShapeDtypeStruct((rows, width), F32),
            jax.ShapeDtypeStruct((1, LANES), F32),
        ),
        in_specs=[pl.BlockSpec(memory_space=pl.ANY)] * 6,
        out_specs=(
            pl.BlockSpec(memory_space=pltpu.VMEM),
            pl.BlockSpec(memory_space=pltpu.VMEM),
        ),
        scratch_shapes=[
            vmem((steps * flat, LANES), F32),
            vmem((steps * flat, LANES), F32),
            vmem((steps * flat, LANES), F32),
            vmem((flat, LANES), F32),
            vmem((rows, width), F32),
            vmem((rows, width), F32),
            vmem((rows + 2, steps, 2, layers, width), F32),
            vmem((rows + 1, steps, layers, width), F32),
            vmem((rows + 2, steps, layers, width), F32),
            vmem((rows + 1, layers, width), F32),
            vmem((rows, layers, width), F32),
            vmem((rows + 1, layers, width), F32),
            vmem((rows, layers, width), F32),
            vmem((2, 1, width), F32),
            vmem((2, 1, width), F32),
            block(CORES * half_tiles),
            block(half_tiles),
            block(half_tiles),
            block(zhs, chunk),
            block(CORES, half_tiles),
            block(CORES, 3 * row_tiles),
            block(3 * row_tiles),
            block(zhs, 3 * row_tiles),
            block(zhs, row_tiles),
            block(CORES, 2 * row_tiles),
            vmem((line, 1, LANES), F32),
            vmem((plane, 1, LANES), F32),
            pltpu.SemaphoreType.DMA((2 * steps + 4,)),
            pltpu.SemaphoreType.DMA((copies,)),
            pltpu.SemaphoreType.DMA((copies,)),
        ],
        compiler_params=pltpu.CompilerParams(
            collective_id=0, has_side_effects=True, vmem_limit_bytes=56 << 20
        ),
        cost_estimate=pl.CostEstimate(
            flops=50 * steps * flat * LANES,
            bytes_accessed=14 * steps * flat * LANES,
            transcendentals=rows * width,
        ),
    )(
        in_tiles(pressure),
        in_tiles(mobility),
        in_tiles(capacity),
        in_tiles(misfit_weight),
        log_permeability,
        direction,
    )
    factor = 0.25 / (layers * steps * tms)
    return jnp.exp(log_permeability) * total * factor, curvature[0, 0]


def solution(mesh):
    placed = (
        P("tm", None, None, "space", None),
        P("tm", None, None, "space", None),
        P("tm", None, None, "space", None),
        P("tm", None, "space", None),
        P("space", None),
        P("space", None),
    )
    return jax.shard_map(
        functools.partial(shards, mesh.shape["tm"], mesh.shape["space"]),
        mesh=mesh,
        in_specs=placed,
        out_specs=(P("space", None), P()),
        check_vma=False,
    )
```

```python
import functools

import jax
import jax.numpy as jnp
from jax import lax
from jax.experimental import pallas as pl
from jax.experimental.pallas import tpu as pltpu
from jax.sharding import PartitionSpec as P

LANES = 128
SUBLANES = 8
CHIPS_X = 4
CORES = 2
Z_LO = 2
MESH = pl.DeviceIdType.MESH
F32 = jnp.float32


def kernel(
    dims,
    p_hbm,
    m_hbm,
    c_hbm,
    w_hbm,
    lp_hbm,
    d_hbm,
    out,
    cur,
    pv,
    mv,
    cv,
    wv,
    lpv,
    dv,
    pm,
    fx,
    adj,
    txa,
    ty,
    sbx,
    sby,
    sbb,
    sce,
    rce,
    inner,
    inner_in,
    inner_sum,
    rsb,
    agb,
    edges,
    edges_in,
    edge_z,
    ghost_z,
    final,
    sz,
    sxy,
    local_sem,
    send_sem,
    recv_sem,
):
    tms, spaces, steps, layers, rows, width = dims
    tiles = width // LANES
    zhs = tms // CORES
    ys = spaces // (CHIPS_X * Z_LO)
    zs = zhs * Z_LO
    last = rows
    row_tiles = tiles // SUBLANES
    row_blocks = rows // SUBLANES
    layer_rows = row_blocks * tiles * SUBLANES
    state_rows = layers * layer_rows

    tm = lax.axis_index("tm")
    sp = lax.axis_index("space")
    zh, core = tm // CORES, tm % CORES
    zl = sp % Z_LO
    x = (sp // Z_LO) % CHIPS_X
    y = sp // (Z_LO * CHIPS_X)
    z = zh * Z_LO + zl
    left = (sp + spaces - 1) % spaces
    right = (sp + 1) % spaces
    other = (tm + 1) - 2 * core

    loads = {}

    def load(name, src, dst, index):
        loads[name] = pltpu.make_async_copy(src, dst, local_sem.at[index])
        loads[name].start()

    for s in range(steps):
        part = pl.ds(s * state_rows, state_rows)
        load(("p", s), p_hbm.at[part, :], pv.at[part, :], 2 * s)
        load(("m", s), m_hbm.at[part, :], mv.at[part, :], 2 * s + 1)
    load("lp", lp_hbm, lpv, 2 * steps)
    load("d", d_hbm, dv, 2 * steps + 1)
    load("c", c_hbm, cv, 2 * steps + 2)
    load("w", w_hbm, wv, 2 * steps + 3)

    line = zs * CORES
    my_line = z * CORES + core
    plane = ys * CHIPS_X
    my_plane = y * CHIPS_X + x

    def line_peer(k):
        index = (my_line + k) % line
        to = index // CORES
        return ((to // Z_LO) * CORES + index % CORES, sp - zl + to % Z_LO)

    def plane_peer(k):
        return (tm, ((my_plane + k) % plane) * Z_LO + zl)

    def z_peer(k):
        return (((zh + k) % zhs) * CORES + core, sp)

    greet = [(t, side) for side in (left, right) for t in range(tms)]
    greet += [((tm + k) % tms, sp) for k in range(1, tms)]
    greet += [plane_peer(k) for k in range(1, plane)]
    barrier = pltpu.get_barrier_semaphore()
    for peer in greet:
        pl.semaphore_signal(barrier, inc=1, device_id=peer, device_id_type=MESH)

    sem_count = [0]
    started = []

    def send(src, dst, device, send_index, recv_index):
        copy = pltpu.make_async_remote_copy(
            src_ref=src,
            dst_ref=dst,
            send_sem=send_sem.at[send_index],
            recv_sem=recv_sem.at[recv_index],
            device_id=device,
            device_id_type=MESH,
        )
        copy.start()
        started.append(copy)

    def arrived(dst, recv_index):
        pltpu.make_async_copy(dst, dst, recv_sem.at[recv_index]).wait()

    def take(n):
        first = sem_count[0]
        sem_count[0] += n
        return first

    def layers_of(ref, s, i, j):
        first = (
            s * state_rows + (i // SUBLANES) * (tiles * SUBLANES) + j * SUBLANES + i % SUBLANES
        )
        return ref[pl.ds(first, layers, stride=layer_rows), :]

    def cut(j):
        return slice(j * LANES, (j + 1) * LANES)

    def spread(s, i):
        for which, ref in enumerate((pv, mv)):
            for j in range(tiles):
                pm[i + 1, s, which, :, cut(j)] = layers_of(ref, s, i, j)

    near, far = pl.ds(0, width // 2), pl.ds(width // 2, width // 2)
    halo = take(2 * steps)
    for s in range(steps):
        loads["p", s].wait()
        loads["m", s].wait()
        spread(s, 0)
        spread(s, rows - 1)
        if s == 0:
            pl.semaphore_wait(barrier, len(greet))
        to_left, to_right = (far, near) if s == 0 else (pl.ds(0, width), pl.ds(0, width))
        for row, goal, side, columns, index in (
            (1, last + 1, left, to_left, halo + 2 * s),
            (last, 0, right, to_right, halo + 2 * s + 1),
        ):
            send(
                pm.at[row, s, :, :, columns],
                pm.at[goal, s, :, :, columns],
                (tm, side),
                index,
                index,
            )

    loads["lp"].wait()
    loads["d"].wait()
    scaled = jnp.exp(lpv[...]) * dv[...]
    sce[0] = scaled[0:1, :]
    sce[1] = scaled[rows - 1 : rows, :]
    edge = take(2)
    send(sce.at[0], rce.at[1], (tm, left), edge, edge)
    send(sce.at[1], rce.at[0], (tm, right), edge + 1, edge + 1)

    wide = (layers, width)
    for i in range(rows):
        row = scaled[i : i + 1, :]
        if i + 1 < rows:
            sbx[i + 1] = jnp.broadcast_to(0.25 * (row + scaled[i + 1 : i + 2, :]), wide)
        sby[i] = jnp.broadcast_to(0.25 * (row + pltpu.roll(row, width - 1, 1)), wide)
        sbb[i] = jnp.broadcast_to(0.25 * (row + pltpu.roll(row, 1, 1)), wide)

    def spread_inner(i, carry):
        for s in range(steps):
            spread(s, i)
        return carry

    lax.fori_loop(1, rows - 1, spread_inner, 0)

    lane = lax.broadcasted_iota(jnp.int32, (layers, LANES), 1)
    not_last = lane < LANES - 1
    not_first = lane > 0

    def face_part(f, s, part):
        for j in part:
            c = cut(j)
            fx[f, s, :, c] = (pm[f, s, 1, :, c] + pm[f + 1, s, 1, :, c]) * (
                pm[f + 1, s, 0, :, c] - pm[f, s, 0, :, c]
            )

    def face_x(f, carry):
        for s in range(steps):
            face_part(f, s, range(tiles))
        return carry

    def cell_row(r, curvature):
        i = r - 1

        def ahead(here, later):
            return jnp.where(not_last, here, later)

        def turned(s, j):
            pressure, mobility = pm[r, s, 0, :, cut(j)], pm[r, s, 1, :, cut(j)]
            return (
                pressure,
                mobility,
                pltpu.roll(pressure, LANES - 1, 1),
                pltpu.roll(mobility, LANES - 1, 1),
            )

        here = [turned(s, 0) for s in range(steps)]
        spill = [0.0] * steps
        for j in range(tiles):
            c = cut(j)
            low, high = None, None
            for s in range(steps):
                pressure, mobility, p_back, m_back = here[s]
                if j + 1 < tiles:
                    here[s] = turned(s, j + 1)
                    p_next, m_next = here[s][2], here[s][3]
                else:
                    p_next, m_next = pressure, mobility
                face = (mobility + ahead(m_back, m_next)) * (ahead(p_back, p_next) - pressure)
                turned_face = pltpu.roll(face, 1, 1)
                before = jnp.where(not_first, turned_face, spill[s])
                spill[s] = turned_face
                change = (
                    fx[r, s, :, c] * sbx[r, :, c]
                    - fx[r - 1, s, :, c] * sbx[r - 1, :, c]
                    + (face * sby[i, :, c] - before * sbb[i, :, c])
                )
                square = layers_of(cv, s, i, j)
                square = square * square
                inverse = pl.reciprocal(square, approx=True)
                inverse = inverse * (2.0 - square * inverse)
                value = layers_of(wv, 0, i, j) * change * inverse
                adj[r, s, :, c] = value
                curvature = curvature + value * change
                low = face * value if low is None else low + face * value
                high = before * value if high is None else high + before * value
            ty[i, 0, :, c] = low
            ty[i, 1, :, c] = high
        return curvature

    def face_terms(f, low=True, high=True):
        for j in range(tiles):
            c = cut(j)
            total = None
            for s in range(steps):
                if low and high:
                    difference = adj[f, s, :, c] - adj[f + 1, s, :, c]
                elif low:
                    difference = adj[f, s, :, c]
                else:
                    difference = -adj[f + 1, s, :, c]
                value = fx[f, s, :, c] * difference
                total = value if total is None else total + value
            txa[f, :, c] = total

    sub = lax.broadcasted_iota(jnp.int32, (SUBLANES, LANES), 0)
    below = [(sub // d) % 2 == 0 for d in (1, 2, 4)]

    def fold(values):
        for bit, d in enumerate((1, 2, 4)):
            pairs = zip(values[::2], values[1::2])
            values = [
                jnp.where(below[bit], a, b) + pltpu.roll(jnp.where(below[bit], b, a), d, 0)
                for a, b in pairs
            ]
        return values[0]

    def folded(get):
        return [
            fold([get(cut(g * SUBLANES + k)) for k in range(SUBLANES)]) for g in range(row_tiles)
        ]

    def pack_total(dst, first, i):
        own = folded(
            lambda c: txa[i, :, c] + txa[i + 1, :, c] + (ty[i, 0, :, c] - ty[i, 1, :, c])
        )
        low = [pltpu.roll(v, 1, 1) for v in folded(lambda c: ty[i, 0, :, c])]
        high = [pltpu.roll(v, LANES - 1, 1) for v in folded(lambda c: ty[i, 1, :, c])]
        zero = jnp.zeros((SUBLANES, LANES), F32)
        low_down = [pltpu.roll(v, 1, 0) for v in low]
        high_up = [pltpu.roll(v, SUBLANES - 1, 0) for v in high]
        for g in range(row_tiles):
            prior = low_down[g - 1] if g else zero
            after = high_up[g + 1] if g + 1 < row_tiles else zero
            from_low = jnp.where(not_first, low[g], jnp.where(sub > 0, low_down[g], prior))
            from_high = jnp.where(
                not_last, high[g], jnp.where(sub < SUBLANES - 1, high_up[g], after)
            )
            dst[first + g] = own[g] + from_low - from_high

    lax.fori_loop(1, rows, face_x, 0)
    loads["c"].wait()
    loads["w"].wait()
    curvature = lax.fori_loop(2, rows, cell_row, jnp.zeros((layers, LANES), F32))

    def inner_faces(f, carry):
        face_terms(f)
        return carry

    lax.fori_loop(2, rows - 1, inner_faces, 0)

    def inner_rows(i, carry):
        pack_total(inner, (i - 2) * row_tiles, i)
        return carry

    lax.fori_loop(2, rows - 2, inner_rows, 0)

    half_tiles = (rows // CORES - 2) * row_tiles
    chunk = half_tiles // zhs
    inner_pair = take(1)
    send(
        inner.at[pl.ds((1 - core) * half_tiles, half_tiles)],
        inner_in,
        (other, sp),
        inner_pair,
        inner_pair,
    )

    near_tiles, far_tiles = range(tiles // 2), range(tiles // 2, tiles)
    product = take(2)
    arrived(pm.at[0, 0, :, :, near], halo + 1)
    face_part(0, 0, near_tiles)
    to_left, to_right = fx.at[0, 0, :, near], fx.at[last, 0, :, far]
    send(to_left, fx.at[last, 0, :, near], (tm, left), product, product)
    arrived(pm.at[last + 1, 0, :, :, far], halo)
    face_part(last, 0, far_tiles)
    send(to_right, fx.at[0, 0, :, far], (tm, right), product + 1, product + 1)
    products = [started.pop(), started.pop()]

    arrived(inner_in, inner_pair)
    inner_sum[...] = inner[pl.ds(core * half_tiles, half_tiles)] + inner_in[...]
    scatter = take(zhs)
    for k in range(1, zhs):
        to = (zh + k) % zhs
        send(
            inner_sum.at[pl.ds(to * chunk, chunk)],
            rsb.at[k],
            z_peer(k),
            scatter + k,
            scatter + k,
        )

    arrived(rce.at[0], edge + 1)
    arrived(rce.at[1], edge)
    sbx[0] = jnp.broadcast_to(0.25 * (rce[0] + scaled[0:1, :]), wide)
    sbx[last] = jnp.broadcast_to(0.25 * (rce[1] + scaled[rows - 1 : rows, :]), wide)
    for s in range(1, steps):
        arrived(pm.at[last + 1, s], halo + 2 * s)
        arrived(pm.at[0, s], halo + 2 * s + 1)
        face_part(0, s, range(tiles))
        face_part(last, s, range(tiles))
    arrived(fx.at[last, 0, :, near], product)
    arrived(fx.at[0, 0, :, far], product + 1)

    for copy in products:
        copy.wait_send()

    @pl.when(sp == 0)
    def _():
        fx[0] = jnp.zeros((steps, layers, width), F32)

    @pl.when(sp == spaces - 1)
    def _():
        fx[last] = jnp.zeros((steps, layers, width), F32)

    curvature = lax.fori_loop(0, 2, lambda k, carry: cell_row(1 + k * (rows - 1), carry), curvature)

    sz[my_line] = jnp.sum(curvature, axis=0, keepdims=True)
    over_line = take(line)
    for k in range(1, line):
        send(sz.at[my_line], sz.at[my_line], line_peer(k), over_line + k, over_line + k)

    face_terms(0, low=False)
    face_terms(last, high=False)
    face_terms(1)
    face_terms(rows - 1)
    for c, (edge_row, inner_row, face) in enumerate(((0, 1, 0), (rows - 1, rows - 2, last))):
        pack_total(edges.at[c], 0, edge_row)
        pack_total(edges.at[c], row_tiles, inner_row)
        for g, value in enumerate(folded(lambda k: txa[face, :, k])):
            edges[c, 2 * row_tiles + g] = value
    edge_pair = take(1)
    send(edges.at[1 - core], edges_in, (other, sp), edge_pair, edge_pair)

    reduced = inner_sum[pl.ds(zh * chunk, chunk)]
    for k in range(1, zhs):
        arrived(rsb.at[k], scatter + k)
        reduced = reduced + rsb[k]
    agb[core, pl.ds(zh * chunk, chunk)] = reduced
    mine = agb.at[core, pl.ds(zh * chunk, chunk)]
    gather = take(zhs)
    forward = take(zhs)
    for k in range(1, zhs):
        send(mine, mine, z_peer(k), gather + k, gather + k)
    send(mine, mine, (other, sp), forward, forward)

    two = 2 * row_tiles
    arrived(edges_in, edge_pair)
    summed = edges[core] + edges_in[...]
    edge_z[zh] = summed
    over_z = take(zhs)
    ghost = take(zhs)
    for k in range(1, zhs):
        send(
            edge_z.at[zh, pl.ds(0, two)],
            edge_z.at[zh, pl.ds(0, two)],
            z_peer(k),
            over_z + k,
            over_z + k,
        )
    side = left + core * (right - left)
    for k in range(zhs):
        send(
            edge_z.at[zh, pl.ds(two, row_tiles)],
            ghost_z.at[zh],
            (((zh + k) % zhs) * CORES + 1 - core, side),
            ghost + k,
            ghost + k,
        )

    for k in range(1, line):
        arrived(sz.at[(my_line + line - k) % line], over_line + k)
    sxy[my_plane] = jnp.sum(sz[...], axis=0)
    over_plane = take(plane)
    for k in range(1, plane):
        send(sxy.at[my_plane], sxy.at[my_plane], plane_peer(k), over_plane + k, over_plane + k)

    def unpack(src, first, i):
        for j in range(tiles):
            low = j % SUBLANES
            out[i : i + 1, cut(j)] = src[first + j // SUBLANES, low : low + 1, :]

    for k in range(1, zhs):
        whose = agb.at[core, pl.ds(((zh + zhs - k) % zhs) * chunk, chunk)]
        arrived(whose, gather + k)
        send(whose, whose, (other, sp), forward + k, forward + k)

    for k in range(1, zhs):
        arrived(edge_z.at[(zh + zhs - k) % zhs, pl.ds(0, two)], over_z + k)
    for k in range(zhs):
        arrived(ghost_z.at[(zh + zhs - k) % zhs], ghost + k)
    total = edge_z[0, 0:two]
    beyond = ghost_z[0]
    for k in range(1, zhs):
        total = total + edge_z[k, 0:two]
        beyond = beyond + ghost_z[k]
    final[core, pl.ds(0, row_tiles)] = total[:row_tiles] + beyond
    final[core, pl.ds(row_tiles, row_tiles)] = total[row_tiles:]
    final_pair = take(1)
    send(final.at[core], final.at[core], (other, sp), final_pair, final_pair)

    for k in range(zhs):
        whose = agb.at[1 - core, pl.ds(((zh + zhs - k) % zhs) * chunk, chunk)]
        arrived(whose, forward + k)
    for i in range(2, rows - 2):
        first = (i - 2) * row_tiles
        unpack(agb.at[first // half_tiles], first % half_tiles, i)
    arrived(final.at[1 - core], final_pair)
    for c, (edge_row, inner_row) in enumerate(((0, 1), (rows - 1, rows - 2))):
        unpack(final.at[c], 0, edge_row)
        unpack(final.at[c], row_tiles, inner_row)

    for k in range(1, plane):
        arrived(sxy.at[(my_plane + plane - k) % plane], over_plane + k)
    whole = jnp.sum(sxy[...], axis=0)
    scale = 1.0 / (layers * steps * tms * rows * spaces * width)
    cur[...] = jnp.broadcast_to(jnp.sum(whole, axis=1, keepdims=True) * scale, cur.shape)

    for copy in started:
        copy.wait_send()


def shards(tms, spaces, pressure, mobility, capacity, misfit_weight, log_permeability, direction):
    _, steps, layers, rows, width = pressure.shape
    dims = (tms, spaces, steps, layers, rows, width)
    tiles = width // LANES
    zhs = tms // CORES
    ys = spaces // (CHIPS_X * Z_LO)
    line = zhs * Z_LO * CORES
    plane = ys * CHIPS_X
    flat = layers * rows * tiles
    row_tiles = tiles // SUBLANES
    half_tiles = (rows // CORES - 2) * row_tiles
    chunk = half_tiles // zhs
    copies = 2 * steps + 4 + 3 + 5 * zhs + line + plane
    vmem = pltpu.VMEM

    def in_tiles(array):
        count = array.size // (SUBLANES * width)
        cut = array.reshape(count, SUBLANES, tiles, LANES).transpose(0, 2, 1, 3)
        return cut.reshape(count * tiles * SUBLANES, LANES)

    def block(*shape):
        return vmem((*shape, SUBLANES, LANES), F32)

    total, curvature = pl.pallas_call(
        functools.partial(kernel, dims),
        out_shape=(
            jax.ShapeDtypeStruct((rows, width), F32),
            jax.ShapeDtypeStruct((1, LANES), F32),
        ),
        in_specs=[pl.BlockSpec(memory_space=pl.ANY)] * 6,
        out_specs=(
            pl.BlockSpec(memory_space=pltpu.VMEM),
            pl.BlockSpec(memory_space=pltpu.VMEM),
        ),
        scratch_shapes=[
            vmem((steps * flat, LANES), F32),
            vmem((steps * flat, LANES), F32),
            vmem((steps * flat, LANES), F32),
            vmem((flat, LANES), F32),
            vmem((rows, width), F32),
            vmem((rows, width), F32),
            vmem((rows + 2, steps, 2, layers, width), F32),
            vmem((rows + 1, steps, layers, width), F32),
            vmem((rows + 2, steps, layers, width), F32),
            vmem((rows + 1, layers, width), F32),
            vmem((rows, 2, layers, width), F32),
            vmem((rows + 1, layers, width), F32),
            vmem((rows, layers, width), F32),
            vmem((rows, layers, width), F32),
            vmem((2, 1, width), F32),
            vmem((2, 1, width), F32),
            block(CORES * half_tiles),
            block(half_tiles),
            block(half_tiles),
            block(zhs, chunk),
            block(CORES, half_tiles),
            block(CORES, 3 * row_tiles),
            block(3 * row_tiles),
            block(zhs, 3 * row_tiles),
            block(zhs, row_tiles),
            block(CORES, 2 * row_tiles),
            vmem((line, 1, LANES), F32),
            vmem((plane, 1, LANES), F32),
            pltpu.SemaphoreType.DMA((2 * steps + 4,)),
            pltpu.SemaphoreType.DMA((copies,)),
            pltpu.SemaphoreType.DMA((copies,)),
        ],
        compiler_params=pltpu.CompilerParams(
            collective_id=0, has_side_effects=True, vmem_limit_bytes=56 << 20
        ),
        cost_estimate=pl.CostEstimate(
            flops=50 * steps * flat * LANES,
            bytes_accessed=14 * steps * flat * LANES,
            transcendentals=rows * width,
        ),
    )(
        in_tiles(pressure),
        in_tiles(mobility),
        in_tiles(capacity),
        in_tiles(misfit_weight),
        log_permeability,
        direction,
    )
    factor = 0.25 / (layers * steps * tms)
    return jnp.exp(log_permeability) * total * factor, curvature[0, 0]


def solution(mesh):
    placed = (
        P("tm", None, None, "space", None),
        P("tm", None, None, "space", None),
        P("tm", None, None, "space", None),
        P("tm", None, "space", None),
        P("space", None),
        P("space", None),
    )
    return jax.shard_map(
        functools.partial(shards, mesh.shape["tm"], mesh.shape["space"]),
        mesh=mesh,
        in_specs=placed,
        out_specs=(P("space", None), P()),
        check_vma=False,
    )
```

```python
import functools

import jax
import jax.numpy as jnp
from jax import lax
from jax.experimental import pallas as pl
from jax.experimental.pallas import tpu as pltpu
from jax.sharding import PartitionSpec as P

LANES = 128
SUBLANES = 8
CHIPS_X = 4
CORES = 2
Z_LO = 2
MESH = pl.DeviceIdType.MESH
F32 = jnp.float32


def kernel(
    dims,
    p_hbm,
    m_hbm,
    c_hbm,
    w_hbm,
    lp_hbm,
    d_hbm,
    out,
    cur,
    pv,
    mv,
    cv,
    wv,
    lpv,
    dv,
    pm,
    fx,
    adj,
    txa,
    ty,
    sbx,
    sby,
    sbb,
    factor,
    px,
    sce,
    rce,
    inner,
    inner_in,
    inner_sum,
    rsb,
    agb,
    edges,
    edges_in,
    edge_z,
    ghost_z,
    final,
    sz,
    sxy,
    local_sem,
    send_sem,
    recv_sem,
):
    tms, spaces, steps, layers, rows, width = dims
    tiles = width // LANES
    zhs = tms // CORES
    ys = spaces // (CHIPS_X * Z_LO)
    zs = zhs * Z_LO
    last = rows
    row_tiles = tiles // SUBLANES
    row_blocks = rows // SUBLANES
    layer_rows = row_blocks * tiles * SUBLANES
    state_rows = layers * layer_rows

    tm = lax.axis_index("tm")
    sp = lax.axis_index("space")
    zh, core = tm // CORES, tm % CORES
    zl = sp % Z_LO
    x = (sp // Z_LO) % CHIPS_X
    y = sp // (Z_LO * CHIPS_X)
    z = zh * Z_LO + zl
    left = (sp + spaces - 1) % spaces
    right = (sp + 1) % spaces
    other = (tm + 1) - 2 * core

    loads = {}

    def load(name, src, dst, index):
        loads[name] = pltpu.make_async_copy(src, dst, local_sem.at[index])
        loads[name].start()

    for s in range(steps):
        part = pl.ds(s * state_rows, state_rows)
        load(("p", s), p_hbm.at[part, :], pv.at[part, :], 2 * s)
        load(("m", s), m_hbm.at[part, :], mv.at[part, :], 2 * s + 1)
    load("lp", lp_hbm, lpv, 2 * steps)
    load("d", d_hbm, dv, 2 * steps + 1)

    line = zs * CORES
    my_line = z * CORES + core
    plane = ys * CHIPS_X
    my_plane = y * CHIPS_X + x

    def line_peer(k):
        index = (my_line + k) % line
        to = index // CORES
        return ((to // Z_LO) * CORES + index % CORES, sp - zl + to % Z_LO)

    def plane_peer(k):
        return (tm, ((my_plane + k) % plane) * Z_LO + zl)

    def z_peer(k):
        return (((zh + k) % zhs) * CORES + core, sp)

    greet = [(t, side) for side in (left, right) for t in range(tms)]
    greet += [((tm + k) % tms, sp) for k in range(1, tms)]
    greet += [plane_peer(k) for k in range(1, plane)]
    barrier = pltpu.get_barrier_semaphore()
    for peer in greet:
        pl.semaphore_signal(barrier, inc=1, device_id=peer, device_id_type=MESH)

    sem_count = [0]
    started = []

    def send(src, dst, device, send_index, recv_index):
        copy = pltpu.make_async_remote_copy(
            src_ref=src,
            dst_ref=dst,
            send_sem=send_sem.at[send_index],
            recv_sem=recv_sem.at[recv_index],
            device_id=device,
            device_id_type=MESH,
        )
        copy.start()
        started.append(copy)

    def arrived(dst, recv_index):
        pltpu.make_async_copy(dst, dst, recv_sem.at[recv_index]).wait()

    def take(n):
        first = sem_count[0]
        sem_count[0] += n
        return first

    def layers_of(ref, s, i, j):
        first = (
            s * state_rows + (i // SUBLANES) * (tiles * SUBLANES) + j * SUBLANES + i % SUBLANES
        )
        return ref[pl.ds(first, layers, stride=layer_rows), :]

    def cut(j):
        return slice(j * LANES, (j + 1) * LANES)

    def spread(s, i):
        for which, ref in enumerate((pv, mv)):
            for j in range(tiles):
                pm[i + 1, s, which, :, cut(j)] = layers_of(ref, s, i, j)

    near, far = pl.ds(0, width // 2), pl.ds(width // 2, width // 2)
    halo = take(2 * steps)
    for s in range(steps):
        loads["p", s].wait()
        loads["m", s].wait()
        spread(s, 0)
        spread(s, rows - 1)
        if s == 0:
            load("c", c_hbm, cv, 2 * steps + 2)
            load("w", w_hbm, wv, 2 * steps + 3)
            pl.semaphore_wait(barrier, len(greet))
        to_left, to_right = (far, near) if s == 0 else (pl.ds(0, width), pl.ds(0, width))
        for row, goal, side, columns, index in (
            (1, last + 1, left, to_left, halo + 2 * s),
            (last, 0, right, to_right, halo + 2 * s + 1),
        ):
            send(
                pm.at[row, s, :, :, columns],
                pm.at[goal, s, :, :, columns],
                (tm, side),
                index,
                index,
            )

    loads["lp"].wait()
    loads["d"].wait()
    conduct = jnp.exp(lpv[...])
    factor[...] = conduct * (0.25 / (layers * steps * tms))
    scaled = conduct * dv[...]
    sce[0] = scaled[0:1, :]
    sce[1] = scaled[rows - 1 : rows, :]
    edge = take(2)
    send(sce.at[0], rce.at[1], (tm, left), edge, edge)
    send(sce.at[1], rce.at[0], (tm, right), edge + 1, edge + 1)

    wide = (layers, width)
    for i in range(rows):
        row = scaled[i : i + 1, :]
        if i + 1 < rows:
            sbx[i + 1] = jnp.broadcast_to(0.25 * (row + scaled[i + 1 : i + 2, :]), wide)
        sby[i] = jnp.broadcast_to(0.25 * (row + pltpu.roll(row, width - 1, 1)), wide)
        sbb[i] = jnp.broadcast_to(0.25 * (row + pltpu.roll(row, 1, 1)), wide)

    def spread_inner(i, carry):
        for s in range(steps):
            spread(s, i)
        return carry

    lax.fori_loop(1, rows - 1, spread_inner, 0)

    lane = lax.broadcasted_iota(jnp.int32, (layers, LANES), 1)
    not_last = lane < LANES - 1
    not_first = lane > 0

    def face_part(f, s, part):
        for j in part:
            c = cut(j)
            fx[f, s, :, c] = (pm[f, s, 1, :, c] + pm[f + 1, s, 1, :, c]) * (
                pm[f + 1, s, 0, :, c] - pm[f, s, 0, :, c]
            )

    def face_x(f, carry):
        for s in range(steps):
            face_part(f, s, range(tiles))
        return carry

    def cell_row(r, curvature, states=range(steps), add=False):
        i = r - 1

        def ahead(here, later):
            return jnp.where(not_last, here, later)

        def turned(s, j):
            pressure, mobility = pm[r, s, 0, :, cut(j)], pm[r, s, 1, :, cut(j)]
            return (
                pressure,
                mobility,
                pltpu.roll(pressure, LANES - 1, 1),
                pltpu.roll(mobility, LANES - 1, 1),
            )

        here = {s: turned(s, 0) for s in states}
        spill = {s: 0.0 for s in states}
        for j in range(tiles):
            c = cut(j)
            piece = pl.ds(j * SUBLANES, SUBLANES)
            low, high = (ty[i, 0, piece, :], ty[i, 1, piece, :]) if add else (None, None)
            for s in states:
                pressure, mobility, p_back, m_back = here[s]
                if j + 1 < tiles:
                    here[s] = turned(s, j + 1)
                    p_next, m_next = here[s][2], here[s][3]
                else:
                    p_next, m_next = pressure, mobility
                face = (mobility + ahead(m_back, m_next)) * (ahead(p_back, p_next) - pressure)
                turned_face = pltpu.roll(face, 1, 1)
                before = jnp.where(not_first, turned_face, spill[s])
                spill[s] = turned_face
                change = (
                    fx[r, s, :, c] * sbx[r, :, c]
                    - fx[r - 1, s, :, c] * sbx[r - 1, :, c]
                    + (face * sby[i, :, c] - before * sbb[i, :, c])
                )
                square = layers_of(cv, s, i, j)
                square = square * square
                inverse = pl.reciprocal(square, approx=True)
                inverse = inverse * (2.0 - square * inverse)
                value = layers_of(wv, 0, i, j) * change * inverse
                adj[r, s, :, c] = value
                curvature = curvature + value * change
                low = face * value if low is None else low + face * value
                high = before * value if high is None else high + before * value
            ty[i, 0, piece, :] = low
            ty[i, 1, piece, :] = high
        return curvature

    sub = lax.broadcasted_iota(jnp.int32, (SUBLANES, LANES), 0)

    def packed(get):
        values = []
        for g in range(row_tiles):
            first = g * SUBLANES * SUBLANES
            parts = [
                get(pl.ds(first + k, SUBLANES, stride=SUBLANES)) for k in range(layers)
            ]
            while len(parts) > 1:
                parts = [a + b for a, b in zip(parts[::2], parts[1::2])]
            values.append(parts[0])
        return values

    def shifted(values, ahead):
        turn, keep, whole = (
            (LANES - 1, not_last, sub < SUBLANES - 1) if ahead else (1, not_first, sub > 0)
        )
        values = [pltpu.roll(v, turn, 1) for v in values]
        moved = [pltpu.roll(v, SUBLANES - 1 if ahead else 1, 0) for v in values]
        outside = moved[1:] + [0.0] if ahead else [0.0] + moved[:-1]
        return [
            jnp.where(keep, v, jnp.where(whole, m, o)) for v, m, o in zip(values, moved, outside)
        ]

    def face_terms(f, low=True, high=True):
        for j in range(tiles):
            c = cut(j)
            total = None
            for s in range(steps):
                if low and high:
                    difference = adj[f, s, :, c] - adj[f + 1, s, :, c]
                elif low:
                    difference = adj[f, s, :, c]
                else:
                    difference = -adj[f + 1, s, :, c]
                value = fx[f, s, :, c] * difference
                total = value if total is None else total + value
            txa[f, pl.ds(j * SUBLANES, SUBLANES), :] = total
        for g, value in enumerate(packed(lambda rows_of: txa[f, rows_of, :])):
            px[f, g] = value

    def pack_total(dst, first, i):
        low = packed(lambda rows_of: ty[i, 0, rows_of, :])
        high = packed(lambda rows_of: ty[i, 1, rows_of, :])
        term = [a - b for a, b in zip(low, shifted(high, True))]
        for g, (a, b) in enumerate(zip(term, shifted(term, False))):
            dst[first + g] = px[i, g] + px[i + 1, g] + (a + b)

    lax.fori_loop(1, rows, face_x, 0)
    loads["c"].wait()
    loads["w"].wait()
    curvature = lax.fori_loop(2, rows, cell_row, jnp.zeros((layers, LANES), F32))

    near_tiles, far_tiles = range(tiles // 2), range(tiles // 2, tiles)
    product = take(2)
    arrived(pm.at[0, 0, :, :, near], halo + 1)
    face_part(0, 0, near_tiles)
    to_left, to_right = fx.at[0, 0, :, near], fx.at[last, 0, :, far]
    send(to_left, fx.at[last, 0, :, near], (tm, left), product, product)
    arrived(pm.at[last + 1, 0, :, :, far], halo)
    face_part(last, 0, far_tiles)
    send(to_right, fx.at[0, 0, :, far], (tm, right), product + 1, product + 1)
    products = [started.pop(), started.pop()]

    def inner_faces(f, carry):
        face_terms(f)
        return carry

    lax.fori_loop(2, rows - 1, inner_faces, 0)

    def inner_rows(i, carry):
        pack_total(inner, (i - 2) * row_tiles, i)
        return carry

    lax.fori_loop(2, rows - 2, inner_rows, 0)

    half_tiles = (rows // CORES - 2) * row_tiles
    chunk = half_tiles // zhs
    inner_pair = take(1)
    send(
        inner.at[pl.ds((1 - core) * half_tiles, half_tiles)],
        inner_in,
        (other, sp),
        inner_pair,
        inner_pair,
    )

    arrived(inner_in, inner_pair)
    inner_sum[...] = inner[pl.ds(core * half_tiles, half_tiles)] + inner_in[...]
    scatter = take(zhs)
    for k in range(1, zhs):
        to = (zh + k) % zhs
        send(
            inner_sum.at[pl.ds(to * chunk, chunk)],
            rsb.at[k],
            z_peer(k),
            scatter + k,
            scatter + k,
        )

    arrived(rce.at[0], edge + 1)
    arrived(rce.at[1], edge)
    sbx[0] = jnp.broadcast_to(0.25 * (rce[0] + scaled[0:1, :]), wide)
    sbx[last] = jnp.broadcast_to(0.25 * (rce[1] + scaled[rows - 1 : rows, :]), wide)
    for s in range(1, steps):
        arrived(pm.at[last + 1, s], halo + 2 * s)
        arrived(pm.at[0, s], halo + 2 * s + 1)
        face_part(0, s, range(tiles))
        face_part(last, s, range(tiles))

    def no_face(states):
        @pl.when(sp == 0)
        def _():
            for s in states:
                fx[0, s] = jnp.zeros(wide, F32)

        @pl.when(sp == spaces - 1)
        def _():
            for s in states:
                fx[last, s] = jnp.zeros(wide, F32)

    def edge_rows(states, add, curvature):
        return lax.fori_loop(
            0, 2, lambda k, carry: cell_row(1 + k * (rows - 1), carry, states, add), curvature
        )

    no_face(range(1, steps))
    curvature = edge_rows(range(1, steps), False, curvature)
    arrived(fx.at[last, 0, :, near], product)
    arrived(fx.at[0, 0, :, far], product + 1)
    for copy in products:
        copy.wait_send()
    no_face(range(1))
    curvature = edge_rows(range(1), True, curvature)

    sz[my_line] = jnp.sum(curvature, axis=0, keepdims=True)
    over_line = take(line)
    for k in range(1, line):
        send(sz.at[my_line], sz.at[my_line], line_peer(k), over_line + k, over_line + k)

    face_terms(0, low=False)
    face_terms(last, high=False)
    face_terms(1)
    face_terms(rows - 1)
    for c, (edge_row, inner_row, face) in enumerate(((0, 1, 0), (rows - 1, rows - 2, last))):
        pack_total(edges.at[c], 0, edge_row)
        pack_total(edges.at[c], row_tiles, inner_row)
        edges[c, pl.ds(2 * row_tiles, row_tiles)] = px[face]
    edge_pair = take(1)
    send(edges.at[1 - core], edges_in, (other, sp), edge_pair, edge_pair)

    reduced = inner_sum[pl.ds(zh * chunk, chunk)]
    for k in range(1, zhs):
        arrived(rsb.at[k], scatter + k)
        reduced = reduced + rsb[k]
    agb[core, pl.ds(zh * chunk, chunk)] = reduced
    mine = agb.at[core, pl.ds(zh * chunk, chunk)]
    gather = take(zhs)
    forward = take(zhs)
    for k in range(1, zhs):
        send(mine, mine, z_peer(k), gather + k, gather + k)
    send(mine, mine, (other, sp), forward, forward)

    two = 2 * row_tiles
    arrived(edges_in, edge_pair)
    summed = edges[core] + edges_in[...]
    edge_z[zh] = summed
    over_z = take(zhs)
    ghost = take(zhs)
    for k in range(1, zhs):
        send(
            edge_z.at[zh, pl.ds(0, two)],
            edge_z.at[zh, pl.ds(0, two)],
            z_peer(k),
            over_z + k,
            over_z + k,
        )
    side = left + core * (right - left)
    for k in range(zhs):
        send(
            edge_z.at[zh, pl.ds(two, row_tiles)],
            ghost_z.at[zh],
            (((zh + k) % zhs) * CORES + 1 - core, side),
            ghost + k,
            ghost + k,
        )

    for k in range(1, line):
        arrived(sz.at[(my_line + line - k) % line], over_line + k)
    sxy[my_plane] = jnp.sum(sz[...], axis=0)
    over_plane = take(plane)
    for k in range(1, plane):
        send(sxy.at[my_plane], sxy.at[my_plane], plane_peer(k), over_plane + k, over_plane + k)

    def unpack(src, first, i):
        for j in range(tiles):
            low = j % SUBLANES
            value = src[first + j // SUBLANES, low : low + 1, :]
            out[i : i + 1, cut(j)] = value * factor[i : i + 1, cut(j)]

    for k in range(1, zhs):
        whose = agb.at[core, pl.ds(((zh + zhs - k) % zhs) * chunk, chunk)]
        arrived(whose, gather + k)
        send(whose, whose, (other, sp), forward + k, forward + k)

    for k in range(1, zhs):
        arrived(edge_z.at[(zh + zhs - k) % zhs, pl.ds(0, two)], over_z + k)
    for k in range(zhs):
        arrived(ghost_z.at[(zh + zhs - k) % zhs], ghost + k)
    total = edge_z[0, 0:two]
    beyond = ghost_z[0]
    for k in range(1, zhs):
        total = total + edge_z[k, 0:two]
        beyond = beyond + ghost_z[k]
    final[core, pl.ds(0, row_tiles)] = total[:row_tiles] + beyond
    final[core, pl.ds(row_tiles, row_tiles)] = total[row_tiles:]
    final_pair = take(1)
    send(final.at[core], final.at[core], (other, sp), final_pair, final_pair)

    for k in range(zhs):
        whose = agb.at[1 - core, pl.ds(((zh + zhs - k) % zhs) * chunk, chunk)]
        arrived(whose, forward + k)
    for i in range(2, rows - 2):
        first = (i - 2) * row_tiles
        unpack(agb.at[first // half_tiles], first % half_tiles, i)
    arrived(final.at[1 - core], final_pair)
    for c, (edge_row, inner_row) in enumerate(((0, 1), (rows - 1, rows - 2))):
        unpack(final.at[c], 0, edge_row)
        unpack(final.at[c], row_tiles, inner_row)

    for k in range(1, plane):
        arrived(sxy.at[(my_plane + plane - k) % plane], over_plane + k)
    whole = jnp.sum(sxy[...], axis=0)
    scale = 1.0 / (layers * steps * tms * rows * spaces * width)
    cur[...] = jnp.broadcast_to(jnp.sum(whole, axis=1, keepdims=True) * scale, cur.shape)

    for copy in started:
        copy.wait_send()


def shards(tms, spaces, pressure, mobility, capacity, misfit_weight, log_permeability, direction):
    _, steps, layers, rows, width = pressure.shape
    dims = (tms, spaces, steps, layers, rows, width)
    tiles = width // LANES
    zhs = tms // CORES
    ys = spaces // (CHIPS_X * Z_LO)
    line = zhs * Z_LO * CORES
    plane = ys * CHIPS_X
    flat = layers * rows * tiles
    row_tiles = tiles // SUBLANES
    half_tiles = (rows // CORES - 2) * row_tiles
    chunk = half_tiles // zhs
    copies = 2 * steps + 4 + 3 + 5 * zhs + line + plane
    vmem = pltpu.VMEM

    def in_tiles(array):
        count = array.size // (SUBLANES * width)
        cut = array.reshape(count, SUBLANES, tiles, LANES).transpose(0, 2, 1, 3)
        return cut.reshape(count * tiles * SUBLANES, LANES)

    def block(*shape):
        return vmem((*shape, SUBLANES, LANES), F32)

    product, curvature = pl.pallas_call(
        functools.partial(kernel, dims),
        out_shape=(
            jax.ShapeDtypeStruct((rows, width), F32),
            jax.ShapeDtypeStruct((1, LANES), F32),
        ),
        in_specs=[pl.BlockSpec(memory_space=pl.ANY)] * 6,
        out_specs=(
            pl.BlockSpec(memory_space=pltpu.VMEM),
            pl.BlockSpec(memory_space=pltpu.VMEM),
        ),
        scratch_shapes=[
            vmem((steps * flat, LANES), F32),
            vmem((steps * flat, LANES), F32),
            vmem((steps * flat, LANES), F32),
            vmem((flat, LANES), F32),
            vmem((rows, width), F32),
            vmem((rows, width), F32),
            vmem((rows + 2, steps, 2, layers, width), F32),
            vmem((rows + 1, steps, layers, width), F32),
            vmem((rows + 2, steps, layers, width), F32),
            vmem((rows + 1, tiles * layers, LANES), F32),
            vmem((rows, 2, tiles * layers, LANES), F32),
            vmem((rows + 1, layers, width), F32),
            vmem((rows, layers, width), F32),
            vmem((rows, layers, width), F32),
            vmem((rows, width), F32),
            block(rows + 1, row_tiles),
            vmem((2, 1, width), F32),
            vmem((2, 1, width), F32),
            block(CORES * half_tiles),
            block(half_tiles),
            block(half_tiles),
            block(zhs, chunk),
            block(CORES, half_tiles),
            block(CORES, 3 * row_tiles),
            block(3 * row_tiles),
            block(zhs, 3 * row_tiles),
            block(zhs, row_tiles),
            block(CORES, 2 * row_tiles),
            vmem((line, 1, LANES), F32),
            vmem((plane, 1, LANES), F32),
            pltpu.SemaphoreType.DMA((2 * steps + 4,)),
            pltpu.SemaphoreType.DMA((copies,)),
            pltpu.SemaphoreType.DMA((copies,)),
        ],
        compiler_params=pltpu.CompilerParams(
            collective_id=0, has_side_effects=True, vmem_limit_bytes=56 << 20
        ),
        cost_estimate=pl.CostEstimate(
            flops=50 * steps * flat * LANES,
            bytes_accessed=14 * steps * flat * LANES,
            transcendentals=rows * width,
        ),
    )(
        in_tiles(pressure),
        in_tiles(mobility),
        in_tiles(capacity),
        in_tiles(misfit_weight),
        log_permeability,
        direction,
    )
    return product, curvature[0, 0]


def solution(mesh):
    placed = (
        P("tm", None, None, "space", None),
        P("tm", None, None, "space", None),
        P("tm", None, None, "space", None),
        P("tm", None, "space", None),
        P("space", None),
        P("space", None),
    )
    return jax.shard_map(
        functools.partial(shards, mesh.shape["tm"], mesh.shape["space"]),
        mesh=mesh,
        in_specs=placed,
        out_specs=(P("space", None), P()),
        check_vma=False,
    )
```

```python
import functools

import jax
import jax.numpy as jnp
from jax import lax
from jax.experimental import pallas as pl
from jax.experimental.pallas import tpu as pltpu
from jax.sharding import PartitionSpec as P

LANES = 128
SUBLANES = 8
CHIPS_X = 4
CORES = 2
Z_LO = 2
MESH = pl.DeviceIdType.MESH
F32 = jnp.float32


def kernel(
    dims,
    p_hbm,
    m_hbm,
    c_hbm,
    w_hbm,
    lp_hbm,
    d_hbm,
    out,
    cur,
    pv,
    mv,
    cv,
    wv,
    lpv,
    dv,
    pm,
    fx,
    adj,
    txa,
    ty,
    sbx,
    sby,
    sbb,
    factor,
    sce,
    rce,
    inner,
    inner_in,
    inner_sum,
    rsb,
    agb,
    edges,
    edges_in,
    edge_z,
    ghost_z,
    final,
    sz,
    sxy,
    local_sem,
    send_sem,
    recv_sem,
):
    tms, spaces, steps, layers, rows, width = dims
    tiles = width // LANES
    zhs = tms // CORES
    ys = spaces // (CHIPS_X * Z_LO)
    zs = zhs * Z_LO
    last = rows
    row_tiles = tiles // SUBLANES
    row_blocks = rows // SUBLANES
    layer_rows = row_blocks * tiles * SUBLANES
    state_rows = layers * layer_rows

    tm = lax.axis_index("tm")
    sp = lax.axis_index("space")
    zh, core = tm // CORES, tm % CORES
    zl = sp % Z_LO
    x = (sp // Z_LO) % CHIPS_X
    y = sp // (Z_LO * CHIPS_X)
    z = zh * Z_LO + zl
    left = (sp + spaces - 1) % spaces
    right = (sp + 1) % spaces
    other = (tm + 1) - 2 * core

    loads = {}

    def load(name, src, dst, index):
        loads[name] = pltpu.make_async_copy(src, dst, local_sem.at[index])
        loads[name].start()

    for s in range(steps):
        part = pl.ds(s * state_rows, state_rows)
        load(("p", s), p_hbm.at[part, :], pv.at[part, :], 2 * s)
        load(("m", s), m_hbm.at[part, :], mv.at[part, :], 2 * s + 1)
    load("lp", lp_hbm, lpv, 2 * steps)
    load("d", d_hbm, dv, 2 * steps + 1)

    line = zs * CORES
    my_line = z * CORES + core
    plane = ys * CHIPS_X
    my_plane = y * CHIPS_X + x

    def apart(k, n):
        return min(k, n - k)

    line_offsets = sorted(
        ((dz, dc) for dz in range(zs) for dc in range(CORES) if (dz, dc) != (0, 0)),
        key=lambda o: -apart(o[0], zs),
    )
    plane_offsets = sorted(
        ((dy, dx) for dy in range(ys) for dx in range(CHIPS_X) if (dy, dx) != (0, 0)),
        key=lambda o: -apart(o[0], ys) - apart(o[1], CHIPS_X),
    )
    z_offsets = sorted(range(1, zhs), key=lambda k: -apart(k, zhs))

    def line_slot(dz, dc):
        return ((z + dz + zs) % zs) * CORES + (core + dc + CORES) % CORES

    def line_peer(dz, dc):
        to = (z + dz) % zs
        return ((to // Z_LO) * CORES + (core + dc) % CORES, sp - zl + to % Z_LO)

    def plane_slot(dy, dx):
        return ((y + dy + ys) % ys) * CHIPS_X + (x + dx + CHIPS_X) % CHIPS_X

    def plane_peer(dy, dx):
        return (tm, plane_slot(dy, dx) * Z_LO + zl)

    def z_peer(k):
        return (((zh + k) % zhs) * CORES + core, sp)

    greet = [(t, side) for side in (left, right) for t in range(tms)]
    greet += [((tm + k) % tms, sp) for k in range(1, tms)]
    greet += [plane_peer(*o) for o in plane_offsets]
    barrier = pltpu.get_barrier_semaphore()
    for peer in greet:
        pl.semaphore_signal(barrier, inc=1, device_id=peer, device_id_type=MESH)

    sem_count = [0]
    started = []

    def send(src, dst, device, send_index, recv_index):
        copy = pltpu.make_async_remote_copy(
            src_ref=src,
            dst_ref=dst,
            send_sem=send_sem.at[send_index],
            recv_sem=recv_sem.at[recv_index],
            device_id=device,
            device_id_type=MESH,
        )
        copy.start()
        started.append(copy)

    def arrived(dst, recv_index):
        pltpu.make_async_copy(dst, dst, recv_sem.at[recv_index]).wait()

    def take(n):
        first = sem_count[0]
        sem_count[0] += n
        return first

    def layers_of(ref, s, i, j):
        first = (
            s * state_rows + (i // SUBLANES) * (tiles * SUBLANES) + j * SUBLANES + i % SUBLANES
        )
        return ref[pl.ds(first, layers, stride=layer_rows), :]

    def cut(j):
        return slice(j * LANES, (j + 1) * LANES)

    def spread(s, i):
        for which, ref in enumerate((pv, mv)):
            for j in range(tiles):
                pm[i + 1, s, which, :, cut(j)] = layers_of(ref, s, i, j)

    def shares(s):
        size = tiles // 2 if s == 0 else tiles // 4
        return range(size), range(size, tiles - size), range(tiles - size, tiles)

    def lanes_of(part):
        return pl.ds(part[0] * LANES, len(part) * LANES)

    halo = take(2 * steps)
    middle = take(2 * steps)
    for s in range(steps):
        loads["p", s].wait()
        loads["m", s].wait()
        spread(s, 0)
        spread(s, rows - 1)
        if s == 0:
            load("c", c_hbm, cv, 2 * steps + 2)
            load("w", w_hbm, wv, 2 * steps + 3)
            pl.semaphore_wait(barrier, len(greet))
        near, both, far = shares(s)
        for first, parts in ((halo, (far, near)), (middle, (both, both))):
            for k, part in enumerate(parts):
                if len(part):
                    row, goal, side = ((1, last + 1, left), (last, 0, right))[k]
                    columns = lanes_of(part)
                    send(
                        pm.at[row, s, :, :, columns],
                        pm.at[goal, s, :, :, columns],
                        (tm, side),
                        first + 2 * s + k,
                        first + 2 * s + k,
                    )

    loads["lp"].wait()
    loads["d"].wait()
    conduct = jnp.exp(lpv[...])
    factor[...] = conduct * (0.25 / (layers * steps * tms))
    scaled = conduct * dv[...]
    sce[0] = scaled[0:1, :]
    sce[1] = scaled[rows - 1 : rows, :]
    edge = take(2)
    send(sce.at[0], rce.at[1], (tm, left), edge, edge)
    send(sce.at[1], rce.at[0], (tm, right), edge + 1, edge + 1)

    wide = (layers, width)
    for i in range(rows):
        row = scaled[i : i + 1, :]
        if i + 1 < rows:
            sbx[i + 1] = jnp.broadcast_to(0.25 * (row + scaled[i + 1 : i + 2, :]), wide)
        sby[i] = jnp.broadcast_to(0.25 * (row + pltpu.roll(row, width - 1, 1)), wide)
        sbb[i] = jnp.broadcast_to(0.25 * (row + pltpu.roll(row, 1, 1)), wide)

    def spread_inner(i, carry):
        for s in range(steps):
            spread(s, i)
        return carry

    lax.fori_loop(1, rows - 1, spread_inner, 0)

    lane = lax.broadcasted_iota(jnp.int32, (layers, LANES), 1)
    not_last = lane < LANES - 1
    not_first = lane > 0

    def face_part(f, s, part):
        for j in part:
            c = cut(j)
            fx[f, s, :, c] = (pm[f, s, 1, :, c] + pm[f + 1, s, 1, :, c]) * (
                pm[f + 1, s, 0, :, c] - pm[f, s, 0, :, c]
            )

    def face_x(f, carry):
        for s in range(steps):
            face_part(f, s, range(tiles))
        return carry

    def cell_row(r, curvature, states=range(steps), add=False):
        i = r - 1

        def ahead(here, later):
            return jnp.where(not_last, here, later)

        def turned(s, j):
            pressure, mobility = pm[r, s, 0, :, cut(j)], pm[r, s, 1, :, cut(j)]
            return (
                pressure,
                mobility,
                pltpu.roll(pressure, LANES - 1, 1),
                pltpu.roll(mobility, LANES - 1, 1),
            )

        here = {s: turned(s, 0) for s in states}
        spill = {s: 0.0 for s in states}
        for j in range(tiles):
            c = cut(j)
            piece = pl.ds(j * SUBLANES, SUBLANES)
            low, high = (ty[i, 0, piece, :], ty[i, 1, piece, :]) if add else (None, None)
            for s in states:
                pressure, mobility, p_back, m_back = here[s]
                if j + 1 < tiles:
                    here[s] = turned(s, j + 1)
                    p_next, m_next = here[s][2], here[s][3]
                else:
                    p_next, m_next = pressure, mobility
                face = (mobility + ahead(m_back, m_next)) * (ahead(p_back, p_next) - pressure)
                turned_face = pltpu.roll(face, 1, 1)
                before = jnp.where(not_first, turned_face, spill[s])
                spill[s] = turned_face
                change = (
                    fx[r, s, :, c] * sbx[r, :, c]
                    - fx[r - 1, s, :, c] * sbx[r - 1, :, c]
                    + (face * sby[i, :, c] - before * sbb[i, :, c])
                )
                square = layers_of(cv, s, i, j)
                square = square * square
                inverse = pl.reciprocal(square, approx=True)
                inverse = inverse * (2.0 - square * inverse)
                value = layers_of(wv, 0, i, j) * change * inverse
                adj[r, s, :, c] = value
                curvature = curvature + value * change
                low = face * value if low is None else low + face * value
                high = before * value if high is None else high + before * value
            ty[i, 0, piece, :] = low
            ty[i, 1, piece, :] = high
        return curvature

    def pack(dst, first, j, value):
        low = j % SUBLANES
        dst[first + j // SUBLANES, low : low + 1, :] = jnp.sum(value, axis=0, keepdims=True)

    def face_terms(f, low=True, high=True):
        for j in range(tiles):
            c = cut(j)
            total = None
            for s in range(steps):
                if low and high:
                    difference = adj[f, s, :, c] - adj[f + 1, s, :, c]
                elif low:
                    difference = adj[f, s, :, c]
                else:
                    difference = -adj[f + 1, s, :, c]
                value = fx[f, s, :, c] * difference
                total = value if total is None else total + value
            txa[f, pl.ds(j * SUBLANES, SUBLANES), :] = total

    def piece(j):
        return pl.ds(j * SUBLANES, SUBLANES)

    def pack_total(dst, first, i):
        high = [pltpu.roll(ty[i, 1, piece(j), :], LANES - 1, 1) for j in range(tiles)] + [0.0]
        terms = [
            ty[i, 0, piece(j), :] - jnp.where(not_last, high[j], high[j + 1])
            for j in range(tiles)
        ]
        low = [0.0] + [pltpu.roll(v, 1, 1) for v in terms]
        for j in range(tiles):
            value = txa[i, piece(j), :] + txa[i + 1, piece(j), :]
            value = value + (terms[j] + jnp.where(not_first, low[j + 1], low[j]))
            pack(dst, first, j, value)

    lax.fori_loop(1, rows, face_x, 0)
    loads["c"].wait()
    loads["w"].wait()
    curvature = lax.fori_loop(2, rows, cell_row, jnp.zeros((layers, LANES), F32))

    product = take(2 * steps)
    products = {}

    def send_products(s):
        near, _, far = shares(s)
        for k, (f, goal, part, side, index) in enumerate(
            ((0, last, near, left, halo + 1), (last, 0, far, right, halo))
        ):
            columns = lanes_of(part)
            cells = 0 if f == 0 else last + 1
            arrived(pm.at[cells, s, :, :, columns], index + 2 * s)
            face_part(f, s, part)
            number = product + 2 * s + k
            send(fx.at[f, s, :, columns], fx.at[goal, s, :, columns], (tm, side), number, number)
            products[s, k] = started.pop()

    send_products(0)

    def inner_faces(f, carry):
        face_terms(f)
        return carry

    lax.fori_loop(2, rows - 1, inner_faces, 0)
    for s in range(1, steps):
        send_products(s)

    def inner_rows(i, carry):
        pack_total(inner, (i - 2) * row_tiles, i)
        return carry

    lax.fori_loop(2, rows - 2, inner_rows, 0)

    half_tiles = (rows // CORES - 2) * row_tiles
    chunk = half_tiles // zhs
    inner_pair = take(1)
    send(
        inner.at[pl.ds((1 - core) * half_tiles, half_tiles)],
        inner_in,
        (other, sp),
        inner_pair,
        inner_pair,
    )

    arrived(inner_in, inner_pair)
    inner_sum[...] = inner[pl.ds(core * half_tiles, half_tiles)] + inner_in[...]
    scatter = take(zhs)
    for k in z_offsets:
        to = (zh + k) % zhs
        send(
            inner_sum.at[pl.ds(to * chunk, chunk)],
            rsb.at[k],
            z_peer(k),
            scatter + k,
            scatter + k,
        )

    arrived(rce.at[0], edge + 1)
    arrived(rce.at[1], edge)
    sbx[0] = jnp.broadcast_to(0.25 * (rce[0] + scaled[0:1, :]), wide)
    sbx[last] = jnp.broadcast_to(0.25 * (rce[1] + scaled[rows - 1 : rows, :]), wide)

    def no_face(states):
        @pl.when(sp == 0)
        def _():
            for s in states:
                fx[0, s] = jnp.zeros(wide, F32)

        @pl.when(sp == spaces - 1)
        def _():
            for s in states:
                fx[last, s] = jnp.zeros(wide, F32)

    def edge_rows(states, add, curvature):
        return lax.fori_loop(
            0, 2, lambda k, carry: cell_row(1 + k * (rows - 1), carry, states, add), curvature
        )

    for s in range(steps):
        near, both, far = shares(s)
        if len(both):
            for f, cells, k in ((last, last + 1, 0), (0, 0, 1)):
                arrived(pm.at[cells, s, :, :, lanes_of(both)], middle + 2 * s + k)
                face_part(f, s, both)
        for k, (f, part) in enumerate(((last, near), (0, far))):
            arrived(fx.at[f, s, :, lanes_of(part)], product + 2 * s + k)
            products[s, k].wait_send()
        no_face((s,))
        curvature = edge_rows((s,), s > 0, curvature)

    sz[my_line] = jnp.sum(curvature, axis=0, keepdims=True)
    over_line = take(line)
    for k, o in enumerate(line_offsets):
        send(sz.at[my_line], sz.at[my_line], line_peer(*o), over_line + k, over_line + k)

    face_terms(0, low=False)
    face_terms(last, high=False)
    face_terms(1)
    face_terms(rows - 1)
    for c, (edge_row, inner_row, face) in enumerate(((0, 1, 0), (rows - 1, rows - 2, last))):
        pack_total(edges.at[c], 0, edge_row)
        pack_total(edges.at[c], row_tiles, inner_row)
        for j in range(tiles):
            pack(edges.at[c], 2 * row_tiles, j, txa[face, piece(j), :])
    edge_pair = take(1)
    send(edges.at[1 - core], edges_in, (other, sp), edge_pair, edge_pair)

    reduced = inner_sum[pl.ds(zh * chunk, chunk)]
    for k in range(1, zhs):
        arrived(rsb.at[k], scatter + k)
        reduced = reduced + rsb[k]
    agb[core, pl.ds(zh * chunk, chunk)] = reduced
    mine = agb.at[core, pl.ds(zh * chunk, chunk)]
    gather = take(zhs)
    forward = take(zhs)
    for k in z_offsets:
        send(mine, mine, z_peer(k), gather + k, gather + k)
    send(mine, mine, (other, sp), forward, forward)

    two = 2 * row_tiles
    arrived(edges_in, edge_pair)
    summed = edges[core] + edges_in[...]
    edge_z[zh] = summed
    over_z = take(zhs)
    ghost = take(zhs)
    for k in z_offsets:
        send(
            edge_z.at[zh, pl.ds(0, two)],
            edge_z.at[zh, pl.ds(0, two)],
            z_peer(k),
            over_z + k,
            over_z + k,
        )
    side = left + core * (right - left)
    for k in z_offsets + [0]:
        send(
            edge_z.at[zh, pl.ds(two, row_tiles)],
            ghost_z.at[zh],
            (((zh + k) % zhs) * CORES + 1 - core, side),
            ghost + k,
            ghost + k,
        )

    for k, (dz, dc) in enumerate(line_offsets):
        arrived(sz.at[line_slot(-dz, -dc)], over_line + k)
    sxy[my_plane] = jnp.sum(sz[...], axis=0)
    over_plane = take(plane)
    for k, o in enumerate(plane_offsets):
        send(sxy.at[my_plane], sxy.at[my_plane], plane_peer(*o), over_plane + k, over_plane + k)

    def unpack(src, first, i):
        for j in range(tiles):
            low = j % SUBLANES
            value = src[first + j // SUBLANES, low : low + 1, :]
            out[i : i + 1, cut(j)] = value * factor[i : i + 1, cut(j)]

    for k in range(1, zhs):
        whose = agb.at[core, pl.ds(((zh + zhs - k) % zhs) * chunk, chunk)]
        arrived(whose, gather + k)
        send(whose, whose, (other, sp), forward + k, forward + k)

    for k in range(1, zhs):
        arrived(edge_z.at[(zh + zhs - k) % zhs, pl.ds(0, two)], over_z + k)
    for k in range(zhs):
        arrived(ghost_z.at[(zh + zhs - k) % zhs], ghost + k)
    total = edge_z[0, 0:two]
    beyond = ghost_z[0]
    for k in range(1, zhs):
        total = total + edge_z[k, 0:two]
        beyond = beyond + ghost_z[k]
    final[core, pl.ds(0, row_tiles)] = total[:row_tiles] + beyond
    final[core, pl.ds(row_tiles, row_tiles)] = total[row_tiles:]
    final_pair = take(1)
    send(final.at[core], final.at[core], (other, sp), final_pair, final_pair)

    for k in range(zhs):
        whose = agb.at[1 - core, pl.ds(((zh + zhs - k) % zhs) * chunk, chunk)]
        arrived(whose, forward + k)
    for i in range(2, rows - 2):
        first = (i - 2) * row_tiles
        unpack(agb.at[first // half_tiles], first % half_tiles, i)
    arrived(final.at[1 - core], final_pair)
    for c, (edge_row, inner_row) in enumerate(((0, 1), (rows - 1, rows - 2))):
        unpack(final.at[c], 0, edge_row)
        unpack(final.at[c], row_tiles, inner_row)

    for k, (dy, dx) in enumerate(plane_offsets):
        arrived(sxy.at[plane_slot(-dy, -dx)], over_plane + k)
    whole = jnp.sum(sxy[...], axis=0)
    scale = 1.0 / (layers * steps * tms * rows * spaces * width)
    cur[...] = jnp.broadcast_to(jnp.sum(whole, axis=1, keepdims=True) * scale, cur.shape)

    for copy in started:
        copy.wait_send()


def shards(tms, spaces, pressure, mobility, capacity, misfit_weight, log_permeability, direction):
    _, steps, layers, rows, width = pressure.shape
    dims = (tms, spaces, steps, layers, rows, width)
    tiles = width // LANES
    zhs = tms // CORES
    ys = spaces // (CHIPS_X * Z_LO)
    line = zhs * Z_LO * CORES
    plane = ys * CHIPS_X
    flat = layers * rows * tiles
    row_tiles = tiles // SUBLANES
    half_tiles = (rows // CORES - 2) * row_tiles
    chunk = half_tiles // zhs
    copies = 6 * steps + 2 + 3 + 5 * zhs + line + plane
    vmem = pltpu.VMEM

    def in_tiles(array):
        count = array.size // (SUBLANES * width)
        cut = array.reshape(count, SUBLANES, tiles, LANES).transpose(0, 2, 1, 3)
        return cut.reshape(count * tiles * SUBLANES, LANES)

    def block(*shape):
        return vmem((*shape, SUBLANES, LANES), F32)

    product, curvature = pl.pallas_call(
        functools.partial(kernel, dims),
        out_shape=(
            jax.ShapeDtypeStruct((rows, width), F32),
            jax.ShapeDtypeStruct((1, LANES), F32),
        ),
        in_specs=[pl.BlockSpec(memory_space=pl.ANY)] * 6,
        out_specs=(
            pl.BlockSpec(memory_space=pltpu.VMEM),
            pl.BlockSpec(memory_space=pltpu.VMEM),
        ),
        scratch_shapes=[
            vmem((steps * flat, LANES), F32),
            vmem((steps * flat, LANES), F32),
            vmem((steps * flat, LANES), F32),
            vmem((flat, LANES), F32),
            vmem((rows, width), F32),
            vmem((rows, width), F32),
            vmem((rows + 2, steps, 2, layers, width), F32),
            vmem((rows + 1, steps, layers, width), F32),
            vmem((rows + 2, steps, layers, width), F32),
            vmem((rows + 1, tiles * layers, LANES), F32),
            vmem((rows, 2, tiles * layers, LANES), F32),
            vmem((rows + 1, layers, width), F32),
            vmem((rows, layers, width), F32),
            vmem((rows, layers, width), F32),
            vmem((rows, width), F32),
            vmem((2, 1, width), F32),
            vmem((2, 1, width), F32),
            block(CORES * half_tiles),
            block(half_tiles),
            block(half_tiles),
            block(zhs, chunk),
            block(CORES, half_tiles),
            block(CORES, 3 * row_tiles),
            block(3 * row_tiles),
            block(zhs, 3 * row_tiles),
            block(zhs, row_tiles),
            block(CORES, 2 * row_tiles),
            vmem((line, 1, LANES), F32),
            vmem((plane, 1, LANES), F32),
            pltpu.SemaphoreType.DMA((2 * steps + 4,)),
            pltpu.SemaphoreType.DMA((copies,)),
            pltpu.SemaphoreType.DMA((copies,)),
        ],
        compiler_params=pltpu.CompilerParams(
            collective_id=0, has_side_effects=True, vmem_limit_bytes=55040 << 10
        ),
        cost_estimate=pl.CostEstimate(
            flops=50 * steps * flat * LANES,
            bytes_accessed=14 * steps * flat * LANES,
            transcendentals=rows * width,
        ),
    )(
        in_tiles(pressure),
        in_tiles(mobility),
        in_tiles(capacity),
        in_tiles(misfit_weight),
        log_permeability,
        direction,
    )
    return product, curvature[0, 0]


def solution(mesh):
    placed = (
        P("tm", None, None, "space", None),
        P("tm", None, None, "space", None),
        P("tm", None, None, "space", None),
        P("tm", None, "space", None),
        P("space", None),
        P("space", None),
    )
    return jax.shard_map(
        functools.partial(shards, mesh.shape["tm"], mesh.shape["space"]),
        mesh=mesh,
        in_specs=placed,
        out_specs=(P("space", None), P()),
        check_vma=False,
    )
```

```python
import functools

import jax
import jax.numpy as jnp
from jax import lax
from jax.experimental import pallas as pl
from jax.experimental.pallas import tpu as pltpu
from jax.sharding import PartitionSpec as P

LANES = 128
SUBLANES = 8
CHIPS_X = 4
CORES = 2
Z_LO = 2
MESH = pl.DeviceIdType.MESH
F32 = jnp.float32


def kernel(
    dims,
    p_hbm,
    m_hbm,
    c_hbm,
    w_hbm,
    lp_hbm,
    d_hbm,
    out,
    cur,
    pv,
    mv,
    cv,
    wv,
    lpv,
    dv,
    pm,
    fx,
    adj,
    txa,
    ty,
    sbx,
    sby,
    sbb,
    factor,
    sce,
    rce,
    inner,
    inner_in,
    inner_sum,
    rsb,
    agb,
    edges,
    edges_in,
    edge_z,
    ghost_z,
    final,
    sz,
    sxy,
    local_sem,
    send_sem,
    recv_sem,
):
    tms, spaces, steps, layers, rows, width = dims
    tiles = width // LANES
    zhs = tms // CORES
    ys = spaces // (CHIPS_X * Z_LO)
    zs = zhs * Z_LO
    last = rows
    row_tiles = tiles // SUBLANES
    row_blocks = rows // SUBLANES
    layer_rows = row_blocks * tiles * SUBLANES
    state_rows = layers * layer_rows

    tm = lax.axis_index("tm")
    sp = lax.axis_index("space")
    zh, core = tm // CORES, tm % CORES
    zl = sp % Z_LO
    x = (sp // Z_LO) % CHIPS_X
    y = sp // (Z_LO * CHIPS_X)
    z = zh * Z_LO + zl
    left = (sp + spaces - 1) % spaces
    right = (sp + 1) % spaces
    other = (tm + 1) - 2 * core

    loads = {}

    def load(name, src, dst, index):
        loads[name] = pltpu.make_async_copy(src, dst, local_sem.at[index])
        loads[name].start()

    line = zs * CORES
    my_line = z * CORES + core
    plane = ys * CHIPS_X
    my_plane = y * CHIPS_X + x

    def apart(k, n):
        return min(k, n - k)

    line_offsets = sorted(
        ((dz, dc) for dz in range(zs) for dc in range(CORES) if (dz, dc) != (0, 0)),
        key=lambda o: -apart(o[0], zs),
    )
    plane_offsets = sorted(
        ((dy, dx) for dy in range(ys) for dx in range(CHIPS_X) if (dy, dx) != (0, 0)),
        key=lambda o: -apart(o[0], ys) - apart(o[1], CHIPS_X),
    )
    z_offsets = sorted(range(1, zhs), key=lambda k: -apart(k, zhs))

    def line_slot(dz, dc):
        return ((z + dz + zs) % zs) * CORES + (core + dc + CORES) % CORES

    def line_peer(dz, dc):
        to = (z + dz) % zs
        return ((to // Z_LO) * CORES + (core + dc) % CORES, sp - zl + to % Z_LO)

    def plane_slot(dy, dx):
        return ((y + dy + ys) % ys) * CHIPS_X + (x + dx + CHIPS_X) % CHIPS_X

    def plane_peer(dy, dx):
        return (tm, plane_slot(dy, dx) * Z_LO + zl)

    def z_peer(k):
        return (((zh + k) % zhs) * CORES + core, sp)

    across = left + zl * (right - left)
    greet = [(apart(dz, zs) + 0.5 * dc, line_peer(dz, dc)) for dz, dc in line_offsets]
    greet += [
        (apart(dy, ys) + apart(dx, CHIPS_X), plane_peer(dy, dx)) for dy, dx in plane_offsets
    ]
    greet += [
        (
            1.5 + Z_LO * apart(k, zhs),
            (((zh + k) % zhs) * CORES + (core + c) % CORES, across),
        )
        for k in range(zhs)
        for c in range(CORES)
    ]
    greet.sort(key=lambda entry: -entry[0])
    barrier = pltpu.get_barrier_semaphore()

    def say(peers):
        for _, peer in peers:
            pl.semaphore_signal(barrier, inc=1, device_id=peer, device_id_type=MESH)

    distant = sum(hops > 2.5 for hops, _ in greet)
    say(greet[:distant])
    for s in range(steps):
        part = pl.ds(s * state_rows, state_rows)
        load(("p", s), p_hbm.at[part, :], pv.at[part, :], 2 * s)
        load(("m", s), m_hbm.at[part, :], mv.at[part, :], 2 * s + 1)
    load("lp", lp_hbm, lpv, 2 * steps)
    load("d", d_hbm, dv, 2 * steps + 1)
    say(greet[distant:])

    sem_count = [0]
    started = []

    def send(src, dst, device, send_index, recv_index):
        copy = pltpu.make_async_remote_copy(
            src_ref=src,
            dst_ref=dst,
            send_sem=send_sem.at[send_index],
            recv_sem=recv_sem.at[recv_index],
            device_id=device,
            device_id_type=MESH,
        )
        copy.start()
        started.append(copy)

    def arrived(dst, recv_index):
        pltpu.make_async_copy(dst, dst, recv_sem.at[recv_index]).wait()

    def take(n):
        first = sem_count[0]
        sem_count[0] += n
        return first

    def layers_of(ref, s, i, j):
        first = (
            s * state_rows + (i // SUBLANES) * (tiles * SUBLANES) + j * SUBLANES + i % SUBLANES
        )
        return ref[pl.ds(first, layers, stride=layer_rows), :]

    def cut(j):
        return slice(j * LANES, (j + 1) * LANES)

    def spread(s, i):
        for which, ref in enumerate((pv, mv)):
            for j in range(tiles):
                pm[i + 1, s, which, :, cut(j)] = layers_of(ref, s, i, j)

    def shares(s):
        size = tiles // 2 if s == 0 else tiles // 4
        return range(size), range(size, tiles - size), range(tiles - size, tiles)

    def lanes_of(part):
        return pl.ds(part[0] * LANES, len(part) * LANES)

    halo = take(2 * steps)
    middle = take(2 * steps)
    for s in range(steps):
        loads["p", s].wait()
        loads["m", s].wait()
        spread(s, 0)
        spread(s, rows - 1)
        if s == 0:
            load("c", c_hbm, cv, 2 * steps + 2)
            load("w", w_hbm, wv, 2 * steps + 3)
            pl.semaphore_wait(barrier, len(greet))
        near, both, far = shares(s)
        for first, parts in ((halo, (far, near)), (middle, (both, both))):
            for k, part in enumerate(parts):
                if len(part):
                    row, goal, side = ((1, last + 1, left), (last, 0, right))[k]
                    columns = lanes_of(part)
                    send(
                        pm.at[row, s, :, :, columns],
                        pm.at[goal, s, :, :, columns],
                        (tm, side),
                        first + 2 * s + k,
                        first + 2 * s + k,
                    )

    loads["lp"].wait()
    loads["d"].wait()
    conduct = jnp.exp(lpv[...])
    factor[...] = conduct * (0.25 / (layers * steps * tms))
    scaled = conduct * dv[...]
    sce[0] = scaled[0:1, :]
    sce[1] = scaled[rows - 1 : rows, :]
    edge = take(2)
    send(sce.at[0], rce.at[1], (tm, left), edge, edge)
    send(sce.at[1], rce.at[0], (tm, right), edge + 1, edge + 1)

    wide = (layers, width)
    for i in range(rows):
        row = scaled[i : i + 1, :]
        if i + 1 < rows:
            sbx[i + 1] = jnp.broadcast_to(0.25 * (row + scaled[i + 1 : i + 2, :]), wide)
        sby[i] = jnp.broadcast_to(0.25 * (row + pltpu.roll(row, width - 1, 1)), wide)
        sbb[i] = jnp.broadcast_to(0.25 * (row + pltpu.roll(row, 1, 1)), wide)

    def spread_inner(i, carry):
        for s in range(steps):
            spread(s, i)
        return carry

    lax.fori_loop(1, rows - 1, spread_inner, 0)

    lane = lax.broadcasted_iota(jnp.int32, (layers, LANES), 1)
    not_last = lane < LANES - 1
    not_first = lane > 0

    def face_part(f, s, part):
        for j in part:
            c = cut(j)
            fx[f, s, :, c] = (pm[f, s, 1, :, c] + pm[f + 1, s, 1, :, c]) * (
                pm[f + 1, s, 0, :, c] - pm[f, s, 0, :, c]
            )

    def face_x(f, carry):
        for s in range(steps):
            face_part(f, s, range(tiles))
        return carry

    def cell_row(r, curvature, states=range(steps), add=False):
        i = r - 1

        def ahead(here, later):
            return jnp.where(not_last, here, later)

        def turned(s, j):
            pressure, mobility = pm[r, s, 0, :, cut(j)], pm[r, s, 1, :, cut(j)]
            return (
                pressure,
                mobility,
                pltpu.roll(pressure, LANES - 1, 1),
                pltpu.roll(mobility, LANES - 1, 1),
            )

        here = {s: turned(s, 0) for s in states}
        spill = {s: 0.0 for s in states}
        for j in range(tiles):
            c = cut(j)
            piece = pl.ds(j * SUBLANES, SUBLANES)
            low, high = (ty[i, 0, piece, :], ty[i, 1, piece, :]) if add else (None, None)
            for s in states:
                pressure, mobility, p_back, m_back = here[s]
                if j + 1 < tiles:
                    here[s] = turned(s, j + 1)
                    p_next, m_next = here[s][2], here[s][3]
                else:
                    p_next, m_next = pressure, mobility
                face = (mobility + ahead(m_back, m_next)) * (ahead(p_back, p_next) - pressure)
                turned_face = pltpu.roll(face, 1, 1)
                before = jnp.where(not_first, turned_face, spill[s])
                spill[s] = turned_face
                change = (
                    fx[r, s, :, c] * sbx[r, :, c]
                    - fx[r - 1, s, :, c] * sbx[r - 1, :, c]
                    + (face * sby[i, :, c] - before * sbb[i, :, c])
                )
                square = layers_of(cv, s, i, j)
                square = square * square
                inverse = pl.reciprocal(square, approx=True)
                inverse = inverse * (2.0 - square * inverse)
                value = layers_of(wv, 0, i, j) * change * inverse
                adj[r, s, :, c] = value
                curvature = curvature + value * change
                low = face * value if low is None else low + face * value
                high = before * value if high is None else high + before * value
            ty[i, 0, piece, :] = low
            ty[i, 1, piece, :] = high
        return curvature

    def pack(dst, first, j, value):
        low = j % SUBLANES
        dst[first + j // SUBLANES, low : low + 1, :] = jnp.sum(value, axis=0, keepdims=True)

    def face_terms(f, low=True, high=True):
        for j in range(tiles):
            c = cut(j)
            total = None
            for s in range(steps):
                if low and high:
                    difference = adj[f, s, :, c] - adj[f + 1, s, :, c]
                elif low:
                    difference = adj[f, s, :, c]
                else:
                    difference = -adj[f + 1, s, :, c]
                value = fx[f, s, :, c] * difference
                total = value if total is None else total + value
            txa[f, pl.ds(j * SUBLANES, SUBLANES), :] = total

    def piece(j):
        return pl.ds(j * SUBLANES, SUBLANES)

    def pack_total(dst, first, i):
        high = [pltpu.roll(ty[i, 1, piece(j), :], LANES - 1, 1) for j in range(tiles)] + [0.0]
        terms = [
            ty[i, 0, piece(j), :] - jnp.where(not_last, high[j], high[j + 1])
            for j in range(tiles)
        ]
        low = [0.0] + [pltpu.roll(v, 1, 1) for v in terms]
        for j in range(tiles):
            value = txa[i, piece(j), :] + txa[i + 1, piece(j), :]
            value = value + (terms[j] + jnp.where(not_first, low[j + 1], low[j]))
            pack(dst, first, j, value)

    lax.fori_loop(1, rows, face_x, 0)
    loads["c"].wait()
    loads["w"].wait()
    curvature = lax.fori_loop(2, rows, cell_row, jnp.zeros((layers, LANES), F32))

    product = take(2 * steps)
    products = {}

    def send_products(s):
        near, _, far = shares(s)
        for k, (f, goal, part, side, index) in enumerate(
            ((0, last, near, left, halo + 1), (last, 0, far, right, halo))
        ):
            columns = lanes_of(part)
            cells = 0 if f == 0 else last + 1
            arrived(pm.at[cells, s, :, :, columns], index + 2 * s)
            face_part(f, s, part)
            number = product + 2 * s + k
            send(fx.at[f, s, :, columns], fx.at[goal, s, :, columns], (tm, side), number, number)
            products[s, k] = started.pop()

    send_products(0)

    def inner_faces(f, carry):
        face_terms(f)
        return carry

    lax.fori_loop(2, rows - 1, inner_faces, 0)
    for s in range(1, steps):
        send_products(s)

    def inner_rows(i, carry):
        pack_total(inner, (i - 2) * row_tiles, i)
        return carry

    lax.fori_loop(2, rows - 2, inner_rows, 0)

    half_tiles = (rows // CORES - 2) * row_tiles
    chunk = half_tiles // zhs
    inner_pair = take(1)
    send(
        inner.at[pl.ds((1 - core) * half_tiles, half_tiles)],
        inner_in,
        (other, sp),
        inner_pair,
        inner_pair,
    )

    arrived(inner_in, inner_pair)
    inner_sum[...] = inner[pl.ds(core * half_tiles, half_tiles)] + inner_in[...]
    scatter = take(zhs)
    for k in z_offsets:
        to = (zh + k) % zhs
        send(
            inner_sum.at[pl.ds(to * chunk, chunk)],
            rsb.at[k],
            z_peer(k),
            scatter + k,
            scatter + k,
        )

    arrived(rce.at[0], edge + 1)
    arrived(rce.at[1], edge)
    sbx[0] = jnp.broadcast_to(0.25 * (rce[0] + scaled[0:1, :]), wide)
    sbx[last] = jnp.broadcast_to(0.25 * (rce[1] + scaled[rows - 1 : rows, :]), wide)

    def no_face(states):
        @pl.when(sp == 0)
        def _():
            for s in states:
                fx[0, s] = jnp.zeros(wide, F32)

        @pl.when(sp == spaces - 1)
        def _():
            for s in states:
                fx[last, s] = jnp.zeros(wide, F32)

    def edge_rows(states, add, curvature):
        return lax.fori_loop(
            0, 2, lambda k, carry: cell_row(1 + k * (rows - 1), carry, states, add), curvature
        )

    for s in range(steps):
        near, both, far = shares(s)
        if len(both):
            for f, cells, k in ((last, last + 1, 0), (0, 0, 1)):
                arrived(pm.at[cells, s, :, :, lanes_of(both)], middle + 2 * s + k)
                face_part(f, s, both)
        for k, (f, part) in enumerate(((last, near), (0, far))):
            arrived(fx.at[f, s, :, lanes_of(part)], product + 2 * s + k)
            products[s, k].wait_send()
        no_face((s,))
        curvature = edge_rows((s,), s > 0, curvature)

    sz[my_line] = jnp.sum(curvature, axis=0, keepdims=True)
    over_line = take(line)
    for k, o in enumerate(line_offsets):
        send(sz.at[my_line], sz.at[my_line], line_peer(*o), over_line + k, over_line + k)

    face_terms(0, low=False)
    face_terms(last, high=False)
    face_terms(1)
    face_terms(rows - 1)
    for c, (edge_row, inner_row, face) in enumerate(((0, 1, 0), (rows - 1, rows - 2, last))):
        pack_total(edges.at[c], 0, edge_row)
        pack_total(edges.at[c], row_tiles, inner_row)
        for j in range(tiles):
            pack(edges.at[c], 2 * row_tiles, j, txa[face, piece(j), :])
    edge_pair = take(1)
    send(edges.at[1 - core], edges_in, (other, sp), edge_pair, edge_pair)

    reduced = inner_sum[pl.ds(zh * chunk, chunk)]
    for k in range(1, zhs):
        arrived(rsb.at[k], scatter + k)
        reduced = reduced + rsb[k]
    agb[core, pl.ds(zh * chunk, chunk)] = reduced
    mine = agb.at[core, pl.ds(zh * chunk, chunk)]
    gather = take(zhs)
    forward = take(zhs)
    for k in z_offsets:
        send(mine, mine, z_peer(k), gather + k, gather + k)
    send(mine, mine, (other, sp), forward, forward)

    two = 2 * row_tiles
    arrived(edges_in, edge_pair)
    summed = edges[core] + edges_in[...]
    edge_z[zh] = summed
    over_z = take(zhs)
    ghost = take(zhs)
    for k in z_offsets:
        send(
            edge_z.at[zh, pl.ds(0, two)],
            edge_z.at[zh, pl.ds(0, two)],
            z_peer(k),
            over_z + k,
            over_z + k,
        )
    side = left + core * (right - left)
    for k in z_offsets + [0]:
        send(
            edge_z.at[zh, pl.ds(two, row_tiles)],
            ghost_z.at[zh],
            (((zh + k) % zhs) * CORES + 1 - core, side),
            ghost + k,
            ghost + k,
        )

    for k, (dz, dc) in enumerate(line_offsets):
        arrived(sz.at[line_slot(-dz, -dc)], over_line + k)
    sxy[my_plane] = jnp.sum(sz[...], axis=0)
    over_plane = take(plane)
    for k, o in enumerate(plane_offsets):
        send(sxy.at[my_plane], sxy.at[my_plane], plane_peer(*o), over_plane + k, over_plane + k)

    def unpack(src, first, i):
        for j in range(tiles):
            low = j % SUBLANES
            value = src[first + j // SUBLANES, low : low + 1, :]
            out[i : i + 1, cut(j)] = value * factor[i : i + 1, cut(j)]

    for k in range(1, zhs):
        whose = agb.at[core, pl.ds(((zh + zhs - k) % zhs) * chunk, chunk)]
        arrived(whose, gather + k)
        send(whose, whose, (other, sp), forward + k, forward + k)

    for k in range(1, zhs):
        arrived(edge_z.at[(zh + zhs - k) % zhs, pl.ds(0, two)], over_z + k)
    for k in range(zhs):
        arrived(ghost_z.at[(zh + zhs - k) % zhs], ghost + k)
    total = edge_z[0, 0:two]
    beyond = ghost_z[0]
    for k in range(1, zhs):
        total = total + edge_z[k, 0:two]
        beyond = beyond + ghost_z[k]
    final[core, pl.ds(0, row_tiles)] = total[:row_tiles] + beyond
    final[core, pl.ds(row_tiles, row_tiles)] = total[row_tiles:]
    final_pair = take(1)
    send(final.at[core], final.at[core], (other, sp), final_pair, final_pair)

    for k in range(zhs):
        whose = agb.at[1 - core, pl.ds(((zh + zhs - k) % zhs) * chunk, chunk)]
        arrived(whose, forward + k)
    for i in range(2, rows - 2):
        first = (i - 2) * row_tiles
        unpack(agb.at[first // half_tiles], first % half_tiles, i)
    arrived(final.at[1 - core], final_pair)
    for c, (edge_row, inner_row) in enumerate(((0, 1), (rows - 1, rows - 2))):
        unpack(final.at[c], 0, edge_row)
        unpack(final.at[c], row_tiles, inner_row)

    for k, (dy, dx) in enumerate(plane_offsets):
        arrived(sxy.at[plane_slot(-dy, -dx)], over_plane + k)
    whole = jnp.sum(sxy[...], axis=0)
    scale = 1.0 / (layers * steps * tms * rows * spaces * width)
    cur[...] = jnp.broadcast_to(jnp.sum(whole, axis=1, keepdims=True) * scale, cur.shape)

    for copy in started:
        copy.wait_send()


def shards(tms, spaces, pressure, mobility, capacity, misfit_weight, log_permeability, direction):
    _, steps, layers, rows, width = pressure.shape
    dims = (tms, spaces, steps, layers, rows, width)
    tiles = width // LANES
    zhs = tms // CORES
    ys = spaces // (CHIPS_X * Z_LO)
    line = zhs * Z_LO * CORES
    plane = ys * CHIPS_X
    flat = layers * rows * tiles
    row_tiles = tiles // SUBLANES
    half_tiles = (rows // CORES - 2) * row_tiles
    chunk = half_tiles // zhs
    copies = 6 * steps + 2 + 3 + 5 * zhs + line + plane
    vmem = pltpu.VMEM

    def in_tiles(array):
        count = array.size // (SUBLANES * width)
        cut = array.reshape(count, SUBLANES, tiles, LANES).transpose(0, 2, 1, 3)
        return cut.reshape(count * tiles * SUBLANES, LANES)

    def block(*shape):
        return vmem((*shape, SUBLANES, LANES), F32)

    product, curvature = pl.pallas_call(
        functools.partial(kernel, dims),
        out_shape=(
            jax.ShapeDtypeStruct((rows, width), F32),
            jax.ShapeDtypeStruct((1, LANES), F32),
        ),
        in_specs=[pl.BlockSpec(memory_space=pl.ANY)] * 6,
        out_specs=(
            pl.BlockSpec(memory_space=pltpu.VMEM),
            pl.BlockSpec(memory_space=pltpu.VMEM),
        ),
        scratch_shapes=[
            vmem((steps * flat, LANES), F32),
            vmem((steps * flat, LANES), F32),
            vmem((steps * flat, LANES), F32),
            vmem((flat, LANES), F32),
            vmem((rows, width), F32),
            vmem((rows, width), F32),
            vmem((rows + 2, steps, 2, layers, width), F32),
            vmem((rows + 1, steps, layers, width), F32),
            vmem((rows + 2, steps, layers, width), F32),
            vmem((rows + 1, tiles * layers, LANES), F32),
            vmem((rows, 2, tiles * layers, LANES), F32),
            vmem((rows + 1, layers, width), F32),
            vmem((rows, layers, width), F32),
            vmem((rows, layers, width), F32),
            vmem((rows, width), F32),
            vmem((2, 1, width), F32),
            vmem((2, 1, width), F32),
            block(CORES * half_tiles),
            block(half_tiles),
            block(half_tiles),
            block(zhs, chunk),
            block(CORES, half_tiles),
            block(CORES, 3 * row_tiles),
            block(3 * row_tiles),
            block(zhs, 3 * row_tiles),
            block(zhs, row_tiles),
            block(CORES, 2 * row_tiles),
            vmem((line, 1, LANES), F32),
            vmem((plane, 1, LANES), F32),
            pltpu.SemaphoreType.DMA((2 * steps + 4,)),
            pltpu.SemaphoreType.DMA((copies,)),
            pltpu.SemaphoreType.DMA((copies,)),
        ],
        compiler_params=pltpu.CompilerParams(
            collective_id=0, has_side_effects=True, vmem_limit_bytes=55040 << 10
        ),
        cost_estimate=pl.CostEstimate(
            flops=50 * steps * flat * LANES,
            bytes_accessed=14 * steps * flat * LANES,
            transcendentals=rows * width,
        ),
    )(
        in_tiles(pressure),
        in_tiles(mobility),
        in_tiles(capacity),
        in_tiles(misfit_weight),
        log_permeability,
        direction,
    )
    return product, curvature[0, 0]


def solution(mesh):
    placed = (
        P("tm", None, None, "space", None),
        P("tm", None, None, "space", None),
        P("tm", None, None, "space", None),
        P("tm", None, "space", None),
        P("space", None),
        P("space", None),
    )
    return jax.shard_map(
        functools.partial(shards, mesh.shape["tm"], mesh.shape["space"]),
        mesh=mesh,
        in_specs=placed,
        out_specs=(P("space", None), P()),
        check_vma=False,
    )
```

```python
import functools

import jax
import jax.numpy as jnp
from jax import lax
from jax.experimental import pallas as pl
from jax.experimental.pallas import tpu as pltpu
from jax.sharding import PartitionSpec as P

LANES = 128
SUBLANES = 8
CHIPS_X = 4
CORES = 2
Z_LO = 2
MESH = pl.DeviceIdType.MESH
F32 = jnp.float32


def kernel(
    dims,
    p_hbm,
    m_hbm,
    c_hbm,
    w_hbm,
    lp_hbm,
    d_hbm,
    out,
    cur,
    pv,
    mv,
    cv,
    wv,
    lpv,
    dv,
    pm,
    fx,
    adj,
    txa,
    ty,
    sbx,
    sby,
    sbb,
    factor,
    sce,
    rce,
    inner,
    inner_in,
    inner_sum,
    rsb,
    agb,
    edges,
    edges_in,
    edge_z,
    ghost_z,
    final,
    sz,
    sxy,
    local_sem,
    send_sem,
    recv_sem,
):
    tms, spaces, steps, layers, rows, width = dims
    tiles = width // LANES
    zhs = tms // CORES
    ys = spaces // (CHIPS_X * Z_LO)
    zs = zhs * Z_LO
    last = rows
    row_tiles = tiles // SUBLANES
    row_blocks = rows // SUBLANES
    layer_rows = row_blocks * tiles * SUBLANES
    state_rows = layers * layer_rows

    tm = lax.axis_index("tm")
    sp = lax.axis_index("space")
    zh, core = tm // CORES, tm % CORES
    zl = sp % Z_LO
    x = (sp // Z_LO) % CHIPS_X
    y = sp // (Z_LO * CHIPS_X)
    z = zh * Z_LO + zl
    left = (sp + spaces - 1) % spaces
    right = (sp + 1) % spaces
    other = (tm + 1) - 2 * core

    loads = {}

    def load(name, src, dst, index):
        loads[name] = pltpu.make_async_copy(src, dst, local_sem.at[index])
        loads[name].start()

    line = zs * CORES
    my_line = z * CORES + core
    plane = ys * CHIPS_X
    my_plane = y * CHIPS_X + x

    def apart(k, n):
        return min(k, n - k)

    line_offsets = sorted(
        ((dz, dc) for dz in range(zs) for dc in range(CORES) if (dz, dc) != (0, 0)),
        key=lambda o: -apart(o[0], zs),
    )
    plane_offsets = sorted(
        ((dy, dx) for dy in range(ys) for dx in range(CHIPS_X) if (dy, dx) != (0, 0)),
        key=lambda o: -apart(o[0], ys) - apart(o[1], CHIPS_X),
    )
    z_offsets = sorted(range(1, zhs), key=lambda k: -apart(k, zhs))

    def line_slot(dz, dc):
        return ((z + dz + zs) % zs) * CORES + (core + dc + CORES) % CORES

    def line_peer(dz, dc):
        to = (z + dz) % zs
        return ((to // Z_LO) * CORES + (core + dc) % CORES, sp - zl + to % Z_LO)

    def plane_slot(dy, dx):
        return ((y + dy + ys) % ys) * CHIPS_X + (x + dx + CHIPS_X) % CHIPS_X

    def plane_peer(dy, dx):
        return (tm, plane_slot(dy, dx) * Z_LO + zl)

    def z_peer(k):
        return (((zh + k) % zhs) * CORES + core, sp)

    across = left + zl * (right - left)
    greet = [(apart(dz, zs) + 0.5 * dc, line_peer(dz, dc)) for dz, dc in line_offsets]
    greet += [
        (apart(dy, ys) + apart(dx, CHIPS_X), plane_peer(dy, dx)) for dy, dx in plane_offsets
    ]
    greet += [
        (
            1.5 + Z_LO * apart(k, zhs),
            (((zh + k) % zhs) * CORES + (core + c) % CORES, across),
        )
        for k in range(zhs)
        for c in range(CORES)
    ]
    greet.sort(key=lambda entry: -entry[0])
    barrier = pltpu.get_barrier_semaphore()

    def say(peers):
        for _, peer in peers:
            pl.semaphore_signal(barrier, inc=1, device_id=peer, device_id_type=MESH)

    distant = sum(hops > 2.5 for hops, _ in greet)
    say(greet[:distant])
    for s in range(steps):
        part = pl.ds(s * state_rows, state_rows)
        load(("p", s), p_hbm.at[part, :], pv.at[part, :], 2 * s)
        load(("m", s), m_hbm.at[part, :], mv.at[part, :], 2 * s + 1)
    load("lp", lp_hbm, lpv, 2 * steps)
    load("d", d_hbm, dv, 2 * steps + 1)
    say(greet[distant:])

    sem_count = [0]
    started = []

    def send(src, dst, device, send_index, recv_index):
        copy = pltpu.make_async_remote_copy(
            src_ref=src,
            dst_ref=dst,
            send_sem=send_sem.at[send_index],
            recv_sem=recv_sem.at[recv_index],
            device_id=device,
            device_id_type=MESH,
        )
        copy.start()
        started.append(copy)

    def arrived(dst, recv_index):
        pltpu.make_async_copy(dst, dst, recv_sem.at[recv_index]).wait()

    def take(n):
        first = sem_count[0]
        sem_count[0] += n
        return first

    def layers_of(ref, s, i, j):
        first = (
            s * state_rows + (i // SUBLANES) * (tiles * SUBLANES) + j * SUBLANES + i % SUBLANES
        )
        return ref[pl.ds(first, layers, stride=layer_rows), :]

    def cut(j):
        return slice(j * LANES, (j + 1) * LANES)

    def spread(s, i):
        for which, ref in enumerate((pv, mv)):
            for j in range(tiles):
                pm[i + 1, s, which, :, cut(j)] = layers_of(ref, s, i, j)

    def shares(s):
        size = tiles // 2 if s == 0 else tiles // 4
        return range(size), range(size, tiles - size), range(tiles - size, tiles)

    def lanes_of(part):
        return pl.ds(part[0] * LANES, len(part) * LANES)

    halo = take(2 * steps)
    middle = take(2 * steps)
    for s in range(steps):
        loads["p", s].wait()
        loads["m", s].wait()
        spread(s, 0)
        spread(s, rows - 1)
        if s == 0:
            load("c", c_hbm, cv, 2 * steps + 2)
            load("w", w_hbm, wv, 2 * steps + 3)
            pl.semaphore_wait(barrier, len(greet))
        near, both, far = shares(s)
        for first, parts in ((halo, (far, near)), (middle, (both, both))):
            for k, part in enumerate(parts):
                if len(part):
                    row, goal, side = ((1, last + 1, left), (last, 0, right))[k]
                    columns = lanes_of(part)
                    send(
                        pm.at[row, s, :, :, columns],
                        pm.at[goal, s, :, :, columns],
                        (tm, side),
                        first + 2 * s + k,
                        first + 2 * s + k,
                    )

    loads["lp"].wait()
    loads["d"].wait()
    conduct = jnp.exp(lpv[...])
    factor[...] = conduct * (0.25 / (layers * steps * tms))
    scaled = conduct * dv[...]
    sce[0] = scaled[0:1, :]
    sce[1] = scaled[rows - 1 : rows, :]
    edge = take(2)
    send(sce.at[0], rce.at[1], (tm, left), edge, edge)
    send(sce.at[1], rce.at[0], (tm, right), edge + 1, edge + 1)

    wide = (layers, width)
    for i in range(rows):
        row = scaled[i : i + 1, :]
        if i + 1 < rows:
            sbx[i + 1] = jnp.broadcast_to(0.25 * (row + scaled[i + 1 : i + 2, :]), wide)
        sby[i] = jnp.broadcast_to(0.25 * (row + pltpu.roll(row, width - 1, 1)), wide)
        sbb[i] = jnp.broadcast_to(0.25 * (row + pltpu.roll(row, 1, 1)), wide)

    def spread_inner(i, carry):
        for s in range(steps):
            spread(s, i)
        return carry

    lax.fori_loop(1, rows - 1, spread_inner, 0)

    lane = lax.broadcasted_iota(jnp.int32, (layers, LANES), 1)
    not_last = lane < LANES - 1
    not_first = lane > 0

    def face_part(f, s, part):
        for j in part:
            c = cut(j)
            fx[f, s, :, c] = (pm[f, s, 1, :, c] + pm[f + 1, s, 1, :, c]) * (
                pm[f + 1, s, 0, :, c] - pm[f, s, 0, :, c]
            )

    def face_x(f, carry):
        for s in range(steps):
            face_part(f, s, range(tiles))
        return carry

    def cell_row(r, curvature, states=range(steps), add=False):
        i = r - 1

        def ahead(here, later):
            return jnp.where(not_last, here, later)

        def turned(s, j):
            pressure, mobility = pm[r, s, 0, :, cut(j)], pm[r, s, 1, :, cut(j)]
            return (
                pressure,
                mobility,
                pltpu.roll(pressure, LANES - 1, 1),
                pltpu.roll(mobility, LANES - 1, 1),
            )

        here = {s: turned(s, 0) for s in states}
        spill = {s: 0.0 for s in states}
        for j in range(tiles):
            c = cut(j)
            piece = pl.ds(j * SUBLANES, SUBLANES)
            low, high = (ty[i, 0, piece, :], ty[i, 1, piece, :]) if add else (None, None)
            for s in states:
                pressure, mobility, p_back, m_back = here[s]
                if j + 1 < tiles:
                    here[s] = turned(s, j + 1)
                    p_next, m_next = here[s][2], here[s][3]
                else:
                    p_next, m_next = pressure, mobility
                face = (mobility + ahead(m_back, m_next)) * (ahead(p_back, p_next) - pressure)
                turned_face = pltpu.roll(face, 1, 1)
                before = jnp.where(not_first, turned_face, spill[s])
                spill[s] = turned_face
                change = (
                    fx[r, s, :, c] * sbx[r, :, c]
                    - fx[r - 1, s, :, c] * sbx[r - 1, :, c]
                    + (face * sby[i, :, c] - before * sbb[i, :, c])
                )
                square = layers_of(cv, s, i, j)
                square = square * square
                inverse = pl.reciprocal(square, approx=True)
                inverse = inverse * (2.0 - square * inverse)
                value = layers_of(wv, 0, i, j) * change * inverse
                adj[r, s, :, c] = value
                curvature = curvature + value * change
                low = face * value if low is None else low + face * value
                high = before * value if high is None else high + before * value
            ty[i, 0, piece, :] = low
            ty[i, 1, piece, :] = high
        return curvature

    def pack(dst, first, j, value):
        low = j % SUBLANES
        dst[first + j // SUBLANES, low : low + 1, :] = jnp.sum(value, axis=0, keepdims=True)

    def face_terms(f, low=True, high=True):
        for j in range(tiles):
            c = cut(j)
            total = None
            for s in range(steps):
                if low and high:
                    difference = adj[f, s, :, c] - adj[f + 1, s, :, c]
                elif low:
                    difference = adj[f, s, :, c]
                else:
                    difference = -adj[f + 1, s, :, c]
                value = fx[f, s, :, c] * difference
                total = value if total is None else total + value
            txa[f, pl.ds(j * SUBLANES, SUBLANES), :] = total

    def piece(j):
        return pl.ds(j * SUBLANES, SUBLANES)

    def pack_total(dst, first, i):
        high = [pltpu.roll(ty[i, 1, piece(j), :], LANES - 1, 1) for j in range(tiles)] + [0.0]
        terms = [
            ty[i, 0, piece(j), :] - jnp.where(not_last, high[j], high[j + 1])
            for j in range(tiles)
        ]
        low = [0.0] + [pltpu.roll(v, 1, 1) for v in terms]
        for j in range(tiles):
            value = txa[i, piece(j), :] + txa[i + 1, piece(j), :]
            value = value + (terms[j] + jnp.where(not_first, low[j + 1], low[j]))
            pack(dst, first, j, value)

    lax.fori_loop(1, rows, face_x, 0)
    loads["c"].wait()
    loads["w"].wait()
    curvature = lax.fori_loop(2, rows, cell_row, jnp.zeros((layers, LANES), F32))

    product = take(2 * steps)
    products = {}

    def send_products(s):
        near, _, far = shares(s)
        for k, (f, goal, part, side, index) in enumerate(
            ((0, last, near, left, halo + 1), (last, 0, far, right, halo))
        ):
            columns = lanes_of(part)
            cells = 0 if f == 0 else last + 1
            arrived(pm.at[cells, s, :, :, columns], index + 2 * s)
            face_part(f, s, part)
            number = product + 2 * s + k
            send(fx.at[f, s, :, columns], fx.at[goal, s, :, columns], (tm, side), number, number)
            products[s, k] = started.pop()

    send_products(0)

    def inner_faces(f, carry):
        face_terms(f)
        return carry

    lax.fori_loop(2, rows - 1, inner_faces, 0)
    for s in range(1, steps):
        send_products(s)

    def inner_rows(i, carry):
        pack_total(inner, (i - 2) * row_tiles, i)
        return carry

    lax.fori_loop(2, rows - 2, inner_rows, 0)

    half_tiles = (rows // CORES - 2) * row_tiles
    chunk = half_tiles // zhs
    inner_pair = take(1)
    send(
        inner.at[pl.ds((1 - core) * half_tiles, half_tiles)],
        inner_in,
        (other, sp),
        inner_pair,
        inner_pair,
    )

    arrived(inner_in, inner_pair)
    inner_sum[...] = inner[pl.ds(core * half_tiles, half_tiles)] + inner_in[...]
    scatter = take(zhs)
    for k in z_offsets:
        to = (zh + k) % zhs
        send(
            inner_sum.at[pl.ds(to * chunk, chunk)],
            rsb.at[k],
            z_peer(k),
            scatter + k,
            scatter + k,
        )

    arrived(rce.at[0], edge + 1)
    arrived(rce.at[1], edge)
    sbx[0] = jnp.broadcast_to(0.25 * (rce[0] + scaled[0:1, :]), wide)
    sbx[last] = jnp.broadcast_to(0.25 * (rce[1] + scaled[rows - 1 : rows, :]), wide)

    def no_face(states):
        @pl.when(sp == 0)
        def _():
            for s in states:
                fx[0, s] = jnp.zeros(wide, F32)

        @pl.when(sp == spaces - 1)
        def _():
            for s in states:
                fx[last, s] = jnp.zeros(wide, F32)

    def edge_rows(states, add, curvature):
        return lax.fori_loop(
            0, 2, lambda k, carry: cell_row(1 + k * (rows - 1), carry, states, add), curvature
        )

    for s in range(steps):
        near, both, far = shares(s)
        if len(both):
            for f, cells, k in ((last, last + 1, 0), (0, 0, 1)):
                arrived(pm.at[cells, s, :, :, lanes_of(both)], middle + 2 * s + k)
                face_part(f, s, both)
        for k, (f, part) in enumerate(((last, near), (0, far))):
            arrived(fx.at[f, s, :, lanes_of(part)], product + 2 * s + k)
            products[s, k].wait_send()
        no_face((s,))
        curvature = edge_rows((s,), s > 0, curvature)

    sz[my_line] = jnp.sum(curvature, axis=0, keepdims=True)
    over_line = take(line)
    for k, o in enumerate(line_offsets):
        send(sz.at[my_line], sz.at[my_line], line_peer(*o), over_line + k, over_line)

    face_terms(0, low=False)
    face_terms(last, high=False)
    face_terms(1)
    face_terms(rows - 1)
    for c, (edge_row, inner_row, face) in enumerate(((0, 1, 0), (rows - 1, rows - 2, last))):
        pack_total(edges.at[c], 0, edge_row)
        pack_total(edges.at[c], row_tiles, inner_row)
        for j in range(tiles):
            pack(edges.at[c], 2 * row_tiles, j, txa[face, piece(j), :])
    edge_pair = take(1)
    send(edges.at[1 - core], edges_in, (other, sp), edge_pair, edge_pair)

    reduced = inner_sum[pl.ds(zh * chunk, chunk)]
    for k in range(1, zhs):
        arrived(rsb.at[k], scatter + k)
        reduced = reduced + rsb[k]
    agb[core, pl.ds(zh * chunk, chunk)] = reduced
    mine = agb.at[core, pl.ds(zh * chunk, chunk)]
    gather = take(zhs)
    forward = take(zhs)
    for k in z_offsets:
        send(mine, mine, z_peer(k), gather + k, gather + k)
    send(mine, mine, (other, sp), forward, forward)

    two = 2 * row_tiles
    arrived(edges_in, edge_pair)
    summed = edges[core] + edges_in[...]
    edge_z[zh] = summed
    over_z = take(zhs)
    ghost = take(zhs)
    for k in z_offsets:
        send(
            edge_z.at[zh, pl.ds(0, two)],
            edge_z.at[zh, pl.ds(0, two)],
            z_peer(k),
            over_z + k,
            over_z + k,
        )
    side = left + core * (right - left)
    for k in z_offsets + [0]:
        send(
            edge_z.at[zh, pl.ds(two, row_tiles)],
            ghost_z.at[zh],
            (((zh + k) % zhs) * CORES + 1 - core, side),
            ghost + k,
            ghost + k,
        )

    arrived(sz.at[pl.ds(0, line - 1)], over_line)
    sxy[my_plane] = jnp.sum(sz[...], axis=0)
    over_plane = take(plane)
    for k, o in enumerate(plane_offsets):
        send(sxy.at[my_plane], sxy.at[my_plane], plane_peer(*o), over_plane + k, over_plane)

    def unpack(src, first, i):
        for j in range(tiles):
            low = j % SUBLANES
            value = src[first + j // SUBLANES, low : low + 1, :]
            out[i : i + 1, cut(j)] = value * factor[i : i + 1, cut(j)]

    for k in range(1, zhs):
        whose = agb.at[core, pl.ds(((zh + zhs - k) % zhs) * chunk, chunk)]
        arrived(whose, gather + k)
        send(whose, whose, (other, sp), forward + k, forward + k)

    for k in range(1, zhs):
        arrived(edge_z.at[(zh + zhs - k) % zhs, pl.ds(0, two)], over_z + k)
    for k in range(zhs):
        arrived(ghost_z.at[(zh + zhs - k) % zhs], ghost + k)
    total = edge_z[0, 0:two]
    beyond = ghost_z[0]
    for k in range(1, zhs):
        total = total + edge_z[k, 0:two]
        beyond = beyond + ghost_z[k]
    final[core, pl.ds(0, row_tiles)] = total[:row_tiles] + beyond
    final[core, pl.ds(row_tiles, row_tiles)] = total[row_tiles:]
    final_pair = take(1)
    send(final.at[core], final.at[core], (other, sp), final_pair, final_pair)

    for k in range(zhs):
        whose = agb.at[1 - core, pl.ds(((zh + zhs - k) % zhs) * chunk, chunk)]
        arrived(whose, forward + k)
    for i in range(2, rows - 2):
        first = (i - 2) * row_tiles
        unpack(agb.at[first // half_tiles], first % half_tiles, i)
    arrived(final.at[1 - core], final_pair)
    for c, (edge_row, inner_row) in enumerate(((0, 1), (rows - 1, rows - 2))):
        unpack(final.at[c], 0, edge_row)
        unpack(final.at[c], row_tiles, inner_row)

    for copy in started:
        copy.wait_send()
    arrived(sxy.at[pl.ds(0, plane - 1)], over_plane)
    whole = jnp.sum(sxy[...], axis=0)
    scale = 1.0 / (layers * steps * tms * rows * spaces * width)
    cur[...] = jnp.broadcast_to(jnp.sum(whole, axis=1, keepdims=True) * scale, cur.shape)


def shards(tms, spaces, pressure, mobility, capacity, misfit_weight, log_permeability, direction):
    _, steps, layers, rows, width = pressure.shape
    dims = (tms, spaces, steps, layers, rows, width)
    tiles = width // LANES
    zhs = tms // CORES
    ys = spaces // (CHIPS_X * Z_LO)
    line = zhs * Z_LO * CORES
    plane = ys * CHIPS_X
    flat = layers * rows * tiles
    row_tiles = tiles // SUBLANES
    half_tiles = (rows // CORES - 2) * row_tiles
    chunk = half_tiles // zhs
    copies = 6 * steps + 2 + 3 + 5 * zhs + line + plane
    vmem = pltpu.VMEM

    def in_tiles(array):
        count = array.size // (SUBLANES * width)
        cut = array.reshape(count, SUBLANES, tiles, LANES).transpose(0, 2, 1, 3)
        return cut.reshape(count * tiles * SUBLANES, LANES)

    def block(*shape):
        return vmem((*shape, SUBLANES, LANES), F32)

    product, curvature = pl.pallas_call(
        functools.partial(kernel, dims),
        out_shape=(
            jax.ShapeDtypeStruct((rows, width), F32),
            jax.ShapeDtypeStruct((1, LANES), F32),
        ),
        in_specs=[pl.BlockSpec(memory_space=pl.ANY)] * 6,
        out_specs=(
            pl.BlockSpec(memory_space=pltpu.VMEM),
            pl.BlockSpec(memory_space=pltpu.VMEM),
        ),
        scratch_shapes=[
            vmem((steps * flat, LANES), F32),
            vmem((steps * flat, LANES), F32),
            vmem((steps * flat, LANES), F32),
            vmem((flat, LANES), F32),
            vmem((rows, width), F32),
            vmem((rows, width), F32),
            vmem((rows + 2, steps, 2, layers, width), F32),
            vmem((rows + 1, steps, layers, width), F32),
            vmem((rows + 2, steps, layers, width), F32),
            vmem((rows + 1, tiles * layers, LANES), F32),
            vmem((rows, 2, tiles * layers, LANES), F32),
            vmem((rows + 1, layers, width), F32),
            vmem((rows, layers, width), F32),
            vmem((rows, layers, width), F32),
            vmem((rows, width), F32),
            vmem((2, 1, width), F32),
            vmem((2, 1, width), F32),
            block(CORES * half_tiles),
            block(half_tiles),
            block(half_tiles),
            block(zhs, chunk),
            block(CORES, half_tiles),
            block(CORES, 3 * row_tiles),
            block(3 * row_tiles),
            block(zhs, 3 * row_tiles),
            block(zhs, row_tiles),
            block(CORES, 2 * row_tiles),
            vmem((line, 1, LANES), F32),
            vmem((plane, 1, LANES), F32),
            pltpu.SemaphoreType.DMA((2 * steps + 4,)),
            pltpu.SemaphoreType.DMA((copies,)),
            pltpu.SemaphoreType.DMA((copies,)),
        ],
        compiler_params=pltpu.CompilerParams(
            collective_id=0, has_side_effects=True, vmem_limit_bytes=55040 << 10
        ),
        cost_estimate=pl.CostEstimate(
            flops=50 * steps * flat * LANES,
            bytes_accessed=14 * steps * flat * LANES,
            transcendentals=rows * width,
        ),
    )(
        in_tiles(pressure),
        in_tiles(mobility),
        in_tiles(capacity),
        in_tiles(misfit_weight),
        log_permeability,
        direction,
    )
    return product, curvature[0, 0]


def solution(mesh):
    placed = (
        P("tm", None, None, "space", None),
        P("tm", None, None, "space", None),
        P("tm", None, None, "space", None),
        P("tm", None, "space", None),
        P("space", None),
        P("space", None),
    )
    return jax.shard_map(
        functools.partial(shards, mesh.shape["tm"], mesh.shape["space"]),
        mesh=mesh,
        in_specs=placed,
        out_specs=(P("space", None), P()),
        check_vma=False,
    )
```

```python
import functools

import jax
import jax.numpy as jnp
from jax import lax
from jax.experimental import pallas as pl
from jax.experimental.pallas import tpu as pltpu
from jax.sharding import PartitionSpec as P

LANES = 128
SUBLANES = 8
CHIPS_X = 4
CORES = 2
Z_LO = 2
MESH = pl.DeviceIdType.MESH
F32 = jnp.float32


def kernel(
    dims,
    p_hbm,
    m_hbm,
    c_hbm,
    w_hbm,
    lp_hbm,
    d_hbm,
    out,
    cur,
    pv,
    mv,
    cv,
    wv,
    lpv,
    dv,
    pm,
    fx,
    adj,
    txa,
    ty,
    sbx,
    sby,
    sbb,
    factor,
    sce,
    rce,
    inner,
    inner_in,
    inner_sum,
    rsb,
    agb,
    edges,
    edges_in,
    edge_z,
    ghost_z,
    final,
    sz,
    sxy,
    local_sem,
    send_sem,
    recv_sem,
):
    tms, spaces, steps, layers, rows, width = dims
    tiles = width // LANES
    zhs = tms // CORES
    ys = spaces // (CHIPS_X * Z_LO)
    zs = zhs * Z_LO
    last = rows
    row_tiles = tiles // SUBLANES
    row_blocks = rows // SUBLANES
    layer_rows = row_blocks * tiles * SUBLANES
    state_rows = layers * layer_rows

    tm = lax.axis_index("tm")
    sp = lax.axis_index("space")
    zh, core = tm // CORES, tm % CORES
    zl = sp % Z_LO
    x = (sp // Z_LO) % CHIPS_X
    y = sp // (Z_LO * CHIPS_X)
    z = zh * Z_LO + zl
    left = (sp + spaces - 1) % spaces
    right = (sp + 1) % spaces
    other = (tm + 1) - 2 * core

    loads = {}

    def load(name, src, dst, index):
        loads[name] = pltpu.make_async_copy(src, dst, local_sem.at[index])
        loads[name].start()

    line = zs * CORES
    my_line = z * CORES + core
    plane = ys * CHIPS_X
    my_plane = y * CHIPS_X + x

    def apart(k, n):
        return min(k, n - k)

    line_offsets = sorted(
        ((dz, dc) for dz in range(zs) for dc in range(CORES) if (dz, dc) != (0, 0)),
        key=lambda o: -apart(o[0], zs),
    )
    plane_offsets = sorted(
        ((dy, dx) for dy in range(ys) for dx in range(CHIPS_X) if (dy, dx) != (0, 0)),
        key=lambda o: -apart(o[0], ys) - apart(o[1], CHIPS_X),
    )
    z_offsets = sorted(range(1, zhs), key=lambda k: -apart(k, zhs))

    def line_slot(dz, dc):
        return ((z + dz + zs) % zs) * CORES + (core + dc + CORES) % CORES

    def line_peer(dz, dc):
        to = (z + dz) % zs
        return ((to // Z_LO) * CORES + (core + dc) % CORES, sp - zl + to % Z_LO)

    def plane_slot(dy, dx):
        return ((y + dy + ys) % ys) * CHIPS_X + (x + dx + CHIPS_X) % CHIPS_X

    def plane_peer(dy, dx):
        return (tm, plane_slot(dy, dx) * Z_LO + zl)

    def z_peer(k):
        return (((zh + k) % zhs) * CORES + core, sp)

    across = left + zl * (right - left)
    greet = [(apart(dz, zs) + 0.5 * dc, line_peer(dz, dc)) for dz, dc in line_offsets]
    greet += [
        (apart(dy, ys) + apart(dx, CHIPS_X), plane_peer(dy, dx)) for dy, dx in plane_offsets
    ]
    greet += [
        (
            1.5 + Z_LO * apart(k, zhs),
            (((zh + k) % zhs) * CORES + (core + c) % CORES, across),
        )
        for k in range(zhs)
        for c in range(CORES)
    ]
    greet.sort(key=lambda entry: -entry[0])
    barrier = pltpu.get_barrier_semaphore()

    def say(peers):
        for _, peer in peers:
            pl.semaphore_signal(barrier, inc=1, device_id=peer, device_id_type=MESH)

    distant = sum(hops > 2.5 for hops, _ in greet)
    say(greet[:distant])
    for s in range(steps):
        part = pl.ds(s * state_rows, state_rows)
        load(("p", s), p_hbm.at[part, :], pv.at[part, :], 2 * s)
        load(("m", s), m_hbm.at[part, :], mv.at[part, :], 2 * s + 1)
    load("lp", lp_hbm, lpv, 2 * steps)
    load("d", d_hbm, dv, 2 * steps + 1)
    say(greet[distant:])

    sem_count = [0]
    started = []

    def send(src, dst, device, send_index, recv_index):
        copy = pltpu.make_async_remote_copy(
            src_ref=src,
            dst_ref=dst,
            send_sem=send_sem.at[send_index],
            recv_sem=recv_sem.at[recv_index],
            device_id=device,
            device_id_type=MESH,
        )
        copy.start()
        started.append(copy)

    def arrived(dst, recv_index):
        pltpu.make_async_copy(dst, dst, recv_sem.at[recv_index]).wait()

    def take(n):
        first = sem_count[0]
        sem_count[0] += n
        return first

    def layers_of(ref, s, i, j):
        first = (
            s * state_rows + (i // SUBLANES) * (tiles * SUBLANES) + j * SUBLANES + i % SUBLANES
        )
        return ref[pl.ds(first, layers, stride=layer_rows), :]

    def cut(j):
        return slice(j * LANES, (j + 1) * LANES)

    def spread(s, i):
        for which, ref in enumerate((pv, mv)):
            for j in range(tiles):
                pm[i + 1, s, which, :, cut(j)] = layers_of(ref, s, i, j)

    def shares(s):
        size = tiles // 2 if s == 0 else tiles // 4
        return range(size), range(size, tiles - size), range(tiles - size, tiles)

    def lanes_of(part):
        return pl.ds(part[0] * LANES, len(part) * LANES)

    halo = take(2 * steps)
    middle = take(2 * steps)
    for s in range(steps):
        loads["p", s].wait()
        loads["m", s].wait()
        spread(s, 0)
        spread(s, rows - 1)
        if s == 0:
            load("c", c_hbm, cv, 2 * steps + 2)
            load("w", w_hbm, wv, 2 * steps + 3)
            pl.semaphore_wait(barrier, len(greet))
        near, both, far = shares(s)
        for first, parts in ((halo, (far, near)), (middle, (both, both))):
            for k, part in enumerate(parts):
                if len(part):
                    row, goal, side = ((1, last + 1, left), (last, 0, right))[k]
                    columns = lanes_of(part)
                    send(
                        pm.at[row, s, :, :, columns],
                        pm.at[goal, s, :, :, columns],
                        (tm, side),
                        first + 2 * s + k,
                        first + 2 * s + k,
                    )

    loads["lp"].wait()
    loads["d"].wait()
    conduct = jnp.exp(lpv[...])
    factor[...] = conduct * (0.25 / (layers * steps * tms))
    scaled = conduct * dv[...]
    sce[0] = scaled[0:1, :]
    sce[1] = scaled[rows - 1 : rows, :]
    edge = take(2)
    send(sce.at[0], rce.at[1], (tm, left), edge, edge)
    send(sce.at[1], rce.at[0], (tm, right), edge + 1, edge + 1)

    wide = (layers, width)
    for i in range(rows):
        row = scaled[i : i + 1, :]
        if i + 1 < rows:
            sbx[i + 1] = jnp.broadcast_to(0.25 * (row + scaled[i + 1 : i + 2, :]), wide)
        sby[i] = jnp.broadcast_to(0.25 * (row + pltpu.roll(row, width - 1, 1)), wide)
        sbb[i] = jnp.broadcast_to(0.25 * (row + pltpu.roll(row, 1, 1)), wide)

    def spread_inner(i, carry):
        for s in range(steps):
            spread(s, i)
        return carry

    lax.fori_loop(1, rows - 1, spread_inner, 0)

    lane = lax.broadcasted_iota(jnp.int32, (layers, LANES), 1)
    not_last = lane < LANES - 1
    not_first = lane > 0

    def face_part(f, s, part):
        for j in part:
            c = cut(j)
            fx[f, s, :, c] = (pm[f, s, 1, :, c] + pm[f + 1, s, 1, :, c]) * (
                pm[f + 1, s, 0, :, c] - pm[f, s, 0, :, c]
            )

    def face_x(f, carry):
        for s in range(steps):
            face_part(f, s, range(tiles))
        return carry

    def cell_row(r, curvature, states=range(steps), add=False):
        i = r - 1

        def ahead(here, later):
            return jnp.where(not_last, here, later)

        def turned(s, j):
            pressure, mobility = pm[r, s, 0, :, cut(j)], pm[r, s, 1, :, cut(j)]
            return (
                pressure,
                mobility,
                pltpu.roll(pressure, LANES - 1, 1),
                pltpu.roll(mobility, LANES - 1, 1),
            )

        here = {s: turned(s, 0) for s in states}
        spill = {s: 0.0 for s in states}
        for j in range(tiles):
            c = cut(j)
            piece = pl.ds(j * SUBLANES, SUBLANES)
            low, high = (ty[i, 0, piece, :], ty[i, 1, piece, :]) if add else (None, None)
            for s in states:
                pressure, mobility, p_back, m_back = here[s]
                if j + 1 < tiles:
                    here[s] = turned(s, j + 1)
                    p_next, m_next = here[s][2], here[s][3]
                else:
                    p_next, m_next = pressure, mobility
                face = (mobility + ahead(m_back, m_next)) * (ahead(p_back, p_next) - pressure)
                turned_face = pltpu.roll(face, 1, 1)
                before = jnp.where(not_first, turned_face, spill[s])
                spill[s] = turned_face
                change = (
                    fx[r, s, :, c] * sbx[r, :, c]
                    - fx[r - 1, s, :, c] * sbx[r - 1, :, c]
                    + (face * sby[i, :, c] - before * sbb[i, :, c])
                )
                square = layers_of(cv, s, i, j)
                square = square * square
                inverse = pl.reciprocal(square, approx=True)
                inverse = inverse * (2.0 - square * inverse)
                value = layers_of(wv, 0, i, j) * change * inverse
                adj[r, s, :, c] = value
                curvature = curvature + value * change
                low = face * value if low is None else low + face * value
                high = before * value if high is None else high + before * value
            ty[i, 0, piece, :] = low
            ty[i, 1, piece, :] = high
        return curvature

    def pack(dst, first, j, value):
        low = j % SUBLANES
        dst[first + j // SUBLANES, low : low + 1, :] = jnp.sum(value, axis=0, keepdims=True)

    def face_terms(f, low=True, high=True):
        for j in range(tiles):
            c = cut(j)
            total = None
            for s in range(steps):
                if low and high:
                    difference = adj[f, s, :, c] - adj[f + 1, s, :, c]
                elif low:
                    difference = adj[f, s, :, c]
                else:
                    difference = -adj[f + 1, s, :, c]
                value = fx[f, s, :, c] * difference
                total = value if total is None else total + value
            txa[f, pl.ds(j * SUBLANES, SUBLANES), :] = total

    def piece(j):
        return pl.ds(j * SUBLANES, SUBLANES)

    def pack_total(dst, first, i):
        high = [pltpu.roll(ty[i, 1, piece(j), :], LANES - 1, 1) for j in range(tiles)] + [0.0]
        terms = [
            ty[i, 0, piece(j), :] - jnp.where(not_last, high[j], high[j + 1])
            for j in range(tiles)
        ]
        low = [0.0] + [pltpu.roll(v, 1, 1) for v in terms]
        for j in range(tiles):
            value = txa[i, piece(j), :] + txa[i + 1, piece(j), :]
            value = value + (terms[j] + jnp.where(not_first, low[j + 1], low[j]))
            pack(dst, first, j, value)

    lax.fori_loop(1, rows, face_x, 0)
    loads["c"].wait()
    loads["w"].wait()
    curvature = lax.fori_loop(2, rows, cell_row, jnp.zeros((layers, LANES), F32))

    product = take(2 * steps)
    products = {}

    def send_products(s):
        near, _, far = shares(s)
        for k, (f, goal, part, side, index) in enumerate(
            ((0, last, near, left, halo + 1), (last, 0, far, right, halo))
        ):
            columns = lanes_of(part)
            cells = 0 if f == 0 else last + 1
            arrived(pm.at[cells, s, :, :, columns], index + 2 * s)
            face_part(f, s, part)
            number = product + 2 * s + k
            send(fx.at[f, s, :, columns], fx.at[goal, s, :, columns], (tm, side), number, number)
            products[s, k] = started.pop()

    send_products(0)

    def inner_faces(f, carry):
        face_terms(f)
        return carry

    lax.fori_loop(2, rows - 1, inner_faces, 0)
    for s in range(1, steps):
        send_products(s)

    def inner_rows(i, carry):
        pack_total(inner, (i - 2) * row_tiles, i)
        return carry

    lax.fori_loop(2, rows - 2, inner_rows, 0)

    half_tiles = (rows // CORES - 2) * row_tiles
    chunk = half_tiles // zhs
    inner_pair = take(1)
    send(
        inner.at[pl.ds((1 - core) * half_tiles, half_tiles)],
        inner_in,
        (other, sp),
        inner_pair,
        inner_pair,
    )

    arrived(inner_in, inner_pair)
    inner_sum[...] = inner[pl.ds(core * half_tiles, half_tiles)] + inner_in[...]
    scatter = take(zhs)
    for k in z_offsets:
        to = (zh + k) % zhs
        send(
            inner_sum.at[pl.ds(to * chunk, chunk)],
            rsb.at[k],
            z_peer(k),
            scatter + k,
            scatter + k,
        )

    arrived(rce.at[0], edge + 1)
    arrived(rce.at[1], edge)
    sbx[0] = jnp.broadcast_to(0.25 * (rce[0] + scaled[0:1, :]), wide)
    sbx[last] = jnp.broadcast_to(0.25 * (rce[1] + scaled[rows - 1 : rows, :]), wide)

    def no_face(states):
        @pl.when(sp == 0)
        def _():
            for s in states:
                fx[0, s] = jnp.zeros(wide, F32)

        @pl.when(sp == spaces - 1)
        def _():
            for s in states:
                fx[last, s] = jnp.zeros(wide, F32)

    def edge_rows(states, add, curvature):
        for r in (1, last):
            curvature = cell_row(r, curvature, states, add)
        return curvature

    for s in range(steps):
        near, both, far = shares(s)
        if len(both):
            for f, cells, k in ((last, last + 1, 0), (0, 0, 1)):
                arrived(pm.at[cells, s, :, :, lanes_of(both)], middle + 2 * s + k)
                face_part(f, s, both)
        for k, (f, part) in enumerate(((last, near), (0, far))):
            arrived(fx.at[f, s, :, lanes_of(part)], product + 2 * s + k)
            products[s, k].wait_send()
        no_face((s,))
        curvature = edge_rows((s,), s > 0, curvature)

    sz[my_line] = jnp.sum(curvature, axis=0, keepdims=True)
    over_line = take(line)
    for k, o in enumerate(line_offsets):
        send(sz.at[my_line], sz.at[my_line], line_peer(*o), over_line + k, over_line)

    face_terms(0, low=False)
    face_terms(last, high=False)
    face_terms(1)
    face_terms(rows - 1)
    for c, (edge_row, inner_row, face) in enumerate(((0, 1, 0), (rows - 1, rows - 2, last))):
        pack_total(edges.at[c], 0, edge_row)
        pack_total(edges.at[c], row_tiles, inner_row)
        for j in range(tiles):
            pack(edges.at[c], 2 * row_tiles, j, txa[face, piece(j), :])
    edge_pair = take(1)
    send(edges.at[1 - core], edges_in, (other, sp), edge_pair, edge_pair)

    reduced = inner_sum[pl.ds(zh * chunk, chunk)]
    for k in range(1, zhs):
        arrived(rsb.at[k], scatter + k)
        reduced = reduced + rsb[k]
    agb[core, pl.ds(zh * chunk, chunk)] = reduced
    mine = agb.at[core, pl.ds(zh * chunk, chunk)]
    gather = take(zhs)
    forward = take(zhs)
    for k in z_offsets:
        send(mine, mine, z_peer(k), gather + k, gather + k)
    send(mine, mine, (other, sp), forward, forward)

    two = 2 * row_tiles
    arrived(edges_in, edge_pair)
    summed = edges[core] + edges_in[...]
    edge_z[zh] = summed
    over_z = take(zhs)
    ghost = take(zhs)
    for k in z_offsets:
        send(
            edge_z.at[zh, pl.ds(0, two)],
            edge_z.at[zh, pl.ds(0, two)],
            z_peer(k),
            over_z + k,
            over_z + k,
        )
    side = left + core * (right - left)
    for k in z_offsets + [0]:
        send(
            edge_z.at[zh, pl.ds(two, row_tiles)],
            ghost_z.at[zh],
            (((zh + k) % zhs) * CORES + 1 - core, side),
            ghost + k,
            ghost + k,
        )

    arrived(sz.at[pl.ds(0, line - 1)], over_line)
    sxy[my_plane] = jnp.sum(sz[...], axis=0)
    over_plane = take(plane)
    for k, o in enumerate(plane_offsets):
        send(sxy.at[my_plane], sxy.at[my_plane], plane_peer(*o), over_plane + k, over_plane)

    def unpack(src, first, i):
        for j in range(tiles):
            low = j % SUBLANES
            value = src[first + j // SUBLANES, low : low + 1, :]
            out[i : i + 1, cut(j)] = value * factor[i : i + 1, cut(j)]

    for k in range(1, zhs):
        whose = agb.at[core, pl.ds(((zh + zhs - k) % zhs) * chunk, chunk)]
        arrived(whose, gather + k)
        send(whose, whose, (other, sp), forward + k, forward + k)

    for k in range(1, zhs):
        arrived(edge_z.at[(zh + zhs - k) % zhs, pl.ds(0, two)], over_z + k)
    for k in range(zhs):
        arrived(ghost_z.at[(zh + zhs - k) % zhs], ghost + k)
    total = edge_z[0, 0:two]
    beyond = ghost_z[0]
    for k in range(1, zhs):
        total = total + edge_z[k, 0:two]
        beyond = beyond + ghost_z[k]
    final[core, pl.ds(0, row_tiles)] = total[:row_tiles] + beyond
    final[core, pl.ds(row_tiles, row_tiles)] = total[row_tiles:]
    final_pair = take(1)
    send(final.at[core], final.at[core], (other, sp), final_pair, final_pair)

    for k in range(zhs):
        whose = agb.at[1 - core, pl.ds(((zh + zhs - k) % zhs) * chunk, chunk)]
        arrived(whose, forward + k)
    for i in range(2, rows - 2):
        first = (i - 2) * row_tiles
        unpack(agb.at[first // half_tiles], first % half_tiles, i)
    arrived(final.at[1 - core], final_pair)
    for c, (edge_row, inner_row) in enumerate(((0, 1), (rows - 1, rows - 2))):
        unpack(final.at[c], 0, edge_row)
        unpack(final.at[c], row_tiles, inner_row)

    for copy in started:
        copy.wait_send()
    arrived(sxy.at[pl.ds(0, plane - 1)], over_plane)
    whole = jnp.sum(sxy[...], axis=0)
    scale = 1.0 / (layers * steps * tms * rows * spaces * width)
    cur[...] = jnp.broadcast_to(jnp.sum(whole, axis=1, keepdims=True) * scale, cur.shape)


def shards(tms, spaces, pressure, mobility, capacity, misfit_weight, log_permeability, direction):
    _, steps, layers, rows, width = pressure.shape
    dims = (tms, spaces, steps, layers, rows, width)
    tiles = width // LANES
    zhs = tms // CORES
    ys = spaces // (CHIPS_X * Z_LO)
    line = zhs * Z_LO * CORES
    plane = ys * CHIPS_X
    flat = layers * rows * tiles
    row_tiles = tiles // SUBLANES
    half_tiles = (rows // CORES - 2) * row_tiles
    chunk = half_tiles // zhs
    copies = 6 * steps + 2 + 3 + 5 * zhs + line + plane
    vmem = pltpu.VMEM

    def in_tiles(array):
        count = array.size // (SUBLANES * width)
        cut = array.reshape(count, SUBLANES, tiles, LANES).transpose(0, 2, 1, 3)
        return cut.reshape(count * tiles * SUBLANES, LANES)

    def block(*shape):
        return vmem((*shape, SUBLANES, LANES), F32)

    product, curvature = pl.pallas_call(
        functools.partial(kernel, dims),
        out_shape=(
            jax.ShapeDtypeStruct((rows, width), F32),
            jax.ShapeDtypeStruct((1, LANES), F32),
        ),
        in_specs=[pl.BlockSpec(memory_space=pl.ANY)] * 6,
        out_specs=(
            pl.BlockSpec(memory_space=pltpu.VMEM),
            pl.BlockSpec(memory_space=pltpu.VMEM),
        ),
        scratch_shapes=[
            vmem((steps * flat, LANES), F32),
            vmem((steps * flat, LANES), F32),
            vmem((steps * flat, LANES), F32),
            vmem((flat, LANES), F32),
            vmem((rows, width), F32),
            vmem((rows, width), F32),
            vmem((rows + 2, steps, 2, layers, width), F32),
            vmem((rows + 1, steps, layers, width), F32),
            vmem((rows + 2, steps, layers, width), F32),
            vmem((rows + 1, tiles * layers, LANES), F32),
            vmem((rows, 2, tiles * layers, LANES), F32),
            vmem((rows + 1, layers, width), F32),
            vmem((rows, layers, width), F32),
            vmem((rows, layers, width), F32),
            vmem((rows, width), F32),
            vmem((2, 1, width), F32),
            vmem((2, 1, width), F32),
            block(CORES * half_tiles),
            block(half_tiles),
            block(half_tiles),
            block(zhs, chunk),
            block(CORES, half_tiles),
            block(CORES, 3 * row_tiles),
            block(3 * row_tiles),
            block(zhs, 3 * row_tiles),
            block(zhs, row_tiles),
            block(CORES, 2 * row_tiles),
            vmem((line, 1, LANES), F32),
            vmem((plane, 1, LANES), F32),
            pltpu.SemaphoreType.DMA((2 * steps + 4,)),
            pltpu.SemaphoreType.DMA((copies,)),
            pltpu.SemaphoreType.DMA((copies,)),
        ],
        compiler_params=pltpu.CompilerParams(
            collective_id=0, has_side_effects=True, vmem_limit_bytes=55040 << 10
        ),
        cost_estimate=pl.CostEstimate(
            flops=50 * steps * flat * LANES,
            bytes_accessed=14 * steps * flat * LANES,
            transcendentals=rows * width,
        ),
    )(
        in_tiles(pressure),
        in_tiles(mobility),
        in_tiles(capacity),
        in_tiles(misfit_weight),
        log_permeability,
        direction,
    )
    return product, curvature[0, 0]


def solution(mesh):
    placed = (
        P("tm", None, None, "space", None),
        P("tm", None, None, "space", None),
        P("tm", None, None, "space", None),
        P("tm", None, "space", None),
        P("space", None),
        P("space", None),
    )
    return jax.shard_map(
        functools.partial(shards, mesh.shape["tm"], mesh.shape["space"]),
        mesh=mesh,
        in_specs=placed,
        out_specs=(P("space", None), P()),
        check_vma=False,
    )
```

```python
import functools

import jax
import jax.numpy as jnp
from jax import lax
from jax.experimental import pallas as pl
from jax.experimental.pallas import tpu as pltpu
from jax.sharding import PartitionSpec as P

LANES = 128
SUBLANES = 8
CHIPS_X = 4
CORES = 2
Z_LO = 2
MESH = pl.DeviceIdType.MESH
F32 = jnp.float32


def kernel(
    dims,
    p_hbm,
    m_hbm,
    c_hbm,
    w_hbm,
    lp_hbm,
    d_hbm,
    out,
    cur,
    pv,
    mv,
    cv,
    wv,
    lpv,
    dv,
    pm,
    fx,
    adj,
    txa,
    ty,
    sbx,
    sby,
    sbb,
    factor,
    sce,
    rce,
    inner,
    inner_in,
    inner_sum,
    rsb,
    agb,
    edges,
    edges_in,
    edge_z,
    ghost_z,
    final,
    sz,
    sxy,
    local_sem,
    send_sem,
    recv_sem,
):
    tms, spaces, steps, layers, rows, width = dims
    tiles = width // LANES
    zhs = tms // CORES
    ys = spaces // (CHIPS_X * Z_LO)
    zs = zhs * Z_LO
    last = rows
    row_tiles = tiles // SUBLANES
    row_blocks = rows // SUBLANES
    layer_rows = row_blocks * tiles * SUBLANES
    state_rows = layers * layer_rows

    tm = lax.axis_index("tm")
    sp = lax.axis_index("space")
    zh, core = tm // CORES, tm % CORES
    zl = sp % Z_LO
    x = (sp // Z_LO) % CHIPS_X
    y = sp // (Z_LO * CHIPS_X)
    z = zh * Z_LO + zl
    left = (sp + spaces - 1) % spaces
    right = (sp + 1) % spaces
    other = (tm + 1) - 2 * core

    loads = {}

    def load(name, src, dst, index):
        loads[name] = pltpu.make_async_copy(src, dst, local_sem.at[index])
        loads[name].start()

    line = zs * CORES
    my_line = z * CORES + core
    plane = ys * CHIPS_X
    my_plane = y * CHIPS_X + x

    def apart(k, n):
        return min(k, n - k)

    line_offsets = sorted(
        ((dz, dc) for dz in range(zs) for dc in range(CORES) if (dz, dc) != (0, 0)),
        key=lambda o: -apart(o[0], zs),
    )
    plane_offsets = sorted(
        ((dy, dx) for dy in range(ys) for dx in range(CHIPS_X) if (dy, dx) != (0, 0)),
        key=lambda o: -apart(o[0], ys) - apart(o[1], CHIPS_X),
    )
    z_offsets = sorted(range(1, zhs), key=lambda k: -apart(k, zhs))

    def line_slot(dz, dc):
        return ((z + dz + zs) % zs) * CORES + (core + dc + CORES) % CORES

    def line_peer(dz, dc):
        to = (z + dz) % zs
        return ((to // Z_LO) * CORES + (core + dc) % CORES, sp - zl + to % Z_LO)

    def plane_slot(dy, dx):
        return ((y + dy + ys) % ys) * CHIPS_X + (x + dx + CHIPS_X) % CHIPS_X

    def plane_peer(dy, dx):
        return (tm, plane_slot(dy, dx) * Z_LO + zl)

    def z_peer(k):
        return (((zh + k) % zhs) * CORES + core, sp)

    across = left + zl * (right - left)
    greet = [(apart(dz, zs) + 0.5 * dc, line_peer(dz, dc)) for dz, dc in line_offsets]
    greet += [
        (apart(dy, ys) + apart(dx, CHIPS_X), plane_peer(dy, dx)) for dy, dx in plane_offsets
    ]
    greet += [
        (
            1.5 + Z_LO * apart(k, zhs),
            (((zh + k) % zhs) * CORES + (core + c) % CORES, across),
        )
        for k in range(zhs)
        for c in range(CORES)
    ]
    greet.sort(key=lambda entry: -entry[0])
    barrier = pltpu.get_barrier_semaphore()

    def say(peers):
        for _, peer in peers:
            pl.semaphore_signal(barrier, inc=1, device_id=peer, device_id_type=MESH)

    distant = sum(hops > 2.5 for hops, _ in greet)
    say(greet[:distant])
    for s in range(steps):
        part = pl.ds(s * state_rows, state_rows)
        load(("p", s), p_hbm.at[part, :], pv.at[part, :], 2 * s)
        load(("m", s), m_hbm.at[part, :], mv.at[part, :], 2 * s + 1)
    load("lp", lp_hbm, lpv, 2 * steps)
    load("d", d_hbm, dv, 2 * steps + 1)
    say(greet[distant:])

    sem_count = [0]
    started = []

    def send(src, dst, device, send_index, recv_index):
        copy = pltpu.make_async_remote_copy(
            src_ref=src,
            dst_ref=dst,
            send_sem=send_sem.at[send_index],
            recv_sem=recv_sem.at[recv_index],
            device_id=device,
            device_id_type=MESH,
        )
        copy.start()
        started.append(copy)

    def arrived(dst, recv_index):
        pltpu.make_async_copy(dst, dst, recv_sem.at[recv_index]).wait()

    def take(n):
        first = sem_count[0]
        sem_count[0] += n
        return first

    def layers_of(ref, s, i, j):
        first = (
            s * state_rows + (i // SUBLANES) * (tiles * SUBLANES) + j * SUBLANES + i % SUBLANES
        )
        return ref[pl.ds(first, layers, stride=layer_rows), :]

    def cut(j):
        return slice(j * LANES, (j + 1) * LANES)

    def spread(s, i):
        for which, ref in enumerate((pv, mv)):
            for j in range(tiles):
                pm[i + 1, s, which, :, cut(j)] = layers_of(ref, s, i, j)

    def shares(s):
        size = tiles // 2 if s == 0 else tiles // 4
        return range(size), range(size, tiles - size), range(tiles - size, tiles)

    def lanes_of(part):
        return pl.ds(part[0] * LANES, len(part) * LANES)

    halo = take(2 * steps)
    middle = take(2 * steps)
    for s in range(steps):
        loads["p", s].wait()
        loads["m", s].wait()
        spread(s, 0)
        spread(s, rows - 1)
        if s == 0:
            load("c", c_hbm, cv, 2 * steps + 2)
            load("w", w_hbm, wv, 2 * steps + 3)
            pl.semaphore_wait(barrier, len(greet))
        near, both, far = shares(s)
        for first, parts in ((halo, (far, near)), (middle, (both, both))):
            for k, part in enumerate(parts):
                if len(part):
                    row, goal, side = ((1, last + 1, left), (last, 0, right))[k]
                    columns = lanes_of(part)
                    send(
                        pm.at[row, s, :, :, columns],
                        pm.at[goal, s, :, :, columns],
                        (tm, side),
                        first + 2 * s + k,
                        first + 2 * s + k,
                    )

    loads["lp"].wait()
    loads["d"].wait()
    conduct = jnp.exp(lpv[...])
    factor[...] = conduct * (0.25 / (layers * steps * tms))
    scaled = conduct * dv[...]
    sce[0] = scaled[0:1, :]
    sce[1] = scaled[rows - 1 : rows, :]
    edge = take(2)
    send(sce.at[0], rce.at[1], (tm, left), edge, edge)
    send(sce.at[1], rce.at[0], (tm, right), edge + 1, edge + 1)

    wide = (layers, width)
    for i in range(rows):
        row = scaled[i : i + 1, :]
        if i + 1 < rows:
            sbx[i + 1] = jnp.broadcast_to(0.25 * (row + scaled[i + 1 : i + 2, :]), wide)
        sby[i] = jnp.broadcast_to(0.25 * (row + pltpu.roll(row, width - 1, 1)), wide)
        sbb[i] = jnp.broadcast_to(0.25 * (row + pltpu.roll(row, 1, 1)), wide)

    def spread_inner(i, carry):
        for s in range(steps):
            spread(s, i)
        return carry

    lax.fori_loop(1, rows - 1, spread_inner, 0)

    lane = lax.broadcasted_iota(jnp.int32, (layers, LANES), 1)
    not_last = lane < LANES - 1
    not_first = lane > 0

    def face_part(f, s, part):
        for j in part:
            c = cut(j)
            fx[f, s, :, c] = (pm[f, s, 1, :, c] + pm[f + 1, s, 1, :, c]) * (
                pm[f + 1, s, 0, :, c] - pm[f, s, 0, :, c]
            )

    def face_x(f, carry):
        for s in range(steps):
            face_part(f, s, range(tiles))
        return carry

    def cell_row(r, curvature, states=range(steps), add=False):
        i = r - 1

        def ahead(here, later):
            return jnp.where(not_last, here, later)

        def turned(s, j):
            pressure, mobility = pm[r, s, 0, :, cut(j)], pm[r, s, 1, :, cut(j)]
            return (
                pressure,
                mobility,
                pltpu.roll(pressure, LANES - 1, 1),
                pltpu.roll(mobility, LANES - 1, 1),
            )

        here = {s: turned(s, 0) for s in states}
        spill = {s: 0.0 for s in states}
        for j in range(tiles):
            c = cut(j)
            piece = pl.ds(j * SUBLANES, SUBLANES)
            low, high = (ty[i, 0, piece, :], ty[i, 1, piece, :]) if add else (None, None)
            for s in states:
                pressure, mobility, p_back, m_back = here[s]
                if j + 1 < tiles:
                    here[s] = turned(s, j + 1)
                    p_next, m_next = here[s][2], here[s][3]
                else:
                    p_next, m_next = pressure, mobility
                face = (mobility + ahead(m_back, m_next)) * (ahead(p_back, p_next) - pressure)
                turned_face = pltpu.roll(face, 1, 1)
                before = jnp.where(not_first, turned_face, spill[s])
                spill[s] = turned_face
                change = (
                    fx[r, s, :, c] * sbx[r, :, c]
                    - fx[r - 1, s, :, c] * sbx[r - 1, :, c]
                    + (face * sby[i, :, c] - before * sbb[i, :, c])
                )
                square = layers_of(cv, s, i, j)
                square = square * square
                inverse = pl.reciprocal(square, approx=True)
                inverse = inverse * (2.0 - square * inverse)
                value = layers_of(wv, 0, i, j) * change * inverse
                adj[r, s, :, c] = value
                curvature = curvature + value * change
                low = face * value if low is None else low + face * value
                high = before * value if high is None else high + before * value
            ty[i, 0, piece, :] = low
            ty[i, 1, piece, :] = high
        return curvature

    def pack(dst, first, j, value):
        low = j % SUBLANES
        dst[first + j // SUBLANES, low : low + 1, :] = jnp.sum(value, axis=0, keepdims=True)

    def face_terms(f, low=True, high=True):
        for j in range(tiles):
            c = cut(j)
            total = None
            for s in range(steps):
                if low and high:
                    difference = adj[f, s, :, c] - adj[f + 1, s, :, c]
                elif low:
                    difference = adj[f, s, :, c]
                else:
                    difference = -adj[f + 1, s, :, c]
                value = fx[f, s, :, c] * difference
                total = value if total is None else total + value
            txa[f, pl.ds(j * SUBLANES, SUBLANES), :] = total

    def piece(j):
        return pl.ds(j * SUBLANES, SUBLANES)

    def pack_total(dst, first, i):
        high = [pltpu.roll(ty[i, 1, piece(j), :], LANES - 1, 1) for j in range(tiles)] + [0.0]
        terms = [
            ty[i, 0, piece(j), :] - jnp.where(not_last, high[j], high[j + 1])
            for j in range(tiles)
        ]
        low = [0.0] + [pltpu.roll(v, 1, 1) for v in terms]
        for j in range(tiles):
            value = txa[i, piece(j), :] + txa[i + 1, piece(j), :]
            value = value + (terms[j] + jnp.where(not_first, low[j + 1], low[j]))
            pack(dst, first, j, value)

    lax.fori_loop(1, rows, face_x, 0)
    loads["c"].wait()
    loads["w"].wait()
    curvature = lax.fori_loop(2, rows, cell_row, jnp.zeros((layers, LANES), F32))

    product = take(2 * steps)
    products = {}

    def send_products(s):
        near, _, far = shares(s)
        for k, (f, goal, part, side, index) in enumerate(
            ((0, last, near, left, halo + 1), (last, 0, far, right, halo))
        ):
            columns = lanes_of(part)
            cells = 0 if f == 0 else last + 1
            arrived(pm.at[cells, s, :, :, columns], index + 2 * s)
            face_part(f, s, part)
            number = product + 2 * s + k
            send(fx.at[f, s, :, columns], fx.at[goal, s, :, columns], (tm, side), number, number)
            products[s, k] = started.pop()

    send_products(0)

    def inner_faces(f, carry):
        face_terms(f)
        return carry

    lax.fori_loop(2, rows - 1, inner_faces, 0)
    for s in range(1, steps):
        send_products(s)

    def inner_rows(i, carry):
        pack_total(inner, (i - 2) * row_tiles, i)
        return carry

    lax.fori_loop(2, rows - 2, inner_rows, 0)

    half_tiles = (rows // CORES - 2) * row_tiles
    chunk = half_tiles // zhs
    inner_pair = take(1)
    send(
        inner.at[pl.ds((1 - core) * half_tiles, half_tiles)],
        inner_in,
        (other, sp),
        inner_pair,
        inner_pair,
    )

    arrived(rce.at[0], edge + 1)
    arrived(rce.at[1], edge)
    sbx[0] = jnp.broadcast_to(0.25 * (rce[0] + scaled[0:1, :]), wide)
    sbx[last] = jnp.broadcast_to(0.25 * (rce[1] + scaled[rows - 1 : rows, :]), wide)

    def no_face(states):
        @pl.when(sp == 0)
        def _():
            for s in states:
                fx[0, s] = jnp.zeros(wide, F32)

        @pl.when(sp == spaces - 1)
        def _():
            for s in states:
                fx[last, s] = jnp.zeros(wide, F32)

    def edge_rows(states, add, curvature):
        return lax.fori_loop(
            0, 2, lambda k, carry: cell_row(1 + k * (rows - 1), carry, states, add), curvature
        )

    for s in range(steps):
        near, both, far = shares(s)
        if len(both):
            for f, cells, k in ((last, last + 1, 0), (0, 0, 1)):
                arrived(pm.at[cells, s, :, :, lanes_of(both)], middle + 2 * s + k)
                face_part(f, s, both)
        for k, (f, part) in enumerate(((last, near), (0, far))):
            arrived(fx.at[f, s, :, lanes_of(part)], product + 2 * s + k)
            products[s, k].wait_send()
        no_face((s,))
        curvature = edge_rows((s,), s > 0, curvature)

    sz[my_line] = jnp.sum(curvature, axis=0, keepdims=True)
    over_line = take(line)
    for k, o in enumerate(line_offsets):
        send(sz.at[my_line], sz.at[my_line], line_peer(*o), over_line + k, over_line)

    arrived(inner_in, inner_pair)
    inner_sum[...] = inner[pl.ds(core * half_tiles, half_tiles)] + inner_in[...]
    scatter = take(zhs)
    for k in z_offsets:
        to = (zh + k) % zhs
        send(
            inner_sum.at[pl.ds(to * chunk, chunk)],
            rsb.at[k],
            z_peer(k),
            scatter + k,
            scatter + k,
        )

    face_terms(0, low=False)
    face_terms(last, high=False)
    face_terms(1)
    face_terms(rows - 1)
    for c, (edge_row, inner_row, face) in enumerate(((0, 1, 0), (rows - 1, rows - 2, last))):
        pack_total(edges.at[c], 0, edge_row)
        pack_total(edges.at[c], row_tiles, inner_row)
        for j in range(tiles):
            pack(edges.at[c], 2 * row_tiles, j, txa[face, piece(j), :])
    edge_pair = take(1)
    send(edges.at[1 - core], edges_in, (other, sp), edge_pair, edge_pair)

    two = 2 * row_tiles
    arrived(edges_in, edge_pair)
    summed = edges[core] + edges_in[...]
    edge_z[zh] = summed
    over_z = take(zhs)
    ghost = take(zhs)
    for k in z_offsets:
        send(
            edge_z.at[zh, pl.ds(0, two)],
            edge_z.at[zh, pl.ds(0, two)],
            z_peer(k),
            over_z + k,
            over_z + k,
        )
    side = left + core * (right - left)
    for k in z_offsets + [0]:
        send(
            edge_z.at[zh, pl.ds(two, row_tiles)],
            ghost_z.at[zh],
            (((zh + k) % zhs) * CORES + 1 - core, side),
            ghost + k,
            ghost + k,
        )

    reduced = inner_sum[pl.ds(zh * chunk, chunk)]
    for k in range(1, zhs):
        arrived(rsb.at[k], scatter + k)
        reduced = reduced + rsb[k]
    agb[core, pl.ds(zh * chunk, chunk)] = reduced
    mine = agb.at[core, pl.ds(zh * chunk, chunk)]
    gather = take(zhs)
    forward = take(zhs)
    for k in z_offsets:
        send(mine, mine, z_peer(k), gather + k, gather + k)
    send(mine, mine, (other, sp), forward, forward)

    arrived(sz.at[pl.ds(0, line - 1)], over_line)
    sxy[my_plane] = jnp.sum(sz[...], axis=0)
    over_plane = take(plane)
    for k, o in enumerate(plane_offsets):
        send(sxy.at[my_plane], sxy.at[my_plane], plane_peer(*o), over_plane + k, over_plane)

    def unpack(src, first, i):
        for j in range(tiles):
            low = j % SUBLANES
            value = src[first + j // SUBLANES, low : low + 1, :]
            out[i : i + 1, cut(j)] = value * factor[i : i + 1, cut(j)]

    for k in range(1, zhs):
        whose = agb.at[core, pl.ds(((zh + zhs - k) % zhs) * chunk, chunk)]
        arrived(whose, gather + k)
        send(whose, whose, (other, sp), forward + k, forward + k)

    for k in range(1, zhs):
        arrived(edge_z.at[(zh + zhs - k) % zhs, pl.ds(0, two)], over_z + k)
    for k in range(zhs):
        arrived(ghost_z.at[(zh + zhs - k) % zhs], ghost + k)
    total = edge_z[0, 0:two]
    beyond = ghost_z[0]
    for k in range(1, zhs):
        total = total + edge_z[k, 0:two]
        beyond = beyond + ghost_z[k]
    final[core, pl.ds(0, row_tiles)] = total[:row_tiles] + beyond
    final[core, pl.ds(row_tiles, row_tiles)] = total[row_tiles:]
    final_pair = take(1)
    send(final.at[core], final.at[core], (other, sp), final_pair, final_pair)

    for k in range(zhs):
        whose = agb.at[1 - core, pl.ds(((zh + zhs - k) % zhs) * chunk, chunk)]
        arrived(whose, forward + k)
    for i in range(2, rows - 2):
        first = (i - 2) * row_tiles
        unpack(agb.at[first // half_tiles], first % half_tiles, i)
    arrived(final.at[1 - core], final_pair)
    for c, (edge_row, inner_row) in enumerate(((0, 1), (rows - 1, rows - 2))):
        unpack(final.at[c], 0, edge_row)
        unpack(final.at[c], row_tiles, inner_row)

    for copy in started:
        copy.wait_send()
    arrived(sxy.at[pl.ds(0, plane - 1)], over_plane)
    whole = jnp.sum(sxy[...], axis=0)
    scale = 1.0 / (layers * steps * tms * rows * spaces * width)
    cur[...] = jnp.broadcast_to(jnp.sum(whole, axis=1, keepdims=True) * scale, cur.shape)


def shards(tms, spaces, pressure, mobility, capacity, misfit_weight, log_permeability, direction):
    _, steps, layers, rows, width = pressure.shape
    dims = (tms, spaces, steps, layers, rows, width)
    tiles = width // LANES
    zhs = tms // CORES
    ys = spaces // (CHIPS_X * Z_LO)
    line = zhs * Z_LO * CORES
    plane = ys * CHIPS_X
    flat = layers * rows * tiles
    row_tiles = tiles // SUBLANES
    half_tiles = (rows // CORES - 2) * row_tiles
    chunk = half_tiles // zhs
    copies = 6 * steps + 2 + 3 + 5 * zhs + line + plane
    vmem = pltpu.VMEM

    def in_tiles(array):
        count = array.size // (SUBLANES * width)
        cut = array.reshape(count, SUBLANES, tiles, LANES).transpose(0, 2, 1, 3)
        return cut.reshape(count * tiles * SUBLANES, LANES)

    def block(*shape):
        return vmem((*shape, SUBLANES, LANES), F32)

    product, curvature = pl.pallas_call(
        functools.partial(kernel, dims),
        out_shape=(
            jax.ShapeDtypeStruct((rows, width), F32),
            jax.ShapeDtypeStruct((1, LANES), F32),
        ),
        in_specs=[pl.BlockSpec(memory_space=pl.ANY)] * 6,
        out_specs=(
            pl.BlockSpec(memory_space=pltpu.VMEM),
            pl.BlockSpec(memory_space=pltpu.VMEM),
        ),
        scratch_shapes=[
            vmem((steps * flat, LANES), F32),
            vmem((steps * flat, LANES), F32),
            vmem((steps * flat, LANES), F32),
            vmem((flat, LANES), F32),
            vmem((rows, width), F32),
            vmem((rows, width), F32),
            vmem((rows + 2, steps, 2, layers, width), F32),
            vmem((rows + 1, steps, layers, width), F32),
            vmem((rows + 2, steps, layers, width), F32),
            vmem((rows + 1, tiles * layers, LANES), F32),
            vmem((rows, 2, tiles * layers, LANES), F32),
            vmem((rows + 1, layers, width), F32),
            vmem((rows, layers, width), F32),
            vmem((rows, layers, width), F32),
            vmem((rows, width), F32),
            vmem((2, 1, width), F32),
            vmem((2, 1, width), F32),
            block(CORES * half_tiles),
            block(half_tiles),
            block(half_tiles),
            block(zhs, chunk),
            block(CORES, half_tiles),
            block(CORES, 3 * row_tiles),
            block(3 * row_tiles),
            block(zhs, 3 * row_tiles),
            block(zhs, row_tiles),
            block(CORES, 2 * row_tiles),
            vmem((line, 1, LANES), F32),
            vmem((plane, 1, LANES), F32),
            pltpu.SemaphoreType.DMA((2 * steps + 4,)),
            pltpu.SemaphoreType.DMA((copies,)),
            pltpu.SemaphoreType.DMA((copies,)),
        ],
        compiler_params=pltpu.CompilerParams(
            collective_id=0, has_side_effects=True, vmem_limit_bytes=55040 << 10
        ),
        cost_estimate=pl.CostEstimate(
            flops=50 * steps * flat * LANES,
            bytes_accessed=14 * steps * flat * LANES,
            transcendentals=rows * width,
        ),
    )(
        in_tiles(pressure),
        in_tiles(mobility),
        in_tiles(capacity),
        in_tiles(misfit_weight),
        log_permeability,
        direction,
    )
    return product, curvature[0, 0]


def solution(mesh):
    placed = (
        P("tm", None, None, "space", None),
        P("tm", None, None, "space", None),
        P("tm", None, None, "space", None),
        P("tm", None, "space", None),
        P("space", None),
        P("space", None),
    )
    return jax.shard_map(
        functools.partial(shards, mesh.shape["tm"], mesh.shape["space"]),
        mesh=mesh,
        in_specs=placed,
        out_specs=(P("space", None), P()),
        check_vma=False,
    )
```

```python
import functools

import jax
import jax.numpy as jnp
from jax import lax
from jax.experimental import pallas as pl
from jax.experimental.pallas import tpu as pltpu
from jax.sharding import PartitionSpec as P

LANES = 128
SUBLANES = 8
CHIPS_X = 4
CORES = 2
Z_LO = 2
MESH = pl.DeviceIdType.MESH
F32 = jnp.float32


def kernel(
    dims,
    p_hbm,
    m_hbm,
    c_hbm,
    w_hbm,
    lp_hbm,
    d_hbm,
    out,
    cur,
    pv,
    mv,
    cv,
    wv,
    lpv,
    dv,
    pm,
    fx,
    adj,
    txa,
    ty,
    sbx,
    sby,
    sbb,
    factor,
    sce,
    rce,
    inner,
    inner_in,
    inner_sum,
    rsb,
    agb,
    edges,
    edges_in,
    edge_z,
    ghost_z,
    final,
    sz,
    sxy,
    local_sem,
    send_sem,
    recv_sem,
):
    tms, spaces, steps, layers, rows, width = dims
    tiles = width // LANES
    zhs = tms // CORES
    ys = spaces // (CHIPS_X * Z_LO)
    zs = zhs * Z_LO
    last = rows
    row_tiles = tiles // SUBLANES
    row_blocks = rows // SUBLANES
    layer_rows = row_blocks * tiles * SUBLANES
    state_rows = layers * layer_rows

    tm = lax.axis_index("tm")
    sp = lax.axis_index("space")
    zh, core = tm // CORES, tm % CORES
    zl = sp % Z_LO
    x = (sp // Z_LO) % CHIPS_X
    y = sp // (Z_LO * CHIPS_X)
    z = zh * Z_LO + zl
    left = (sp + spaces - 1) % spaces
    right = (sp + 1) % spaces
    other = (tm + 1) - 2 * core

    loads = {}

    def load(name, src, dst, index):
        loads[name] = pltpu.make_async_copy(src, dst, local_sem.at[index])
        loads[name].start()

    line = zs * CORES
    my_line = z * CORES + core
    plane = ys * CHIPS_X
    my_plane = y * CHIPS_X + x

    def apart(k, n):
        return min(k, n - k)

    line_offsets = sorted(
        ((dz, dc) for dz in range(zs) for dc in range(CORES) if (dz, dc) != (0, 0)),
        key=lambda o: -apart(o[0], zs),
    )
    plane_offsets = sorted(
        ((dy, dx) for dy in range(ys) for dx in range(CHIPS_X) if (dy, dx) != (0, 0)),
        key=lambda o: -apart(o[0], ys) - apart(o[1], CHIPS_X),
    )
    z_offsets = sorted(range(1, zhs), key=lambda k: -apart(k, zhs))

    def line_slot(dz, dc):
        return ((z + dz + zs) % zs) * CORES + (core + dc + CORES) % CORES

    def line_peer(dz, dc):
        to = (z + dz) % zs
        return ((to // Z_LO) * CORES + (core + dc) % CORES, sp - zl + to % Z_LO)

    def plane_slot(dy, dx):
        return ((y + dy + ys) % ys) * CHIPS_X + (x + dx + CHIPS_X) % CHIPS_X

    def plane_peer(dy, dx):
        return (tm, plane_slot(dy, dx) * Z_LO + zl)

    def z_peer(k):
        return (((zh + k) % zhs) * CORES + core, sp)

    across = left + zl * (right - left)
    greet = [(apart(dz, zs) + 0.5 * dc, line_peer(dz, dc)) for dz, dc in line_offsets]
    greet += [
        (apart(dy, ys) + apart(dx, CHIPS_X), plane_peer(dy, dx)) for dy, dx in plane_offsets
    ]
    greet += [
        (
            1.5 + Z_LO * apart(k, zhs),
            (((zh + k) % zhs) * CORES + (core + c) % CORES, across),
        )
        for k in range(zhs)
        for c in range(CORES)
    ]
    greet.sort(key=lambda entry: -entry[0])
    barrier = pltpu.get_barrier_semaphore()

    def say(peers):
        for _, peer in peers:
            pl.semaphore_signal(barrier, inc=1, device_id=peer, device_id_type=MESH)

    distant = sum(hops > 2.5 for hops, _ in greet)
    say(greet[:distant])
    for s in range(steps):
        part = pl.ds(s * state_rows, state_rows)
        load(("p", s), p_hbm.at[part, :], pv.at[part, :], 2 * s)
        load(("m", s), m_hbm.at[part, :], mv.at[part, :], 2 * s + 1)
    load("lp", lp_hbm, lpv, 2 * steps)
    load("d", d_hbm, dv, 2 * steps + 1)
    say(greet[distant:])

    sem_count = [0]
    started = []

    def send(src, dst, device, send_index, recv_index):
        copy = pltpu.make_async_remote_copy(
            src_ref=src,
            dst_ref=dst,
            send_sem=send_sem.at[send_index],
            recv_sem=recv_sem.at[recv_index],
            device_id=device,
            device_id_type=MESH,
        )
        copy.start()
        started.append(copy)

    def arrived(dst, recv_index):
        pltpu.make_async_copy(dst, dst, recv_sem.at[recv_index]).wait()

    def take(n):
        first = sem_count[0]
        sem_count[0] += n
        return first

    def layers_of(ref, s, i, j):
        first = (
            s * state_rows + (i // SUBLANES) * (tiles * SUBLANES) + j * SUBLANES + i % SUBLANES
        )
        return ref[pl.ds(first, layers, stride=layer_rows), :]

    def cut(j):
        return slice(j * LANES, (j + 1) * LANES)

    def spread(s, i):
        for which, ref in enumerate((pv, mv)):
            for j in range(tiles):
                pm[i + 1, s, which, :, cut(j)] = layers_of(ref, s, i, j)

    def shares(s):
        size = tiles // 2 if s == 0 else tiles // 4
        return range(size), range(size, tiles - size), range(tiles - size, tiles)

    def lanes_of(part):
        return pl.ds(part[0] * LANES, len(part) * LANES)

    halo = take(2 * steps)
    middle = take(2 * steps)
    for s in range(steps):
        loads["p", s].wait()
        loads["m", s].wait()
        spread(s, 0)
        spread(s, rows - 1)
        if s == 0:
            load("c", c_hbm, cv, 2 * steps + 2)
            load("w", w_hbm, wv, 2 * steps + 3)
            pl.semaphore_wait(barrier, len(greet))
        near, both, far = shares(s)
        for first, parts in ((halo, (far, near)), (middle, (both, both))):
            for k, part in enumerate(parts):
                if len(part):
                    row, goal, side = ((1, last + 1, left), (last, 0, right))[k]
                    columns = lanes_of(part)
                    send(
                        pm.at[row, s, :, :, columns],
                        pm.at[goal, s, :, :, columns],
                        (tm, side),
                        first + 2 * s + k,
                        first + 2 * s + k,
                    )

    loads["lp"].wait()
    loads["d"].wait()
    conduct = jnp.exp(lpv[...])
    factor[...] = conduct * (0.25 / (layers * steps * tms))
    scaled = conduct * dv[...]
    sce[0] = scaled[0:1, :]
    sce[1] = scaled[rows - 1 : rows, :]
    edge = take(2)
    send(sce.at[0], rce.at[1], (tm, left), edge, edge)
    send(sce.at[1], rce.at[0], (tm, right), edge + 1, edge + 1)

    wide = (layers, width)
    for i in range(rows):
        row = scaled[i : i + 1, :]
        if i + 1 < rows:
            sbx[i + 1] = jnp.broadcast_to(0.25 * (row + scaled[i + 1 : i + 2, :]), wide)
        sby[i] = jnp.broadcast_to(0.25 * (row + pltpu.roll(row, width - 1, 1)), wide)
        sbb[i] = jnp.broadcast_to(0.25 * (row + pltpu.roll(row, 1, 1)), wide)

    def spread_inner(i, carry):
        for s in range(steps):
            spread(s, i)
        return carry

    lax.fori_loop(1, rows - 1, spread_inner, 0)

    lane = lax.broadcasted_iota(jnp.int32, (layers, LANES), 1)
    not_last = lane < LANES - 1
    not_first = lane > 0

    def face_part(f, s, part):
        for j in part:
            c = cut(j)
            fx[f, s, :, c] = (pm[f, s, 1, :, c] + pm[f + 1, s, 1, :, c]) * (
                pm[f + 1, s, 0, :, c] - pm[f, s, 0, :, c]
            )

    def face_x(f, carry):
        for s in range(steps):
            face_part(f, s, range(tiles))
        return carry

    def cell_row(r, curvature, states=range(steps), add=False):
        i = r - 1

        def ahead(here, later):
            return jnp.where(not_last, here, later)

        def turned(s, j):
            pressure, mobility = pm[r, s, 0, :, cut(j)], pm[r, s, 1, :, cut(j)]
            return (
                pressure,
                mobility,
                pltpu.roll(pressure, LANES - 1, 1),
                pltpu.roll(mobility, LANES - 1, 1),
            )

        here = {s: turned(s, 0) for s in states}
        spill = {s: 0.0 for s in states}
        for j in range(tiles):
            c = cut(j)
            piece = pl.ds(j * SUBLANES, SUBLANES)
            low, high = (ty[i, 0, piece, :], ty[i, 1, piece, :]) if add else (None, None)
            for s in states:
                pressure, mobility, p_back, m_back = here[s]
                if j + 1 < tiles:
                    here[s] = turned(s, j + 1)
                    p_next, m_next = here[s][2], here[s][3]
                else:
                    p_next, m_next = pressure, mobility
                face = (mobility + ahead(m_back, m_next)) * (ahead(p_back, p_next) - pressure)
                turned_face = pltpu.roll(face, 1, 1)
                before = jnp.where(not_first, turned_face, spill[s])
                spill[s] = turned_face
                change = (
                    fx[r, s, :, c] * sbx[r, :, c]
                    - fx[r - 1, s, :, c] * sbx[r - 1, :, c]
                    + (face * sby[i, :, c] - before * sbb[i, :, c])
                )
                square = layers_of(cv, s, i, j)
                square = square * square
                inverse = pl.reciprocal(square, approx=True)
                inverse = inverse * (2.0 - square * inverse)
                value = layers_of(wv, 0, i, j) * change * inverse
                adj[r, s, :, c] = value
                curvature = curvature + value * change
                low = face * value if low is None else low + face * value
                high = before * value if high is None else high + before * value
            ty[i, 0, piece, :] = low
            ty[i, 1, piece, :] = high
        return curvature

    def pack(dst, first, j, value):
        low = j % SUBLANES
        dst[first + j // SUBLANES, low : low + 1, :] = jnp.sum(value, axis=0, keepdims=True)

    def face_terms(f, low=True, high=True):
        for j in range(tiles):
            c = cut(j)
            total = None
            for s in range(steps):
                if low and high:
                    difference = adj[f, s, :, c] - adj[f + 1, s, :, c]
                elif low:
                    difference = adj[f, s, :, c]
                else:
                    difference = -adj[f + 1, s, :, c]
                value = fx[f, s, :, c] * difference
                total = value if total is None else total + value
            txa[f, pl.ds(j * SUBLANES, SUBLANES), :] = total

    def piece(j):
        return pl.ds(j * SUBLANES, SUBLANES)

    def pack_total(dst, first, i):
        high = [pltpu.roll(ty[i, 1, piece(j), :], LANES - 1, 1) for j in range(tiles)] + [0.0]
        terms = [
            ty[i, 0, piece(j), :] - jnp.where(not_last, high[j], high[j + 1])
            for j in range(tiles)
        ]
        low = [0.0] + [pltpu.roll(v, 1, 1) for v in terms]
        for j in range(tiles):
            value = txa[i, piece(j), :] + txa[i + 1, piece(j), :]
            value = value + (terms[j] + jnp.where(not_first, low[j + 1], low[j]))
            pack(dst, first, j, value)

    lax.fori_loop(1, rows, face_x, 0)
    loads["c"].wait()
    loads["w"].wait()
    curvature = lax.fori_loop(2, rows, cell_row, jnp.zeros((layers, LANES), F32))

    product = take(2 * steps)
    products = {}

    def send_products(s):
        near, _, far = shares(s)
        for k, (f, goal, part, side, index) in enumerate(
            ((0, last, near, left, halo + 1), (last, 0, far, right, halo))
        ):
            columns = lanes_of(part)
            cells = 0 if f == 0 else last + 1
            arrived(pm.at[cells, s, :, :, columns], index + 2 * s)
            face_part(f, s, part)
            number = product + 2 * s + k
            send(fx.at[f, s, :, columns], fx.at[goal, s, :, columns], (tm, side), number, number)
            products[s, k] = started.pop()

    for s in range(steps):
        send_products(s)

    def inner_faces(f, carry):
        face_terms(f)
        return carry

    lax.fori_loop(2, rows - 1, inner_faces, 0)

    def inner_rows(i, carry):
        pack_total(inner, (i - 2) * row_tiles, i)
        return carry

    lax.fori_loop(2, rows - 2, inner_rows, 0)

    half_tiles = (rows // CORES - 2) * row_tiles
    chunk = half_tiles // zhs
    inner_pair = take(1)
    send(
        inner.at[pl.ds((1 - core) * half_tiles, half_tiles)],
        inner_in,
        (other, sp),
        inner_pair,
        inner_pair,
    )

    arrived(inner_in, inner_pair)
    inner_sum[...] = inner[pl.ds(core * half_tiles, half_tiles)] + inner_in[...]
    scatter = take(zhs)
    for k in z_offsets:
        to = (zh + k) % zhs
        send(
            inner_sum.at[pl.ds(to * chunk, chunk)],
            rsb.at[k],
            z_peer(k),
            scatter + k,
            scatter + k,
        )

    arrived(rce.at[0], edge + 1)
    arrived(rce.at[1], edge)
    sbx[0] = jnp.broadcast_to(0.25 * (rce[0] + scaled[0:1, :]), wide)
    sbx[last] = jnp.broadcast_to(0.25 * (rce[1] + scaled[rows - 1 : rows, :]), wide)

    def no_face(states):
        @pl.when(sp == 0)
        def _():
            for s in states:
                fx[0, s] = jnp.zeros(wide, F32)

        @pl.when(sp == spaces - 1)
        def _():
            for s in states:
                fx[last, s] = jnp.zeros(wide, F32)

    def edge_rows(states, add, curvature):
        return lax.fori_loop(
            0, 2, lambda k, carry: cell_row(1 + k * (rows - 1), carry, states, add), curvature
        )

    for s in range(steps):
        near, both, far = shares(s)
        if len(both):
            for f, cells, k in ((last, last + 1, 0), (0, 0, 1)):
                arrived(pm.at[cells, s, :, :, lanes_of(both)], middle + 2 * s + k)
                face_part(f, s, both)
        for k, (f, part) in enumerate(((last, near), (0, far))):
            arrived(fx.at[f, s, :, lanes_of(part)], product + 2 * s + k)
            products[s, k].wait_send()
        no_face((s,))
        curvature = edge_rows((s,), s > 0, curvature)

    sz[my_line] = jnp.sum(curvature, axis=0, keepdims=True)
    over_line = take(line)
    for k, o in enumerate(line_offsets):
        send(sz.at[my_line], sz.at[my_line], line_peer(*o), over_line + k, over_line)

    face_terms(0, low=False)
    face_terms(last, high=False)
    face_terms(1)
    face_terms(rows - 1)
    for c, (edge_row, inner_row, face) in enumerate(((0, 1, 0), (rows - 1, rows - 2, last))):
        pack_total(edges.at[c], 0, edge_row)
        pack_total(edges.at[c], row_tiles, inner_row)
        for j in range(tiles):
            pack(edges.at[c], 2 * row_tiles, j, txa[face, piece(j), :])
    edge_pair = take(1)
    send(edges.at[1 - core], edges_in, (other, sp), edge_pair, edge_pair)

    reduced = inner_sum[pl.ds(zh * chunk, chunk)]
    for k in range(1, zhs):
        arrived(rsb.at[k], scatter + k)
        reduced = reduced + rsb[k]
    agb[core, pl.ds(zh * chunk, chunk)] = reduced
    mine = agb.at[core, pl.ds(zh * chunk, chunk)]
    gather = take(zhs)
    forward = take(zhs)
    for k in z_offsets:
        send(mine, mine, z_peer(k), gather + k, gather + k)
    send(mine, mine, (other, sp), forward, forward)

    two = 2 * row_tiles
    arrived(edges_in, edge_pair)
    summed = edges[core] + edges_in[...]
    edge_z[zh] = summed
    over_z = take(zhs)
    ghost = take(zhs)
    for k in z_offsets:
        send(
            edge_z.at[zh, pl.ds(0, two)],
            edge_z.at[zh, pl.ds(0, two)],
            z_peer(k),
            over_z + k,
            over_z + k,
        )
    side = left + core * (right - left)
    for k in z_offsets + [0]:
        send(
            edge_z.at[zh, pl.ds(two, row_tiles)],
            ghost_z.at[zh],
            (((zh + k) % zhs) * CORES + 1 - core, side),
            ghost + k,
            ghost + k,
        )

    arrived(sz.at[pl.ds(0, line - 1)], over_line)
    sxy[my_plane] = jnp.sum(sz[...], axis=0)
    over_plane = take(plane)
    for k, o in enumerate(plane_offsets):
        send(sxy.at[my_plane], sxy.at[my_plane], plane_peer(*o), over_plane + k, over_plane)

    def unpack(src, first, i):
        for j in range(tiles):
            low = j % SUBLANES
            value = src[first + j // SUBLANES, low : low + 1, :]
            out[i : i + 1, cut(j)] = value * factor[i : i + 1, cut(j)]

    for k in range(1, zhs):
        whose = agb.at[core, pl.ds(((zh + zhs - k) % zhs) * chunk, chunk)]
        arrived(whose, gather + k)
        send(whose, whose, (other, sp), forward + k, forward + k)

    for k in range(1, zhs):
        arrived(edge_z.at[(zh + zhs - k) % zhs, pl.ds(0, two)], over_z + k)
    for k in range(zhs):
        arrived(ghost_z.at[(zh + zhs - k) % zhs], ghost + k)
    total = edge_z[0, 0:two]
    beyond = ghost_z[0]
    for k in range(1, zhs):
        total = total + edge_z[k, 0:two]
        beyond = beyond + ghost_z[k]
    final[core, pl.ds(0, row_tiles)] = total[:row_tiles] + beyond
    final[core, pl.ds(row_tiles, row_tiles)] = total[row_tiles:]
    final_pair = take(1)
    send(final.at[core], final.at[core], (other, sp), final_pair, final_pair)

    for k in range(zhs):
        whose = agb.at[1 - core, pl.ds(((zh + zhs - k) % zhs) * chunk, chunk)]
        arrived(whose, forward + k)
    for i in range(2, rows - 2):
        first = (i - 2) * row_tiles
        unpack(agb.at[first // half_tiles], first % half_tiles, i)
    arrived(final.at[1 - core], final_pair)
    for c, (edge_row, inner_row) in enumerate(((0, 1), (rows - 1, rows - 2))):
        unpack(final.at[c], 0, edge_row)
        unpack(final.at[c], row_tiles, inner_row)

    for copy in started:
        copy.wait_send()
    arrived(sxy.at[pl.ds(0, plane - 1)], over_plane)
    whole = jnp.sum(sxy[...], axis=0)
    scale = 1.0 / (layers * steps * tms * rows * spaces * width)
    cur[...] = jnp.broadcast_to(jnp.sum(whole, axis=1, keepdims=True) * scale, cur.shape)


def shards(tms, spaces, pressure, mobility, capacity, misfit_weight, log_permeability, direction):
    _, steps, layers, rows, width = pressure.shape
    dims = (tms, spaces, steps, layers, rows, width)
    tiles = width // LANES
    zhs = tms // CORES
    ys = spaces // (CHIPS_X * Z_LO)
    line = zhs * Z_LO * CORES
    plane = ys * CHIPS_X
    flat = layers * rows * tiles
    row_tiles = tiles // SUBLANES
    half_tiles = (rows // CORES - 2) * row_tiles
    chunk = half_tiles // zhs
    copies = 6 * steps + 2 + 3 + 5 * zhs + line + plane
    vmem = pltpu.VMEM

    def in_tiles(array):
        count = array.size // (SUBLANES * width)
        cut = array.reshape(count, SUBLANES, tiles, LANES).transpose(0, 2, 1, 3)
        return cut.reshape(count * tiles * SUBLANES, LANES)

    def block(*shape):
        return vmem((*shape, SUBLANES, LANES), F32)

    product, curvature = pl.pallas_call(
        functools.partial(kernel, dims),
        out_shape=(
            jax.ShapeDtypeStruct((rows, width), F32),
            jax.ShapeDtypeStruct((1, LANES), F32),
        ),
        in_specs=[pl.BlockSpec(memory_space=pl.ANY)] * 6,
        out_specs=(
            pl.BlockSpec(memory_space=pltpu.VMEM),
            pl.BlockSpec(memory_space=pltpu.VMEM),
        ),
        scratch_shapes=[
            vmem((steps * flat, LANES), F32),
            vmem((steps * flat, LANES), F32),
            vmem((steps * flat, LANES), F32),
            vmem((flat, LANES), F32),
            vmem((rows, width), F32),
            vmem((rows, width), F32),
            vmem((rows + 2, steps, 2, layers, width), F32),
            vmem((rows + 1, steps, layers, width), F32),
            vmem((rows + 2, steps, layers, width), F32),
            vmem((rows + 1, tiles * layers, LANES), F32),
            vmem((rows, 2, tiles * layers, LANES), F32),
            vmem((rows + 1, layers, width), F32),
            vmem((rows, layers, width), F32),
            vmem((rows, layers, width), F32),
            vmem((rows, width), F32),
            vmem((2, 1, width), F32),
            vmem((2, 1, width), F32),
            block(CORES * half_tiles),
            block(half_tiles),
            block(half_tiles),
            block(zhs, chunk),
            block(CORES, half_tiles),
            block(CORES, 3 * row_tiles),
            block(3 * row_tiles),
            block(zhs, 3 * row_tiles),
            block(zhs, row_tiles),
            block(CORES, 2 * row_tiles),
            vmem((line, 1, LANES), F32),
            vmem((plane, 1, LANES), F32),
            pltpu.SemaphoreType.DMA((2 * steps + 4,)),
            pltpu.SemaphoreType.DMA((copies,)),
            pltpu.SemaphoreType.DMA((copies,)),
        ],
        compiler_params=pltpu.CompilerParams(
            collective_id=0, has_side_effects=True, vmem_limit_bytes=55040 << 10
        ),
        cost_estimate=pl.CostEstimate(
            flops=50 * steps * flat * LANES,
            bytes_accessed=14 * steps * flat * LANES,
            transcendentals=rows * width,
        ),
    )(
        in_tiles(pressure),
        in_tiles(mobility),
        in_tiles(capacity),
        in_tiles(misfit_weight),
        log_permeability,
        direction,
    )
    return product, curvature[0, 0]


def solution(mesh):
    placed = (
        P("tm", None, None, "space", None),
        P("tm", None, None, "space", None),
        P("tm", None, None, "space", None),
        P("tm", None, "space", None),
        P("space", None),
        P("space", None),
    )
    return jax.shard_map(
        functools.partial(shards, mesh.shape["tm"], mesh.shape["space"]),
        mesh=mesh,
        in_specs=placed,
        out_specs=(P("space", None), P()),
        check_vma=False,
    )
```
